128 devices in a mesh: dp: 32 (over y, z, core), seq: 4 (over x).
Axes of the slice: x: 4, y: 4, z: 4, core: 2. Of those that a mesh axis runs over, the one named last changes fastest.
Arguments:
- layer_input: bfloat16 [32, 1024, 1152], P('dp', 'seq'), may hold values from -10 to 10
- out_grad: bfloat16 [32, 1024, 1152], P('dp', 'seq'), may hold values from -6 to 6
- segment_ids: int32 [32, 1024], P('dp'), may hold values from 0 to 254, as said below
- adapter_ids: int32 [32], P('dp'), may hold values from 0 to 7
- gain_attn_in: float32 [1152], replicated, may hold values from 0.25 to 1.75
- gain_attn_out: float32 [1152], replicated, may hold values from 0.25 to 1.75
- gain_mlp_in: float32 [1152], replicated, may hold values from 0.25 to 1.75
- gain_mlp_out: float32 [1152], replicated, may hold values from 0.25 to 1.75
- w_query: bfloat16 [1152, 1024], P(None, 'dp'), may hold values from -2 to 2
- w_key: bfloat16 [1152, 256], P(None, 'dp'), may hold values from -2 to 2
- w_value: bfloat16 [1152, 256], P(None, 'dp'), may hold values from -2 to 2
- w_out: bfloat16 [1024, 1152], P('dp'), may hold values from -0.1875 to 0.1875
- w_gate: bfloat16 [1152, 6912], P(None, 'dp'), may hold values from -0.1875 to 0.1875
- w_up: bfloat16 [1152, 6912], P(None, 'dp'), may hold values from -0.1875 to 0.1875
- w_down: bfloat16 [6912, 1152], P('dp'), may hold values from -0.078125 to 0.078125
- qkv_adapt_in: bfloat16 [8, 3, 16, 1152], replicated, may hold values from -0.1875 to 0.1875
- q_adapt_out: bfloat16 [8, 16, 1024], replicated, may hold values from -0.75 to 0.75
- kv_adapt_out: bfloat16 [8, 2, 16, 256], replicated, may hold values from -0.75 to 0.75
- o_adapt_in: bfloat16 [8, 16, 1024], replicated, may hold values from -0.1875 to 0.1875
- o_adapt_out: bfloat16 [8, 16, 1152], replicated, may hold values from -0.75 to 0.75
- mlp_adapt_in: bfloat16 [8, 2, 16, 1152], replicated, may hold values from -0.1875 to 0.1875
- mlp_adapt_out: bfloat16 [8, 2, 16, 6912], replicated, may hold values from -0.75 to 0.75
- down_adapt_in: bfloat16 [8, 16, 6912], replicated, may hold values from -0.078125 to 0.078125
- down_adapt_out: bfloat16 [8, 16, 1152], replicated, may hold values from -0.75 to 0.75
Outputs:
- layer_output: bfloat16 [32, 1024, 1152], P('dp', 'seq')
- input_grad: bfloat16 [32, 1024, 1152], P('dp', 'seq')
- grad_qkv_adapt_in: float32 [8, 3, 16, 1152], replicated
- grad_q_adapt_out: float32 [8, 16, 1024], replicated
- grad_kv_adapt_out: float32 [8, 2, 16, 256], replicated
- grad_o_adapt_in: float32 [8, 16, 1024], replicated
- grad_o_adapt_out: float32 [8, 16, 1152], replicated
- grad_mlp_adapt_in: float32 [8, 2, 16, 1152], replicated
- grad_mlp_adapt_out: float32 [8, 2, 16, 6912], replicated
- grad_down_adapt_in: float32 [8, 16, 6912], replicated
- grad_down_adapt_out: float32 [8, 16, 1152], replicated
The draws below stay inside these ranges and needn't reach their ends.
Inputs may be any that keep to these rules, and one draw needn't show every extreme that they name: `segment_ids`: within each sequence the segment numbers start at 0, never fall and rise by at most one from token to token; each sequence holds one document of at least 770 tokens.
All inputs are finite; a program needn't handle non-finite values.
Results may differ from the reference program's by a relative error of at most 0.024.
Values may be sent and summed in bfloat16 or wider, within the bound.
A program may use at most 256 MiB of HBM per device.

```python
import jax
import jax.numpy as jnp
from jax import lax

D = 1152
FF = 6912
HEADS = 4
HEAD_DIM = 256
RANK = 16
ADAPTERS = 8
LEN = 1024
SEQUENCES = 32
QDIM = 1024


def marked_channels(key):
    keys = jax.random.split(key, 3)
    count = max(2, D // 128)
    order = jax.random.permutation(keys[0], jnp.arange(D, dtype=jnp.int32))
    marked = (order < count).astype(jnp.float32)
    signs = jnp.where(jax.random.randint(keys[1], (D,), 0, 2) == 1, 1.0, -1.0).astype(jnp.float32)
    pattern = jnp.where(jax.random.randint(keys[2], (HEAD_DIM,), 0, 2) == 1, 1.0, -1.0).astype(jnp.float32)
    return (marked, signs, pattern, 0.42 / count)


def draw_layer_input(key, part):
    marked, signs, _, _ = marked_channels(key)
    key = jax.random.fold_in(key, 21)
    noise = jax.random.truncated_normal(key, -6.0, 6.0, (SEQUENCES, LEN, D), jnp.float32)
    return (noise + 4.0 * (marked * signs)[None, None, :]).astype(jnp.bfloat16)


def draw_w_query(key, part):
    marked, signs, pattern, lift = marked_channels(key)
    key = jax.random.fold_in(key, 23)
    keys = jax.random.split(key, 2)
    noise = jax.random.truncated_normal(keys[0], -6.0, 6.0, (D, HEADS * HEAD_DIM), jnp.float32) * D ** (-0.5)
    strength = jax.random.uniform(keys[1], (HEADS,), jnp.float32, 0.4, 1.2)
    columns = (strength[:, None] * pattern[None, :]).reshape(HEADS * HEAD_DIM)
    return (noise + lift * (marked * signs)[:, None] * columns[None, :]).astype(jnp.bfloat16)


def draw_w_key(key, part):
    marked, signs, pattern, lift = marked_channels(key)
    key = jax.random.fold_in(key, 22)
    noise = jax.random.truncated_normal(key, -6.0, 6.0, (D, HEAD_DIM), jnp.float32) * (D / 2.0) ** (-0.5)
    return (noise + lift * (marked * signs)[:, None] * pattern[None, :]).astype(jnp.bfloat16)


def draw_w_value(key, part):
    marked, _, _, _ = marked_channels(key)
    key = jax.random.fold_in(key, 24)
    noise = jax.random.truncated_normal(key, -6.0, 6.0, (D, HEAD_DIM), jnp.float32) * D ** (-0.5)
    return (noise * (1.0 - 0.95 * marked)[:, None]).astype(jnp.bfloat16)


def draw_segment_ids(key, part):
    key = jax.random.fold_in(key, 11)
    keys = jax.random.split(key, 5)
    least = 3 * LEN // 4 + 2
    rows = jnp.arange(SEQUENCES, dtype=jnp.int32)[:, None]
    fullest = jax.random.randint(keys[4], (), 0, SEQUENCES)
    is_fullest = rows == fullest
    longest = jax.random.randint(keys[0], (SEQUENCES, 1), least, LEN + 1)
    longest = jnp.where(is_fullest, least, longest)
    first_pos = jax.random.randint(keys[1], (SEQUENCES, 1), 0, LEN - longest + 1)
    rate_shift = jax.random.randint(keys[2], (SEQUENCES, 1), 2, 8)
    rate_shift = jnp.where(is_fullest, 0, rate_shift)
    draws = jax.random.randint(keys[3], (SEQUENCES, LEN), 0, 1 << 20)
    threshold = jnp.right_shift(jnp.int32(1 << 20), rate_shift)
    position = jnp.arange(LEN, dtype=jnp.int32)[None, :]
    inside = (position > first_pos) & (position < first_pos + longest)
    boundary = (draws < threshold) & jnp.logical_not(inside) | (position == first_pos) | (position == first_pos + longest) | (position == 0)
    return (jnp.cumsum(boundary.astype(jnp.int32), axis=1) - 1).astype(jnp.int32)


def touch_ends(result, key, low, top_value):
    longest = result.shape.index(max(result.shape))
    spots = []
    for shift in (0, 1):
        where = [jax.random.randint(jax.random.fold_in(key, axis), (), 0, length) for axis, length in enumerate(result.shape)]
        where[longest] = (where[longest] + shift) % result.shape[longest]
        spots.append(tuple(where))
    return result.at[spots[0]].set(low).at[spots[1]].set(top_value)


def level_of(own_key, extent, pieces, low, top_value):
    gain, own = 1.0, jax.random.fold_in(own_key, 6)
    for dim, blocks in pieces:
        heights = jnp.exp(jax.random.uniform(jax.random.fold_in(own, dim), (blocks,), jnp.float32, low / len(pieces), top_value / len(pieces)))
        gain = gain * jnp.repeat(heights, extent[dim] // blocks).reshape([-1 if axis == dim else 1 for axis in range(len(extent))])
    return gain


def normal_values(stream_key, extent, deviation, limit, cuts=(), held_as=jnp.bfloat16):
    result = deviation * jax.random.normal(stream_key, extent, jnp.float32)
    if cuts:
        result = result * level_of(stream_key, extent, cuts, -0.22, 0.18)
    return jnp.clip(result, -limit, limit).astype(held_as)


def setup_inputs(seed: int = 0) -> dict:
    splits = jax.random.split(jax.random.key(seed), 25)
    return {
        "layer_input": draw_layer_input(jax.random.fold_in(splits[24], 71), 0),
        "out_grad": normal_values(splits[1], (SEQUENCES, LEN, D), 1.0, 6.0, ((0, 32), (1, 4))),
        "segment_ids": draw_segment_ids(jax.random.fold_in(splits[24], 71), 0),
        "adapter_ids": touch_ends(jax.random.randint(splits[3], (SEQUENCES,), 0, ADAPTERS), jax.random.fold_in(splits[3], 1), 0, ADAPTERS - 1).astype(jnp.int32),
        "gain_attn_in": jnp.clip(1.0 + 0.15 * jax.random.normal(splits[4], (D,), jnp.float32), 0.25, 1.75),
        "gain_attn_out": jnp.clip(1.0 + 0.15 * jax.random.normal(splits[5], (D,), jnp.float32), 0.25, 1.75),
        "gain_mlp_in": jnp.clip(1.0 + 0.15 * jax.random.normal(splits[6], (D,), jnp.float32), 0.25, 1.75),
        "gain_mlp_out": jnp.clip(1.0 + 0.15 * jax.random.normal(splits[7], (D,), jnp.float32), 0.25, 1.75),
        "w_query": draw_w_query(jax.random.fold_in(splits[24], 71), 0),
        "w_key": draw_w_key(jax.random.fold_in(splits[24], 71), 0),
        "w_value": draw_w_value(jax.random.fold_in(splits[24], 71), 0),
        "w_out": normal_values(splits[11], (QDIM, D), QDIM ** -0.5, 0.1875, ((0, 32),)),
        "w_gate": normal_values(splits[12], (D, FF), D ** -0.5, 0.1875, ((1, 32),)),
        "w_up": normal_values(splits[13], (D, FF), D ** -0.5, 0.1875, ((1, 32),)),
        "w_down": normal_values(splits[14], (FF, D), FF ** -0.5, 0.078125, ((0, 32),)),
        "qkv_adapt_in": normal_values(splits[15], (ADAPTERS, 3, RANK, D), D ** -0.5, 0.1875),
        "q_adapt_out": normal_values(splits[16], (ADAPTERS, RANK, QDIM), (4 * RANK) ** -0.5, 0.75),
        "kv_adapt_out": normal_values(splits[17], (ADAPTERS, 2, RANK, HEAD_DIM), (4 * RANK) ** -0.5, 0.75),
        "o_adapt_in": normal_values(splits[18], (ADAPTERS, RANK, QDIM), QDIM ** -0.5, 0.1875),
        "o_adapt_out": normal_values(splits[19], (ADAPTERS, RANK, D), (4 * RANK) ** -0.5, 0.75),
        "mlp_adapt_in": normal_values(splits[20], (ADAPTERS, 2, RANK, D), D ** -0.5, 0.1875),
        "mlp_adapt_out": normal_values(splits[21], (ADAPTERS, 2, RANK, FF), (4 * RANK) ** -0.5, 0.75),
        "down_adapt_in": normal_values(splits[22], (ADAPTERS, RANK, FF), FF ** -0.5, 0.078125),
        "down_adapt_out": normal_values(splits[23], (ADAPTERS, RANK, D), (4 * RANK) ** -0.5, 0.75),
    }


epsilon = 1e-06
softcap = 50.0
masked_value = -1000000000.0
highest = lax.Precision.HIGHEST

@jax.custom_vjp
def low(v):
    return lax.optimization_barrier(v.astype(jnp.bfloat16)).astype(jnp.float32)

@jax.custom_vjp
def low_back(v):
    return v

def low_keep(v):
    return (low(v), None)

def low_pass(kept, grad):
    return (grad,)

def back_keep(v):
    return (v, None)

def back_low(kept, grad):
    return (low(grad),)
low.defvjp(low_keep, low_pass)
low_back.defvjp(back_keep, back_low)

def normed(values, gain_vector):
    return values * lax.rsqrt(lax.optimization_barrier(jnp.mean(values * values, -1, keepdims=True)) + epsilon) * gain_vector

def adapted(inputs, weight, down_part, up_part):
    latent = low(low_back(jnp.dot(inputs, down_part.T, precision=highest)))
    return jnp.dot(inputs, weight, precision=highest) + jnp.dot(latent, up_part, precision=highest)

def attention(queries, key_rows, value_rows, segments):
    length = queries.shape[0]
    block_rows = min(512, length)
    score_scale = HEAD_DIM ** (-0.5)
    starts = jnp.arange(0, length, block_rows).astype(jnp.int32)
    key_pos = jnp.arange(length, dtype=jnp.int32)

    def one_block(row_start):
        query_block = lax.dynamic_slice_in_dim(queries, row_start, block_rows, 0)
        raw_scores = low_back(jnp.einsum('bhe,ke->hbk', query_block, key_rows, precision=highest))
        capped = softcap * jnp.tanh(raw_scores * (score_scale / softcap))
        query_seg = lax.dynamic_slice_in_dim(segments, row_start, block_rows, 0)
        query_pos = row_start + jnp.arange(block_rows, dtype=jnp.int32)
        allowed = (query_seg[:, None] == segments[None, :]) & (key_pos[None, :] <= query_pos[:, None])
        allowed = allowed[None]
        shown_scores = jnp.where(allowed, capped, masked_value)
        row_peak = lax.optimization_barrier(jnp.max(shown_scores, -1, keepdims=True))
        exponent = jnp.where(allowed, jnp.exp(shown_scores - row_peak), 0.0)
        row_total = lax.optimization_barrier(jnp.sum(exponent, -1, keepdims=True))
        probabilities = low(exponent / row_total)
        return jnp.einsum('hbk,ke->bhe', probabilities, value_rows, precision=highest)
    blocks = lax.map(jax.checkpoint(one_block), starts)
    return blocks.reshape(length, queries.shape[1], queries.shape[2])

def layer(inputs, picked, gains, weights, segments):
    qkv_in, q_out, kv_out, o_in, o_out, mlp_in, mlp_out, down_in, down_out = picked
    gain_first, gain_second, gain_third, gain_fourth = gains
    query_w, key_w, value_w, out_w, gate_w, up_w, down_w = weights
    length = inputs.shape[0]
    first = low(normed(inputs, gain_first))
    queries = low(low_back(adapted(first, query_w, qkv_in[0], q_out)))
    key_rows = low(low_back(adapted(first, key_w, qkv_in[1], kv_out[0])))
    value_rows = low(low_back(adapted(first, value_w, qkv_in[2], kv_out[1])))
    context = attention(queries.reshape(length, HEADS, HEAD_DIM), key_rows, value_rows, segments)
    context = low(low_back(context.reshape(length, HEADS * HEAD_DIM)))
    attn_proj = low_back(adapted(context, out_w, o_in, o_out))
    mixed = inputs + normed(attn_proj, gain_second)
    second = low(normed(mixed, gain_third))
    gate = low_back(adapted(second, gate_w, mlp_in[0], mlp_out[0]))
    upward = low_back(adapted(second, up_w, mlp_in[1], mlp_out[1]))
    hidden = low(jax.nn.gelu(gate, approximate=True) * upward)
    down_proj = low_back(adapted(hidden, down_w, down_in, down_out))
    return mixed + normed(down_proj, gain_fourth)

def reference(layer_input, out_grad, segment_ids, adapter_ids, gain_attn_in, gain_attn_out, gain_mlp_in, gain_mlp_out, w_query, w_key, w_value, w_out, w_gate, w_up, w_down, qkv_adapt_in, q_adapt_out, kv_adapt_out, o_adapt_in, o_adapt_out, mlp_adapt_in, mlp_adapt_out, down_adapt_in, down_adapt_out):
    gains = (gain_attn_in.astype(jnp.float32), gain_attn_out.astype(jnp.float32), gain_mlp_in.astype(jnp.float32), gain_mlp_out.astype(jnp.float32))
    weights = tuple((weight.astype(jnp.float32) for weight in (w_query, w_key, w_value, w_out, w_gate, w_up, w_down)))
    tables = tuple((adapter_table.astype(jnp.float32) for adapter_table in (qkv_adapt_in, q_adapt_out, kv_adapt_out, o_adapt_in, o_adapt_out, mlp_adapt_in, mlp_adapt_out, down_adapt_in, down_adapt_out)))

    def per_sequence(totals, item):
        inputs, cotangent, segments, chosen = item
        picked = tuple((adapter_table[chosen] for adapter_table in tables))

        def forward(input_rows, picked_rows):
            return layer(input_rows, picked_rows, gains, weights, segments)
        output, pull = jax.vjp(forward, inputs.astype(jnp.float32), picked)
        input_cot, picked_cot = pull(cotangent.astype(jnp.float32))
        totals = tuple((running.at[chosen].add(update) for running, update in zip(totals, picked_cot)))
        return (totals, (output.astype(jnp.bfloat16), input_cot.astype(jnp.bfloat16)))
    start_totals = tuple((jnp.zeros(adapter_table.shape, jnp.float32) for adapter_table in tables))
    totals, outputs = lax.scan(per_sequence, start_totals, (layer_input, out_grad, segment_ids, adapter_ids.astype(jnp.int32)))
    return (outputs[0], outputs[1], totals[0], totals[1], totals[2], totals[3], totals[4], totals[5], totals[6], totals[7], totals[8])
```

```python
import functools

import jax
import jax.numpy as jnp
from jax import lax
from jax.experimental import pallas as pl
from jax.experimental.pallas import tpu as pltpu
from jax.sharding import PartitionSpec as P

epsilon = 1e-06
softcap = 50.0
highest = lax.Precision.HIGHEST
MESH = pl.DeviceIdType.MESH
bf16 = jnp.bfloat16
f32 = jnp.float32

D = 1152
SEQ = 4
ROWS = 256
UNITS = 54
BLOCK = 64
TILE = 256
MIB = 1 << 20


def dot(a, b):
    return lax.dot_general(a, b, (((1,), (0,)), ((), ())), preferred_element_type=f32)


def dot_nt(a, b):
    return lax.dot_general(a, b, (((1,), (1,)), ((), ())), preferred_element_type=f32)


def dot_tn(a, b):
    return lax.dot_general(a, b, (((0,), (0,)), ((), ())), preferred_element_type=f32)


def normed(values, gain_vector):
    return values * lax.rsqrt(jnp.mean(values * values, -1, keepdims=True) + epsilon) * gain_vector


def norm_back(values, gain_vector, cotangent):
    inverse = lax.rsqrt(jnp.mean(values * values, -1, keepdims=True) + epsilon)
    scaled = cotangent * gain_vector
    mean_part = jnp.mean(scaled * values, -1, keepdims=True)
    return inverse * (scaled - values * (inverse * inverse * mean_part))


def seq_peers():
    dp, me = lax.axis_index("dp"), lax.axis_index("seq")
    return [(dp, lax.rem(me + shift, SEQ)) for shift in (1, 2, 3)]


def greet(peers):
    barrier = pltpu.get_barrier_semaphore()
    for peer in peers:
        pl.semaphore_signal(barrier, inc=1, device_id=peer, device_id_type=MESH)
    pl.semaphore_wait(barrier, len(peers))


def mlp_kernel(
    tokens, w_gate, w_up, w_down, first_gu, second_gate, second_up, first_down, second_down,
    mixed, out_grad, gain_in, gain_out,
    layer_out, mixed_grad, grad_gate_out, grad_up_out, grad_down_in, grad_gu_in, grad_down_out,
    act_gate, act_up, hidden, latents, down_latents, down_grads, total, thin, thin_gu,
    send_one, recv_one, send_two, recv_two,
    send_sem, recv_sem,
):
    me = lax.axis_index("seq")
    peers = seq_peers()
    steps = w_gate.shape[0]
    greet(peers)

    def forward(chunk):
        rows = tokens[chunk]
        latent = dot_nt(rows, first_gu[...]).astype(bf16)
        latents[chunk] = latent
        total[...] = jnp.zeros_like(total)
        thin[...] = jnp.zeros_like(thin)

        def step(j, _):
            gate = dot_nt(rows, w_gate[j]) + dot(latent, second_gate[j])
            upward = dot_nt(rows, w_up[j]) + dot(latent, second_up[j])
            inner = 0.7978845608028654 * (gate + 0.044715 * (gate * gate * gate))
            bent = jnp.tanh(inner)
            half = 0.5 * (1.0 + bent)
            gelu = gate * half
            slope = half + 0.5 * gate * (1.0 - bent * bent) * (
                0.7978845608028654 * (1.0 + 0.134145 * (gate * gate))
            )
            act_gate[j, chunk] = gelu
            act_up[j, chunk] = upward * slope
            mid = (gelu * upward).astype(bf16)
            hidden[j, chunk] = mid
            total[...] += dot(mid, w_down[j])
            thin[...] += dot_nt(mid, first_down[j])
            return 0

        lax.fori_loop(0, steps, step, 0)
        down_latent = thin[...].astype(bf16)
        down_latents[chunk] = down_latent
        return total[...] + dot(down_latent, second_down[...])

    def copy(src, dst, peer, slot):
        return pltpu.make_async_remote_copy(
            src_ref=src, dst_ref=dst, send_sem=send_sem.at[slot], recv_sem=recv_sem.at[slot],
            device_id=peer, device_id_type=MESH,
        )

    sent = []
    for shift in (2, 1, 3):
        chunk = lax.rem(me + shift, SEQ)
        send_one[shift - 1] = forward(chunk).astype(bf16)
        moving = copy(send_one.at[shift - 1], recv_one.at[shift - 1], peers[shift - 1], shift - 1)
        moving.start()
        sent.append(moving)
    down_proj = forward(me)
    for moving in sent:
        moving.wait()
    for slot in range(3):
        down_proj = down_proj + recv_one[slot].astype(f32)
    cotangent = out_grad[...].astype(f32)
    layer_out[...] = (mixed[...] + normed(down_proj, gain_out[...])).astype(bf16)
    down_grads[me] = norm_back(down_proj, gain_out[...], cotangent).astype(bf16)
    gathered = []
    for shift in (1, 3, 2):
        moving = copy(down_grads.at[me], down_grads.at[me], peers[shift - 1], 2 + shift)
        moving.start()
        gathered.append(moving)

    grad_gate_out[...] = jnp.zeros_like(grad_gate_out)
    grad_up_out[...] = jnp.zeros_like(grad_up_out)
    grad_down_in[...] = jnp.zeros_like(grad_down_in)
    grad_gu_in[...] = jnp.zeros_like(grad_gu_in)
    grad_down_out[...] = jnp.zeros_like(grad_down_out)

    def backward(chunk):
        rows = down_grads[chunk]
        latent = latents[chunk]
        latent_grad = dot_nt(rows, second_down[...]).astype(bf16)
        total[...] = jnp.zeros_like(total)
        thin_gu[...] = jnp.zeros_like(thin_gu)

        def step(j, _):
            hidden_grad = dot_nt(rows, w_down[j]) + dot(latent_grad, first_down[j])
            gate_grad = (hidden_grad * act_up[j, chunk]).astype(bf16)
            up_grad = (hidden_grad * act_gate[j, chunk]).astype(bf16)
            total[...] += dot(gate_grad, w_gate[j]) + dot(up_grad, w_up[j])
            thin_gu[...] += dot_nt(gate_grad, second_gate[j]) + dot_nt(up_grad, second_up[j])
            grad_gate_out[j] += dot_tn(latent, gate_grad)
            grad_up_out[j] += dot_tn(latent, up_grad)
            grad_down_in[j] += dot_tn(latent_grad, hidden[j, chunk])
            return 0

        lax.fori_loop(0, steps, step, 0)
        gu_grad = thin_gu[...].astype(bf16)
        grad_gu_in[...] += dot_tn(gu_grad, tokens[chunk])
        grad_down_out[...] += dot_tn(down_latents[chunk], rows)
        return total[...] + dot(gu_grad, first_gu[...])

    own = backward(me)
    returned = []
    for order, shift in ((0, 1), (1, 3), (2, 2)):
        gathered[order].wait()
        source = SEQ - shift
        chunk = lax.rem(me + source, SEQ)
        send_two[source - 1] = backward(chunk).astype(bf16)
        moving = copy(send_two.at[source - 1], recv_two.at[source - 1], peers[source - 1], 5 + source)
        moving.start()
        returned.append(moving)
    for moving in returned:
        moving.wait()
    for slot in range(3):
        own = own + recv_two[slot].astype(f32)
    mixed_grad[...] = cotangent + norm_back(mixed[...], gain_in[...], own)


def feed_forward(*arrays):
    steps = arrays[1].shape[0]
    vmem = pl.BlockSpec(memory_space=pltpu.VMEM)
    outs = [
        jax.ShapeDtypeStruct((ROWS, D), bf16),
        jax.ShapeDtypeStruct((ROWS, D), f32),
        jax.ShapeDtypeStruct((steps, 32, TILE), f32),
        jax.ShapeDtypeStruct((steps, 32, TILE), f32),
        jax.ShapeDtypeStruct((steps, 16, TILE), f32),
        jax.ShapeDtypeStruct((32, D), f32),
        jax.ShapeDtypeStruct((16, D), f32),
    ]
    return pl.pallas_call(
        mlp_kernel,
        out_shape=outs,
        in_specs=[vmem] * len(arrays),
        out_specs=[vmem] * len(outs),
        scratch_shapes=[
            pltpu.VMEM((steps, SEQ, ROWS, TILE), f32),
            pltpu.VMEM((steps, SEQ, ROWS, TILE), f32),
            pltpu.VMEM((steps, SEQ, ROWS, TILE), bf16),
            pltpu.VMEM((SEQ, ROWS, 32), bf16),
            pltpu.VMEM((SEQ, ROWS, 16), bf16),
            pltpu.VMEM((SEQ, ROWS, D), bf16),
            pltpu.VMEM((ROWS, D), f32),
            pltpu.VMEM((ROWS, 16), f32),
            pltpu.VMEM((ROWS, 32), f32),
            pltpu.VMEM((3, ROWS, D), bf16),
            pltpu.VMEM((3, ROWS, D), bf16),
            pltpu.VMEM((3, ROWS, D), bf16),
            pltpu.VMEM((3, ROWS, D), bf16),
            pltpu.SemaphoreType.DMA((9,)),
            pltpu.SemaphoreType.DMA((9,)),
        ],
        compiler_params=pltpu.CompilerParams(
            collective_id=1, has_side_effects=True, vmem_limit_bytes=62 * MIB
        ),
        name="feed_forward",
    )(*arrays)


def project(inputs, weight_rows, down_sel, up_sel):
    latent = dot_nt(inputs, down_sel).astype(bf16)
    return dot_nt(inputs, weight_rows) + dot(latent, up_sel), latent


def project_back(grad_rows, weight_rows, down_sel, up_sel, inputs, latent):
    latent_grad = dot_nt(grad_rows, up_sel).astype(bf16)
    input_cot = dot(grad_rows, weight_rows) + dot(latent_grad, down_sel)
    return input_cot, dot_tn(latent_grad, inputs), dot_tn(latent, grad_rows)


def my_quarter(rows, axis):
    me = lax.axis_index("seq")
    part = lax.dynamic_slice_in_dim(rows, me * UNITS, UNITS, axis)
    widths = [(0, 0)] * rows.ndim
    widths[axis] = (0, BLOCK - UNITS)
    return jnp.pad(part, widths)


def body(
    layer_input, out_grad, segment_ids, adapter_ids,
    gain_attn_in, gain_attn_out, gain_mlp_in, gain_mlp_out,
    w_query, w_key, w_value, w_out, w_gate, w_up, w_down,
    qkv_adapt_in, q_adapt_out, kv_adapt_out, o_adapt_in, o_adapt_out,
    mlp_adapt_in, mlp_adapt_out, down_adapt_in, down_adapt_out,
):
    me = lax.axis_index("seq")
    shards = 32
    x = layer_input[0].astype(f32)
    cotangent = out_grad[0]
    chosen = adapter_ids[0]
    pick = lambda table: lax.dynamic_index_in_dim(table, chosen, 0, keepdims=False)
    qkv_in, q_out, kv_out = pick(qkv_adapt_in), pick(q_adapt_out), pick(kv_adapt_out)
    o_in, o_out = pick(o_adapt_in), pick(o_adapt_out)
    mlp_in, mlp_out = pick(mlp_adapt_in), pick(mlp_adapt_out)
    down_in, down_out = pick(down_adapt_in), pick(down_adapt_out)

    attn_pack = jnp.concatenate([w_query.T, w_key.T, w_value.T, w_out], 0)
    attn_all = lax.all_gather(attn_pack, "dp", axis=0, tiled=False)
    wq = attn_all[:, :32].reshape(1024, D)
    wk = attn_all[:, 32:40].reshape(256, D)
    wv = attn_all[:, 40:48].reshape(256, D)
    wo = attn_all[:, 48:].reshape(1024, D)
    mlp_pack = jnp.stack([my_quarter(w_gate.T, 0), my_quarter(w_up.T, 0), my_quarter(w_down, 0)])
    mlp_all = lax.all_gather(mlp_pack, "dp", axis=1, tiled=True)
    steps = shards * BLOCK // TILE
    mlp_all = mlp_all.reshape(3, steps, TILE, D)

    def hidden_slice(table):
        part = my_quarter(table.reshape(16, shards, 216), 2)
        return part.reshape(16, steps, TILE).transpose(1, 0, 2)

    zeros = jnp.zeros((steps, 16, TILE), bf16)
    second_gate = jnp.concatenate([hidden_slice(mlp_out[0]), zeros], 1)
    second_up = jnp.concatenate([zeros, hidden_slice(mlp_out[1])], 1)
    first_down = hidden_slice(down_in)

    first_norm = normed(x, gain_attn_in).astype(bf16)
    q, q_latent = project(first_norm, wq, qkv_in[0], q_out)
    k, k_latent = project(first_norm, wk, qkv_in[1], kv_out[0])
    v, v_latent = project(first_norm, wv, qkv_in[2], kv_out[1])
    q = q.astype(bf16).reshape(ROWS, 4, 256)
    kv = jnp.concatenate([k, v], 1).astype(bf16)
    kv_all = lax.all_gather(kv, "seq", axis=0, tiled=True)
    keys, values = kv_all[:, :256], kv_all[:, 256:]
    segments = segment_ids[0]
    mine = lax.dynamic_slice_in_dim(segments, me * ROWS, ROWS)
    position = me * ROWS + jnp.arange(ROWS)
    allowed = (mine[:, None] == segments[None]) & (jnp.arange(1024)[None] <= position[:, None])
    scale = 1.0 / 16.0
    raw = jnp.einsum("qhe,ke->hqk", q, keys, preferred_element_type=f32)
    bent = jnp.tanh(raw * (scale / softcap))
    exponent = jnp.where(allowed[None], jnp.exp(softcap * bent), 0.0)
    probs = exponent / jnp.sum(exponent, -1, keepdims=True)
    probs_low = probs.astype(bf16)
    context = jnp.einsum("hqk,ke->qhe", probs_low, values, preferred_element_type=f32)
    context = context.astype(bf16).reshape(ROWS, 1024)
    o_latent = dot_nt(context, o_in).astype(bf16)
    attn_proj = dot(context, wo) + dot(o_latent, o_out)
    mixed = x + normed(attn_proj, gain_attn_out)
    second_norm = normed(mixed, gain_mlp_in).astype(bf16)
    tokens = lax.all_gather(second_norm, "seq", axis=0, tiled=False)

    layer_out, mixed_grad, g_gate, g_up, g_down_in, g_gu_in, g_down_out = feed_forward(
        tokens, mlp_all[0], mlp_all[1], mlp_all[2], mlp_in.reshape(32, D),
        second_gate, second_up, first_down, down_out,
        mixed, cotangent, gain_mlp_in[None], gain_mlp_out[None],
    )

    def hidden_full(part):
        part = part.transpose(1, 0, 2).reshape(16, shards, BLOCK)[:, :, :UNITS]
        full = jnp.zeros((16, shards, 4, UNITS), f32)
        full = lax.dynamic_update_slice_in_dim(full, part[:, :, None], me, 2)
        return full.reshape(16, shards * 4 * UNITS)

    attn_grad = norm_back(attn_proj, gain_attn_out, mixed_grad).astype(bf16)
    o_latent_grad = dot_nt(attn_grad, o_out).astype(bf16)
    context_grad = (dot_nt(attn_grad, wo) + dot(o_latent_grad, o_in)).astype(bf16)
    g_o_in = dot_tn(o_latent_grad, context)
    g_o_out = dot_tn(o_latent, attn_grad)
    head_grads = context_grad.reshape(ROWS, 4, 256)
    prob_grad = jnp.einsum("qhe,ke->hqk", head_grads, values, preferred_element_type=f32)
    centre = jnp.sum(probs * prob_grad, -1, keepdims=True)
    raw_grad = (probs * (prob_grad - centre) * (1.0 - bent * bent) * scale).astype(bf16)
    q_grad = jnp.einsum("hqk,ke->qhe", raw_grad, keys, preferred_element_type=f32)
    q_grad = q_grad.astype(bf16).reshape(ROWS, 1024)
    k_part = jnp.einsum("hqk,qhe->ke", raw_grad, q, preferred_element_type=f32)
    v_part = jnp.einsum("hqk,qhe->ke", probs_low, head_grads, preferred_element_type=f32)
    kv_grad = lax.psum_scatter(
        jnp.concatenate([k_part, v_part], 1).astype(bf16), "seq", scatter_dimension=0, tiled=True
    )
    k_grad, v_grad = kv_grad[:, :256], kv_grad[:, 256:]
    q_cot, g_q_in, g_q_out = project_back(q_grad, wq, qkv_in[0], q_out, first_norm, q_latent)
    k_cot, g_k_in, g_k_out = project_back(k_grad, wk, qkv_in[1], kv_out[0], first_norm, k_latent)
    v_cot, g_v_in, g_v_out = project_back(v_grad, wv, qkv_in[2], kv_out[1], first_norm, v_latent)
    input_grad = (mixed_grad + norm_back(x, gain_attn_in, q_cot + k_cot + v_cot)).astype(bf16)

    picked = (
        jnp.stack([g_q_in, g_k_in, g_v_in]),
        g_q_out,
        jnp.stack([g_k_out, g_v_out]),
        g_o_in,
        g_o_out,
        g_gu_in.reshape(2, 16, D),
        jnp.stack([hidden_full(g_gate[:, :16]), hidden_full(g_up[:, 16:])]),
        hidden_full(g_down_in),
        g_down_out,
    )
    chooser = (chosen == jnp.arange(8)).astype(f32)
    spread = tuple(chooser.reshape((8,) + (1,) * g.ndim) * g[None] for g in picked)
    summed = lax.psum(spread, ("dp", "seq"))
    return (layer_out[None], input_grad[None]) + tuple(summed)


def solution(mesh):
    tokens = P("dp", "seq", None)
    columns, rows = P(None, "dp"), P("dp", None)
    placed = (
        (tokens, tokens, P("dp", None), P("dp"))
        + (P(),) * 4
        + (columns, columns, columns, rows, columns, columns, rows)
        + (P(),) * 9
    )
    return jax.shard_map(
        body,
        mesh=mesh,
        in_specs=placed,
        out_specs=(tokens, tokens) + (P(),) * 9,
        check_vma=False,
    )
```

```python
import functools

import jax
import jax.numpy as jnp
from jax import lax
from jax.experimental import pallas as pl
from jax.experimental.pallas import tpu as pltpu
from jax.sharding import PartitionSpec as P

epsilon = 1e-06
softcap = 50.0
MESH = pl.DeviceIdType.MESH
bf16 = jnp.bfloat16
f32 = jnp.float32

D = 1152
SEQ = 4
ROWS = 256
UNITS = 54
BLOCK = 64
TILE = 256
MIB = 1 << 20


def dot(a, b):
    return lax.dot_general(a, b, (((1,), (0,)), ((), ())), preferred_element_type=f32)


def dot_nt(a, b):
    return lax.dot_general(a, b, (((1,), (1,)), ((), ())), preferred_element_type=f32)


def dot_tn(a, b):
    return lax.dot_general(a, b, (((0,), (0,)), ((), ())), preferred_element_type=f32)


def normed(values, gain_vector):
    return values * lax.rsqrt(jnp.mean(values * values, -1, keepdims=True) + epsilon) * gain_vector


def norm_back(values, gain_vector, cotangent):
    inverse = lax.rsqrt(jnp.mean(values * values, -1, keepdims=True) + epsilon)
    scaled = cotangent * gain_vector
    mean_part = jnp.mean(scaled * values, -1, keepdims=True)
    return inverse * (scaled - values * (inverse * inverse * mean_part))


def seq_peers():
    dp, me = lax.axis_index("dp"), lax.axis_index("seq")
    return [(dp, lax.rem(me + shift, SEQ)) for shift in (1, 2, 3)]


def greet(peers):
    barrier = pltpu.get_barrier_semaphore()
    for peer in peers:
        pl.semaphore_signal(barrier, inc=1, device_id=peer, device_id_type=MESH)
    pl.semaphore_wait(barrier, len(peers))


def place():
    dp = lax.axis_index("dp")
    return lax.axis_index("seq"), dp // 8, lax.rem(dp // 2, 4), lax.rem(dp, 2)


def at(x, y, z, core):
    return ((lax.rem(y, 4) * 4 + lax.rem(z, 4)) * 2 + core, lax.rem(x, 4))


def plane_peers():
    x, y, z, core = place()
    return [at(x, y + k, z, core) for k in (1, 2, 3)] + [at(x, y, z + k, core) for k in (1, 2, 3)]


def sibling():
    x, y, z, core = place()
    return at(x, y, z, 1 - core)


def remote(src, dst, send_sem, recv_sem, peer):
    return pltpu.make_async_remote_copy(
        src_ref=src, dst_ref=dst, send_sem=send_sem, recv_sem=recv_sem,
        device_id=peer, device_id_type=MESH,
    )


class PlaneGather:
    def __init__(self, own, buffer, send_sem, recv_sem):
        self.x, self.y, self.z, self.core = place()
        self.own, self.buffer, self.send, self.recv = own, buffer, send_sem, recv_sem

    def _copy(self, src, dst, slot, peer):
        return remote(src, dst, self.send.at[slot], self.recv.at[slot], peer)

    def _first(self, k):
        x, y, z, core = self.x, self.y, self.z, self.core
        peer = at(x, y + k * (1 - core), z + k * core, core)
        return self._copy(self.own, self.buffer.at[y, z, core], k - 1, peer)

    def _line(self, core, back):
        if core == 0:
            return self.buffer.at[:, lax.rem(self.z + 4 - back, 4), 0]
        return self.buffer.at[lax.rem(self.y + 4 - back, 4), :, 1]

    def _second(self, core, k):
        line = self._line(core, 0)
        peer = at(self.x, self.y + k * core, self.z + k * (1 - core), core)
        return self._copy(line, line, 2 + k, peer)

    def _swap(self, core, back):
        line = self._line(core, back)
        return self._copy(line, line, 6 + back, at(self.x, self.y, self.z, 1 - core))

    def _both(self, act):
        for core in (0, 1):
            pl.when(self.core == core)(functools.partial(act, core))

    def start(self):
        for k in (1, 2, 3):
            self._first(k).start()

    def middle(self):
        for k in (1, 2, 3):
            self._first(k).wait()

        def act(core):
            for k in (1, 3, 2):
                self._second(core, k).start()
            self._swap(core, 0).start()

        self._both(act)

    def late(self):
        def act(core):
            for k in (1, 3, 2):
                self._second(core, k).wait()
                self._swap(core, k).start()

        self._both(act)

    def finish(self):
        def act(core):
            for back in range(4):
                self._swap(core, back).wait()

        self._both(act)


def allowed_pairs(segment_rows, segment_column, me, chunk):
    keys = lax.broadcasted_iota(jnp.int32, (ROWS, ROWS), 1) + chunk * ROWS
    queries = lax.broadcasted_iota(jnp.int32, (ROWS, ROWS), 0) + me * ROWS
    return (segment_column[...] == segment_rows[chunk]) & (keys <= queries)


SCORE = 1.0 / 16.0


def attention_kernel(
    layer_input, pack_qkv, pack_o, pack_gu, pack_down, segment_rows, segment_column,
    gain_first, gain_second, gain_third,
    first_qkv, second_q, second_kv, first_o, second_o,
    all_gu, all_down, all_tokens, out_qkv, out_kv_rows, out_o, out_kv,
    queries, totals, context, attn_proj, mixed, qkv_latent, o_latent,
    got_qkv, got_o, kv_rows, first_norm, kv_all, second_norm,
    sem_s, sem_r, kv_s, kv_r, tok_s, tok_r, loc,
):
    me, y, z, core = place()
    line = seq_peers()
    greet(line + plane_peers() + [sibling()])
    gathers = [
        PlaneGather(own, got, sem_s.at[i], sem_r.at[i])
        for i, (own, got) in enumerate(
            ((pack_qkv, got_qkv), (pack_o, got_o), (pack_gu, all_gu), (pack_down, all_down))
        )
    ]
    g_qkv, g_o, g_gu, g_down = gathers
    own_copies = [
        pltpu.make_async_copy(g.own, g.buffer.at[y, z, core], loc.at[i])
        for i, g in enumerate(gathers)
    ]
    g_qkv.start()
    for moving in own_copies:
        moving.start()
    values = layer_input[...].astype(f32)
    first_norm[...] = normed(values, gain_first[...]).astype(bf16)
    latent = dot_nt(first_norm[...], first_qkv[...]).astype(bf16)
    qkv_latent[...] = latent
    for moving in own_copies:
        moving.wait()
    g_qkv.middle()
    g_o.start()
    g_qkv.late()
    g_o.middle()
    g_gu.start()
    g_qkv.finish()

    def unmix(i, _):
        pairs = got_qkv[i, :, :, 32:48].astype(f32).reshape(8, 2, 8, D)
        kv_rows[pl.ds(i * 64, 64)] = pairs[:, 0].reshape(64, D).astype(bf16)
        kv_rows[pl.ds(256 + i * 64, 64)] = pairs[:, 1].reshape(64, D).astype(bf16)
        return 0

    lax.fori_loop(0, 4, unmix, 0)
    kv = dot_nt(first_norm[...], kv_rows[...]) + dot(latent, second_kv[...])
    kv_all[me] = kv.astype(bf16)

    def kv_copy(shift):
        return remote(kv_all.at[me], kv_all.at[me], kv_s.at[shift - 1], kv_r.at[shift - 1], line[shift - 1])

    for shift in (1, 2, 3):
        pl.when(me + shift < SEQ)(lambda shift=shift: kv_copy(shift).start())

    def query(h, _):
        rows = got_qkv[h, :, :, 0:32].reshape(256, D)
        queries[h] = (dot_nt(first_norm[...], rows) + dot(latent, second_q[h])).astype(bf16)
        context[h] = jnp.zeros((ROWS, 256), f32)
        totals[h] = jnp.zeros((ROWS, 1), f32)
        return 0

    lax.fori_loop(0, 4, query, 0)
    g_gu.middle()
    g_down.start()

    def attend(chunk):
        keys, held = kv_all[chunk, :, 0:256], kv_all[chunk, :, 256:512]
        allowed = allowed_pairs(segment_rows, segment_column, me, chunk)

        def head(h, _):
            bent = jnp.tanh(dot_nt(queries[h], keys) * (SCORE / softcap))
            weight = jnp.where(allowed, jnp.exp(softcap * bent), 0.0).astype(bf16)
            totals[h] += jnp.sum(weight.astype(f32), -1, keepdims=True)
            context[h] += dot(weight, held)
            return 0

        lax.fori_loop(0, 4, head, 0)

    attend(me)
    g_o.late()
    g_o.finish()
    keep = [
        pltpu.make_async_copy(got_qkv, out_qkv, loc.at[0]),
        pltpu.make_async_copy(got_o, out_o, loc.at[1]),
        pltpu.make_async_copy(kv_rows, out_kv_rows, loc.at[2]),
    ]
    for moving in keep:
        moving.start()
    for shift in (1, 2, 3):
        def arrived(shift=shift):
            kv_copy(shift).wait_recv()
            attend(me - shift)

        pl.when(me >= shift)(arrived)

    total = jnp.zeros((ROWS, D), f32)
    thin = jnp.zeros((ROWS, 16), f32)
    for h in range(4):
        context[h] = context[h] / totals[h]
        low = context[h].astype(bf16)
        total = total + dot(low, got_o[h].reshape(256, D))
        thin = thin + dot_nt(low, first_o[h])
    o_latent[...] = thin.astype(bf16)
    proj = total + dot(o_latent[...], second_o[...])
    attn_proj[...] = proj
    mid = values + normed(proj, gain_second[...])
    mixed[...] = mid
    second_norm[...] = normed(mid, gain_third[...]).astype(bf16)
    spread = [remote(second_norm, all_tokens.at[me], tok_s.at[i], tok_r.at[i], line[i]) for i in range(3)]
    for moving in spread:
        moving.start()
    mine = pltpu.make_async_copy(second_norm, all_tokens.at[me], loc.at[3])
    mine.start()
    g_gu.late()
    g_down.middle()
    g_gu.finish()
    g_down.late()
    g_down.finish()
    kept_kv = pltpu.make_async_copy(kv_all, out_kv, loc.at[4])
    kept_kv.start()
    for moving in keep + [mine, kept_kv]:
        moving.wait()
    for moving in spread:
        moving.wait()
    for shift in (1, 2, 3):
        pl.when(me + shift < SEQ)(lambda shift=shift: kv_copy(shift).wait_send())


def attention_forward(*arrays):
    vmem = pl.BlockSpec(memory_space=pltpu.VMEM)
    hbm = pl.BlockSpec(memory_space=pl.ANY)
    shape = jax.ShapeDtypeStruct
    outs = [
        (shape((4, 4, 2, 128, D), bf16), hbm),
        (shape((4, 4, 2, 64, D), bf16), hbm),
        (shape((SEQ, ROWS, D), bf16), hbm),
        (shape((4, 4, 2, 48, D), bf16), hbm),
        (shape((512, D), bf16), hbm),
        (shape((4, 4, 2, 32, D), bf16), hbm),
        (shape((SEQ, ROWS, 512), bf16), hbm),
        (shape((4, ROWS, 256), bf16), vmem),
        (shape((4, ROWS, 1), f32), vmem),
        (shape((4, ROWS, 256), f32), vmem),
        (shape((ROWS, D), f32), vmem),
        (shape((ROWS, D), f32), vmem),
        (shape((ROWS, 48), bf16), vmem),
        (shape((ROWS, 16), bf16), vmem),
    ]
    ins = [vmem, vmem, vmem, hbm, hbm] + [vmem] * (len(arrays) - 5)
    dma = pltpu.SemaphoreType.DMA
    return pl.pallas_call(
        attention_kernel,
        out_shape=[s for s, _ in outs],
        in_specs=ins,
        out_specs=[m for _, m in outs],
        scratch_shapes=[
            pltpu.VMEM((4, 4, 2, 48, D), bf16),
            pltpu.VMEM((4, 4, 2, 32, D), bf16),
            pltpu.VMEM((512, D), bf16),
            pltpu.VMEM((ROWS, D), bf16),
            pltpu.VMEM((SEQ, ROWS, 512), bf16),
            pltpu.VMEM((ROWS, D), bf16),
            dma((4, 10)), dma((4, 10)), dma((3,)), dma((3,)), dma((3,)), dma((3,)), dma((5,)),
        ],
        compiler_params=pltpu.CompilerParams(
            collective_id=2, has_side_effects=True, vmem_limit_bytes=60 * MIB
        ),
        name="attention_forward",
    )(*arrays)


def mlp_kernel(
    tokens, w_gu, w_down, first_gu, second_gate, second_up, first_down, second_down,
    mixed, out_grad, gain_in, gain_out,
    layer_out, mixed_grad, grad_gate_out, grad_up_out, grad_down_in, grad_gu_in, grad_down_out,
    act_gate, act_up, hidden, latents, down_latents, down_grads, total, thin, thin_gu,
    send_one, recv_one, send_two, recv_two,
    send_sem, recv_sem,
):
    me = lax.axis_index("seq")
    peers = seq_peers()
    steps = second_gate.shape[0]
    greet(peers)

    def gate_rows(j):
        return w_gu[j // 2, pl.ds(2 * lax.rem(j, 2), 2), :, 0:64].reshape(TILE, D)

    def up_rows(j):
        return w_gu[j // 2, pl.ds(2 * lax.rem(j, 2), 2), :, 64:128].reshape(TILE, D)

    def down_rows(j):
        return w_down[j // 2, pl.ds(2 * lax.rem(j, 2), 2)].reshape(TILE, D)

    def forward(chunk):
        rows = tokens[chunk]
        latent = dot_nt(rows, first_gu[...]).astype(bf16)
        latents[chunk] = latent
        total[...] = jnp.zeros_like(total)
        thin[...] = jnp.zeros_like(thin)

        def step(j, _):
            gate = dot_nt(rows, gate_rows(j)) + dot(latent, second_gate[j])
            upward = dot_nt(rows, up_rows(j)) + dot(latent, second_up[j])
            inner = 0.7978845608028654 * (gate + 0.044715 * (gate * gate * gate))
            bent = jnp.tanh(inner)
            half = 0.5 * (1.0 + bent)
            gelu = gate * half
            slope = half + 0.5 * gate * (1.0 - bent * bent) * (
                0.7978845608028654 * (1.0 + 0.134145 * (gate * gate))
            )
            act_gate[j, chunk] = gelu
            act_up[j, chunk] = upward * slope
            mid = (gelu * upward).astype(bf16)
            hidden[j, chunk] = mid
            total[...] += dot(mid, down_rows(j))
            thin[...] += dot_nt(mid, first_down[j])
            return 0

        lax.fori_loop(0, steps, step, 0)
        down_latent = thin[...].astype(bf16)
        down_latents[chunk] = down_latent
        return total[...] + dot(down_latent, second_down[...])

    def copy(src, dst, peer, slot):
        return pltpu.make_async_remote_copy(
            src_ref=src, dst_ref=dst, send_sem=send_sem.at[slot], recv_sem=recv_sem.at[slot],
            device_id=peer, device_id_type=MESH,
        )

    sent = []
    for shift in (2, 1, 3):
        chunk = lax.rem(me + shift, SEQ)
        send_one[shift - 1] = forward(chunk).astype(bf16)
        moving = copy(send_one.at[shift - 1], recv_one.at[shift - 1], peers[shift - 1], shift - 1)
        moving.start()
        sent.append(moving)
    down_proj = forward(me)
    for moving in sent:
        moving.wait()
    for slot in range(3):
        down_proj = down_proj + recv_one[slot].astype(f32)
    cotangent = out_grad[...].astype(f32)
    layer_out[...] = (mixed[...] + normed(down_proj, gain_out[...])).astype(bf16)
    down_grads[me] = norm_back(down_proj, gain_out[...], cotangent).astype(bf16)
    gathered = []
    for shift in (1, 3, 2):
        moving = copy(down_grads.at[me], down_grads.at[me], peers[shift - 1], 2 + shift)
        moving.start()
        gathered.append(moving)

    grad_gate_out[...] = jnp.zeros_like(grad_gate_out)
    grad_up_out[...] = jnp.zeros_like(grad_up_out)
    grad_down_in[...] = jnp.zeros_like(grad_down_in)
    grad_gu_in[...] = jnp.zeros_like(grad_gu_in)
    grad_down_out[...] = jnp.zeros_like(grad_down_out)

    def backward(chunk):
        rows = down_grads[chunk]
        latent = latents[chunk]
        latent_grad = dot_nt(rows, second_down[...]).astype(bf16)
        total[...] = jnp.zeros_like(total)
        thin_gu[...] = jnp.zeros_like(thin_gu)

        def step(j, _):
            hidden_grad = dot_nt(rows, down_rows(j)) + dot(latent_grad, first_down[j])
            gate_grad = (hidden_grad * act_up[j, chunk]).astype(bf16)
            up_grad = (hidden_grad * act_gate[j, chunk]).astype(bf16)
            total[...] += dot(gate_grad, gate_rows(j)) + dot(up_grad, up_rows(j))
            thin_gu[...] += dot_nt(gate_grad, second_gate[j]) + dot_nt(up_grad, second_up[j])
            grad_gate_out[j] += dot_tn(latent, gate_grad)
            grad_up_out[j] += dot_tn(latent, up_grad)
            grad_down_in[j] += dot_tn(latent_grad, hidden[j, chunk])
            return 0

        lax.fori_loop(0, steps, step, 0)
        gu_grad = thin_gu[...].astype(bf16)
        grad_gu_in[...] += dot_tn(gu_grad, tokens[chunk])
        grad_down_out[...] += dot_tn(down_latents[chunk], rows)
        return total[...] + dot(gu_grad, first_gu[...])

    own = backward(me)
    returned = []
    for order, shift in ((0, 1), (1, 3), (2, 2)):
        gathered[order].wait()
        source = SEQ - shift
        chunk = lax.rem(me + source, SEQ)
        send_two[source - 1] = backward(chunk).astype(bf16)
        moving = copy(send_two.at[source - 1], recv_two.at[source - 1], peers[source - 1], 5 + source)
        moving.start()
        returned.append(moving)
    for moving in returned:
        moving.wait()
    for slot in range(3):
        own = own + recv_two[slot].astype(f32)
    mixed_grad[...] = cotangent + norm_back(mixed[...], gain_in[...], own)


def feed_forward(*arrays):
    steps = 8
    vmem = pl.BlockSpec(memory_space=pltpu.VMEM)
    outs = [
        jax.ShapeDtypeStruct((ROWS, D), bf16),
        jax.ShapeDtypeStruct((ROWS, D), f32),
        jax.ShapeDtypeStruct((steps, 32, TILE), f32),
        jax.ShapeDtypeStruct((steps, 32, TILE), f32),
        jax.ShapeDtypeStruct((steps, 16, TILE), f32),
        jax.ShapeDtypeStruct((32, D), f32),
        jax.ShapeDtypeStruct((16, D), f32),
    ]
    return pl.pallas_call(
        mlp_kernel,
        out_shape=outs,
        in_specs=[vmem] * len(arrays),
        out_specs=[vmem] * len(outs),
        scratch_shapes=[
            pltpu.VMEM((steps, SEQ, ROWS, TILE), f32),
            pltpu.VMEM((steps, SEQ, ROWS, TILE), f32),
            pltpu.VMEM((steps, SEQ, ROWS, TILE), bf16),
            pltpu.VMEM((SEQ, ROWS, 32), bf16),
            pltpu.VMEM((SEQ, ROWS, 16), bf16),
            pltpu.VMEM((SEQ, ROWS, D), bf16),
            pltpu.VMEM((ROWS, D), f32),
            pltpu.VMEM((ROWS, 16), f32),
            pltpu.VMEM((ROWS, 32), f32),
            pltpu.VMEM((3, ROWS, D), bf16),
            pltpu.VMEM((3, ROWS, D), bf16),
            pltpu.VMEM((3, ROWS, D), bf16),
            pltpu.VMEM((3, ROWS, D), bf16),
            pltpu.SemaphoreType.DMA((9,)),
            pltpu.SemaphoreType.DMA((9,)),
        ],
        compiler_params=pltpu.CompilerParams(
            collective_id=1, has_side_effects=True, vmem_limit_bytes=62 * MIB
        ),
        name="feed_forward",
    )(*arrays)


EARLY = 52
LATE = 10


class LineSum:
    def __init__(self, parts, landed, send_sem, recv_sem):
        self.me, self.peers = lax.axis_index("seq"), seq_peers()
        self.parts, self.landed, self.send, self.recv = parts, landed, send_sem, recv_sem

    def _copy(self, shift):
        return remote(
            self.parts.at[lax.rem(self.me + shift, SEQ)], self.landed.at[shift - 1],
            self.send.at[shift - 1], self.recv.at[shift - 1], self.peers[shift - 1],
        )

    def start(self):
        for shift in (2, 1, 3):
            self._copy(shift).start()

    def finish(self):
        for shift in (1, 3, 2):
            self._copy(shift).wait()


class PlaneExchange:
    def __init__(self, first, second, third, fourth, send_sem, recv_sem):
        self.x, self.y, self.z, self.core = place()
        self.first, self.second, self.third, self.fourth = first, second, third, fourth
        self.send, self.recv = send_sem, recv_sem

    def _copy(self, src, dst, slot, peer):
        return remote(src, dst, self.send.at[slot], self.recv.at[slot], peer)

    def _along_y(self, k):
        y = lax.rem(self.y + k, 4)
        return self._copy(self.first.at[y], self.second.at[k], k - 1, at(self.x, y, self.z, self.core))

    def _along_z(self, k):
        z = lax.rem(self.z + k, 4)
        return self._copy(self.second.at[:, z], self.third.at[k], 2 + k, at(self.x, self.y, z, self.core))

    def _across(self):
        return self._copy(self.third.at[:, :, 1 - self.core], self.fourth, 6, sibling())

    def start(self):
        for k in (2, 1, 3):
            self._along_y(k).start()
        self.second[0] = self.first[self.y]

    def middle(self):
        for k in (1, 3, 2):
            self._along_y(k).wait()
        for k in (2, 1, 3):
            self._along_z(k).start()
        self.third[0] = self.second[:, self.z]

    def late(self):
        for k in (1, 3, 2):
            self._along_z(k).wait()
        self._across().start()

    def finish(self):
        self._across().wait()

    def total(self, chosen, count, out):
        slots = self.first.shape[3]
        out[...] = jnp.zeros_like(out)

        def add(i, _):
            kz, ky = i // 4, lax.rem(i, 4)
            pair = (lax.rem(self.y + 4 - ky, 4) * 4 + lax.rem(self.z + 4 - kz, 4)) * 2
            for own in (True, False):
                source = pair + (self.core if own else 1 - self.core)
                marks = chosen(source)
                for slot in range(slots):
                    held = self.third[kz, ky, self.core, slot] if own else self.fourth[kz, ky, slot]
                    held = held.astype(f32)
                    for a in range(count):
                        out[slot, a] += marks[a : a + 1] * held
            return 0

        lax.fori_loop(0, 16, add, 0)


class LineGather:
    def __init__(self, buffer, send_sem, recv_sem):
        self.me, self.peers = lax.axis_index("seq"), seq_peers()
        self.buffer, self.send, self.recv = buffer, send_sem, recv_sem

    def _copy(self, shift):
        mine = self.buffer.at[self.me]
        return remote(mine, mine, self.send.at[shift - 1], self.recv.at[shift - 1], self.peers[shift - 1])

    def start(self):
        for shift in (2, 1, 3):
            self._copy(shift).start()

    def finish(self):
        for shift in (1, 3, 2):
            self._copy(shift).wait()


def attention_back_kernel(
    layer_input, mixed_grad, attn_proj, context, totals, queries, kv_all,
    segment_rows, segment_column, gain_first, gain_second,
    first_qkv, second_q, second_kv, first_o, second_o, qkv_latent, o_latent,
    got_qkv, kv_rows, got_o,
    grad_gate_out, grad_up_out, grad_down_in, grad_gu_in, grad_down_out,
    marks, marks_late,
    input_grad, all_early, all_late,
    attn_grad, head_grads, query_grads, centre, key_part, value_part, kv_send, kv_landed, kv_own,
    packed, early, early_landed, early_sum, e2, e3, e4, early_total, early_line,
    late, late_landed, late_sum, l2, l3, l4, late_total, late_line,
    line_s, line_r, kv_s, kv_r, plane_s, plane_r, spread_s, spread_r, out_s, out_r, loc,
):
    me, y, z, core = place()
    line = seq_peers()
    greet(line + plane_peers() + [sibling()])

    attn_grad[...] = norm_back(attn_proj[...], gain_second[...], mixed_grad[...]).astype(bf16)
    o_grad = dot_nt(attn_grad[...], second_o[...]).astype(bf16)

    def put(start, rows, buffer):
        for i in range(rows.shape[1] // 128):
            buffer[start + i] = rows[:, i * 128 : (i + 1) * 128].astype(bf16)

    for h in range(4):
        low = (dot_nt(attn_grad[...], got_o[h].reshape(256, D)) + dot(o_grad, first_o[h])).astype(bf16)
        head_grads[h] = low
        centre[h] = jnp.sum(low.astype(f32) * context[h], -1, keepdims=True)
        query_grads[h] = jnp.zeros((ROWS, 256), f32)
        put(189 + 2 * h, dot_tn(o_grad, context[h].astype(bf16)), early)
    put(197, dot_tn(o_latent[...], attn_grad[...]), early)

    for j in range(8):
        packed[0:16, j * TILE : (j + 1) * TILE] = grad_gate_out[j, 0:16].astype(bf16)
        packed[16:32, j * TILE : (j + 1) * TILE] = grad_up_out[j, 16:32].astype(bf16)
        packed[32:48, j * TILE : (j + 1) * TILE] = grad_down_in[j].astype(bf16)

    def unpad(j, _):
        start = jnp.minimum((j * 128 // 216) // 2 * 128, 2048 - 256)
        lane = start + lax.broadcasted_iota(jnp.int32, (256, 128), 0)
        within = lane & 63
        unit = (lane >> 6) * 216 + me * UNITS + within
        goal = j * 128 + lax.broadcasted_iota(jnp.int32, (256, 128), 1)
        chosen = jnp.where((unit == goal) & (within < UNITS), 1.0, 0.0).astype(bf16)
        moved = dot(packed[:, pl.ds(pl.multiple_of(start, 128), 256)], chosen)
        early[j] = moved[0:16].astype(bf16)
        early[54 + j] = moved[16:32].astype(bf16)
        early[108 + j] = moved[32:48].astype(bf16)
        return 0

    lax.fori_loop(0, 54, unpad, 0)
    put(162, grad_gu_in[0:16], early)
    put(171, grad_gu_in[16:32], early)
    put(180, grad_down_out[...], early)
    early[206] = jnp.zeros((16, 128), bf16)
    early[207] = jnp.zeros((16, 128), bf16)
    early_parts = early.reshape(SEQ, EARLY, 16, 128)
    e_line = LineSum(early_parts, early_landed, line_s.at[0], line_r.at[0])
    e_line.start()

    def attend_back(chunk):
        keys, held = kv_all[chunk, :, 0:256], kv_all[chunk, :, 256:512]
        allowed = allowed_pairs(segment_rows, segment_column, me, chunk)
        key_part[...] = jnp.zeros_like(key_part)
        value_part[...] = jnp.zeros_like(value_part)

        def head(h, _):
            bent = jnp.tanh(dot_nt(queries[h], keys) * (SCORE / softcap))
            weight = jnp.where(allowed, jnp.exp(softcap * bent), 0.0).astype(bf16).astype(f32)
            probs = weight / totals[h]
            prob_grad = dot_nt(head_grads[h], held)
            raw_grad = (probs * (prob_grad - centre[h]) * ((1.0 - bent * bent) * SCORE)).astype(bf16)
            query_grads[h] += dot(raw_grad, keys)
            key_part[...] += dot_tn(raw_grad, queries[h])
            value_part[...] += dot_tn(probs.astype(bf16), head_grads[h])
            return 0

        lax.fori_loop(0, 4, head, 0)

    def kv_copy(shift):
        peer = line[3 - shift]
        return remote(kv_send.at[shift - 1], kv_landed.at[shift - 1], kv_s.at[shift - 1], kv_r.at[shift - 1], peer)

    for shift in (3, 2, 1):
        def earlier(shift=shift):
            attend_back(me - shift)
            kv_send[shift - 1, :, 0:256] = key_part[...].astype(bf16)
            kv_send[shift - 1, :, 256:512] = value_part[...].astype(bf16)
            kv_copy(shift).start()

        pl.when(me >= shift)(earlier)

    e_line.finish()

    def add_early(i, _):
        own = early_parts[me, i].astype(f32)
        for s in range(3):
            own = own + early_landed[s, i].astype(f32)
        early_sum[i] = own.astype(bf16)
        return 0

    lax.fori_loop(0, EARLY, add_early, 0)
    for i in range(EARLY, 64):
        early_sum[i] = jnp.zeros((16, 128), bf16)
    e_plane = PlaneExchange(early_sum.reshape(4, 4, 2, 2, 16, 128), e2, e3, e4, plane_s.at[0], plane_r.at[0])
    e_plane.start()

    attend_back(me)
    kv_own[:, 0:256] = key_part[...]
    kv_own[:, 256:512] = value_part[...]
    e_plane.middle()
    for shift in (1, 2, 3):
        def landed(shift=shift):
            kv_copy(shift).wait_recv()
            kv_own[...] += kv_landed[shift - 1].astype(f32)

        pl.when(me + shift < SEQ)(landed)
    e_plane.late()

    key_value = kv_own[...].astype(bf16)
    values = layer_input[...].astype(f32)
    first_norm = normed(values, gain_first[...]).astype(bf16)
    thin = dot_nt(key_value, second_kv[...])
    total = dot(key_value, kv_rows[...])
    for h in range(4):
        low = query_grads[h].astype(bf16)
        total = total + dot(low, got_qkv[h, :, :, 0:32].reshape(256, D))
        thin = thin + dot_nt(low, second_q[h])
        put(27 + 2 * h, dot_tn(qkv_latent[...], low)[0:16], late)
    qkv_grad = thin.astype(bf16)
    total = total + dot(qkv_grad, first_qkv[...])
    e_plane.finish()
    e_plane.total(lambda s: marks[s], 8, early_total)
    early_line[me] = early_total[...].astype(bf16)
    e_spread = LineGather(early_line, spread_s.at[0], spread_r.at[0])
    e_spread.start()

    in_grad = dot_tn(qkv_grad, first_norm)
    for i in range(3):
        put(9 * i, in_grad[16 * i : 16 * i + 16], late)
    kv_out_grad = dot_tn(qkv_latent[...], key_value)
    put(35, kv_out_grad[16:32, 0:256], late)
    put(37, kv_out_grad[32:48, 256:512], late)
    late[39] = jnp.zeros((16, 128), bf16)
    late_parts = late.reshape(SEQ, LATE, 16, 128)
    l_line = LineSum(late_parts, late_landed, line_s.at[1], line_r.at[1])
    l_line.start()
    input_grad[...] = (mixed_grad[...] + norm_back(values, gain_first[...], total)).astype(bf16)

    e_spread.finish()
    own_early = pltpu.make_async_copy(early_line, all_early.at[y, z, core], loc.at[0])
    own_early.start()
    e_out = PlaneGather(early_line, all_early, out_s.at[0], out_r.at[0])
    e_out.start()

    l_line.finish()
    for i in range(LATE):
        own = late_parts[me, i].astype(f32)
        for s in range(3):
            own = own + late_landed[s, i].astype(f32)
        low = own.astype(bf16)
        for k in range(3 if i < LATE - 1 else 5):
            late_sum[3 * i + k, 0] = low
    l_plane = PlaneExchange(late_sum.reshape(4, 4, 2, 1, 16, 128), l2, l3, l4, plane_s.at[1], plane_r.at[1])
    l_plane.start()
    l_plane.middle()
    l_plane.late()
    l_plane.finish()
    group = lax.rem((y * 4 + z) * 2 + core, 3)
    l_plane.total(lambda s: marks_late[group, s], 3, late_total)
    late_line[me] = late_total[...].astype(bf16)
    l_spread = LineGather(late_line, spread_s.at[1], spread_r.at[1])
    l_spread.start()
    own_early.wait()
    e_out.middle()
    l_spread.finish()
    own_late = pltpu.make_async_copy(late_line, all_late.at[y, z, core], loc.at[1])
    own_late.start()
    l_out = PlaneGather(late_line, all_late, out_s.at[1], out_r.at[1])
    l_out.start()
    own_late.wait()
    l_out.middle()
    e_out.late()
    l_out.late()
    e_out.finish()
    l_out.finish()
    for shift in (1, 2, 3):
        pl.when(me >= shift)(lambda shift=shift: kv_copy(shift).wait_send())


def attention_back(*arrays):
    vmem = pl.BlockSpec(memory_space=pltpu.VMEM)
    hbm = pl.BlockSpec(memory_space=pl.ANY)
    shape = jax.ShapeDtypeStruct
    dma = pltpu.SemaphoreType.DMA

    def reduction(blocks, slots, count):
        return [
            pltpu.VMEM((SEQ * blocks, 16, 128), bf16),
            pltpu.VMEM((3, blocks, 16, 128), bf16),
            pltpu.VMEM((32 * slots, 16, 128) if slots > 1 else (32, 1, 16, 128), bf16),
            pltpu.VMEM((4, 4, 2, slots, 16, 128), bf16),
            pltpu.VMEM((4, 4, 2, slots, 16, 128), bf16),
            pltpu.VMEM((4, 4, slots, 16, 128), bf16),
            pltpu.VMEM((slots, count, 16, 128), f32),
            pltpu.VMEM((SEQ, slots, count, 16, 128), bf16),
        ]

    return pl.pallas_call(
        attention_back_kernel,
        out_shape=[
            shape((ROWS, D), bf16),
            shape((4, 4, 2, SEQ, 2, 8, 16, 128), bf16),
            shape((4, 4, 2, SEQ, 1, 3, 16, 128), bf16),
        ],
        in_specs=[vmem] * len(arrays),
        out_specs=[vmem, hbm, hbm],
        scratch_shapes=[
            pltpu.VMEM((ROWS, D), bf16),
            pltpu.VMEM((4, ROWS, 256), bf16),
            pltpu.VMEM((4, ROWS, 256), f32),
            pltpu.VMEM((4, ROWS, 1), f32),
            pltpu.VMEM((ROWS, 256), f32),
            pltpu.VMEM((ROWS, 256), f32),
            pltpu.VMEM((3, ROWS, 512), bf16),
            pltpu.VMEM((3, ROWS, 512), bf16),
            pltpu.VMEM((ROWS, 512), f32),
            pltpu.VMEM((48, 2048), bf16),
        ]
        + reduction(EARLY, 2, 8)
        + reduction(LATE, 1, 3)
        + [dma((2, 3))] * 2
        + [dma((3,))] * 2
        + [dma((2, 7))] * 2
        + [dma((2, 3))] * 2
        + [dma((2, 10))] * 2
        + [dma((2,))],
        compiler_params=pltpu.CompilerParams(
            collective_id=3, has_side_effects=True, vmem_limit_bytes=60 * MIB
        ),
        name="attention_back",
    )(*arrays)


def my_quarter(rows, axis):
    me = lax.axis_index("seq")
    part = lax.dynamic_slice_in_dim(rows, me * UNITS, UNITS, axis)
    widths = [(0, 0)] * rows.ndim
    widths[axis] = (0, BLOCK - UNITS)
    return jnp.pad(part, widths)


def body(
    layer_input, out_grad, segment_ids, adapter_ids,
    gain_attn_in, gain_attn_out, gain_mlp_in, gain_mlp_out,
    w_query, w_key, w_value, w_out, w_gate, w_up, w_down,
    qkv_adapt_in, q_adapt_out, kv_adapt_out, o_adapt_in, o_adapt_out,
    mlp_adapt_in, mlp_adapt_out, down_adapt_in, down_adapt_out,
):
    me = lax.axis_index("seq")
    shards = 32
    cotangent = out_grad[0]
    chosen = adapter_ids[0]
    ids = lax.all_gather(adapter_ids, "dp", axis=0, tiled=True)
    marks = (ids[:, None] == jnp.arange(9)[None, :]).astype(f32)
    marks_late = jnp.pad(marks.reshape(32, 3, 3).transpose(1, 0, 2), ((0, 0), (0, 0), (0, 5)))
    marks_late = jnp.broadcast_to(marks_late[..., None], (3, 32, 8, 128))
    marks = jnp.broadcast_to(marks[:, :8, None], (32, 8, 128))
    pick = lambda table: lax.dynamic_index_in_dim(table, chosen, 0, keepdims=False)
    qkv_in, q_out, kv_out = pick(qkv_adapt_in), pick(q_adapt_out), pick(kv_adapt_out)
    o_in, o_out = pick(o_adapt_in), pick(o_adapt_out)
    mlp_in, mlp_out = pick(mlp_adapt_in), pick(mlp_adapt_out)
    down_in, down_out = pick(down_adapt_in), pick(down_adapt_out)

    pack_qkv = jnp.concatenate([w_query.T, w_key.T, w_value.T], 0)
    pack_gu = jnp.concatenate([my_quarter(w_gate.T, 0), my_quarter(w_up.T, 0)], 0)
    pack_down = my_quarter(w_down, 0)
    steps = shards * BLOCK // TILE

    def hidden_slice(table):
        part = my_quarter(table.reshape(16, shards, 216), 2)
        return part.reshape(16, steps, TILE).transpose(1, 0, 2)

    zeros = jnp.zeros((steps, 16, TILE), bf16)
    second_gate = jnp.concatenate([hidden_slice(mlp_out[0]), zeros], 1)
    second_up = jnp.concatenate([zeros, hidden_slice(mlp_out[1])], 1)
    first_down = hidden_slice(down_in)

    segments = segment_ids[0]
    mine = lax.dynamic_slice_in_dim(segments, me * ROWS, ROWS)
    second_q = jnp.pad(q_out, ((0, 32), (0, 0))).reshape(48, 4, 256).transpose(1, 0, 2)
    blank = jnp.zeros((16, 256), bf16)
    second_kv = jnp.concatenate(
        [
            jnp.zeros((16, 512), bf16),
            jnp.concatenate([kv_out[0], blank], 1),
            jnp.concatenate([blank, kv_out[1]], 1),
        ],
        0,
    )
    (
        w_gu_all, w_down_all, tokens, qkv_all, kv_rows, o_all, kv_all,
        q, totals, context, attn_proj, mixed, qkv_latent, o_latent,
    ) = attention_forward(
        layer_input[0], pack_qkv, w_out, pack_gu, pack_down,
        segments.reshape(SEQ, 1, ROWS), mine[:, None],
        gain_attn_in[None], gain_attn_out[None], gain_mlp_in[None],
        qkv_in.reshape(48, D), second_q, second_kv,
        o_in.reshape(16, 4, 256).transpose(1, 0, 2), o_out,
    )
    layer_out, mixed_grad, g_gate, g_up, g_down_in, g_gu_in, g_down_out = feed_forward(
        tokens, w_gu_all, w_down_all, mlp_in.reshape(32, D),
        second_gate, second_up, first_down, down_out,
        mixed, cotangent, gain_mlp_in[None], gain_mlp_out[None],
    )

    input_grad, all_early, all_late = attention_back(
        layer_input[0], mixed_grad, attn_proj, context, totals, q, kv_all,
        segments.reshape(SEQ, 1, ROWS), mine[:, None], gain_attn_in[None], gain_attn_out[None],
        qkv_in.reshape(48, D), second_q, second_kv,
        o_in.reshape(16, 4, 256).transpose(1, 0, 2), o_out, qkv_latent, o_latent,
        qkv_all, kv_rows, o_all,
        g_gate, g_up, g_down_in, g_gu_in, g_down_out,
        marks, marks_late,
    )
    early = all_early.reshape(32, SEQ, 2, 8, 16, 128).transpose(1, 0, 2, 3, 4, 5)
    early = early.reshape(SEQ, 64, 8, 16, 128)[:, :EARLY].reshape(SEQ * EARLY, 8, 16, 128)
    late = all_late.reshape(32, SEQ, 3, 16, 128)[:30].reshape(LATE, 3, SEQ, 3, 16, 128)
    late = late.transpose(2, 0, 1, 3, 4, 5).reshape(SEQ * LATE, 9, 16, 128)[:, :8]

    def table(blocks, start, count):
        part = blocks[start : start + count].transpose(1, 2, 0, 3)
        return part.reshape(8, 16, count * 128).astype(f32)

    def tables(blocks, start, count, many):
        return jnp.stack([table(blocks, start + i * count, count) for i in range(many)], 1)

    return (
        layer_out[None],
        input_grad[None],
        tables(late, 0, 9, 3),
        table(late, 27, 8),
        tables(late, 35, 2, 2),
        table(early, 189, 8),
        table(early, 197, 9),
        tables(early, 162, 9, 2),
        tables(early, 0, 54, 2),
        table(early, 108, 54),
        table(early, 180, 9),
    )


def solution(mesh):
    tokens = P("dp", "seq", None)
    columns, rows = P(None, "dp"), P("dp", None)
    placed = (
        (tokens, tokens, P("dp", None), P("dp"))
        + (P(),) * 4
        + (columns, columns, columns, rows, columns, columns, rows)
        + (P(),) * 9
    )
    return jax.shard_map(
        body,
        mesh=mesh,
        in_specs=placed,
        out_specs=(tokens, tokens) + (P(),) * 9,
        check_vma=False,
    )
```

```python
import functools

import jax
import jax.numpy as jnp
from jax import lax
from jax.experimental import pallas as pl
from jax.experimental.pallas import tpu as pltpu
from jax.sharding import PartitionSpec as P

epsilon = 1e-06
softcap = 50.0
MESH = pl.DeviceIdType.MESH
bf16 = jnp.bfloat16
f32 = jnp.float32

D = 1152
SEQ = 4
ROWS = 256
UNITS = 54
BLOCK = 64
TILE = 256
MIB = 1 << 20


def dot(a, b):
    return lax.dot_general(a, b, (((1,), (0,)), ((), ())), preferred_element_type=f32)


def dot_nt(a, b):
    return lax.dot_general(a, b, (((1,), (1,)), ((), ())), preferred_element_type=f32)


def dot_tn(a, b):
    return lax.dot_general(a, b, (((0,), (0,)), ((), ())), preferred_element_type=f32)


def normed(values, gain_vector):
    return values * lax.rsqrt(jnp.mean(values * values, -1, keepdims=True) + epsilon) * gain_vector


def norm_back(values, gain_vector, cotangent):
    inverse = lax.rsqrt(jnp.mean(values * values, -1, keepdims=True) + epsilon)
    scaled = cotangent * gain_vector
    mean_part = jnp.mean(scaled * values, -1, keepdims=True)
    return inverse * (scaled - values * (inverse * inverse * mean_part))


def seq_peers():
    dp, me = lax.axis_index("dp"), lax.axis_index("seq")
    return [(dp, lax.rem(me + shift, SEQ)) for shift in (1, 2, 3)]


def greet(peers):
    barrier = pltpu.get_barrier_semaphore()
    for peer in peers:
        pl.semaphore_signal(barrier, inc=1, device_id=peer, device_id_type=MESH)
    pl.semaphore_wait(barrier, len(peers))


def staged_call(kernel, name, operands, kinds, results, scratch, collective_id=None):
    count, made = len(operands), len(results)
    held = [i for i in range(count) if kinds[i] == "v"]
    given = [i for i in range(made) if results[i][2] == "v"]

    def body(*refs):
        outer = list(refs[: count + made])
        inner = list(outer)
        rest = refs[count + made :]
        for n, i in enumerate(held):
            inner[i] = rest[n]
        for n, i in enumerate(given):
            inner[count + i] = rest[len(held) + n]
        sems, rest = rest[len(held) + len(given)], rest[len(held) + len(given) + 1 :]
        ins = {i: pltpu.make_async_copy(outer[i], inner[i], sems.at[n]) for n, i in enumerate(held)}
        outs = {
            i: pltpu.make_async_copy(inner[count + i], outer[count + i], sems.at[len(held) + n])
            for n, i in enumerate(given)
        }
        waiting, leaving = set(ins), []
        for moving in ins.values():
            moving.start()

        def arrive(*which):
            for i in which or sorted(waiting):
                if i in waiting:
                    waiting.discard(i)
                    ins[i].wait()

        def leave(*which):
            for i in which:
                outs[i].start()
                leaving.append(i)

        kernel(arrive, leave, *inner, *rest)
        leave(*[i for i in given if i not in leaving])
        for i in given:
            outs[i].wait()

    spaces = {"v": pl.ANY, "h": pl.ANY, "s": pltpu.SMEM}
    params = dict(vmem_limit_bytes=62 * MIB)
    if collective_id is not None:
        params.update(collective_id=collective_id, has_side_effects=True)
    return pl.pallas_call(
        body,
        out_shape=[jax.ShapeDtypeStruct(shape, dtype) for shape, dtype, _ in results],
        in_specs=[pl.BlockSpec(memory_space=spaces[k]) for k in kinds],
        out_specs=[pl.BlockSpec(memory_space=pl.ANY)] * made,
        scratch_shapes=[pltpu.VMEM(operands[i].shape, operands[i].dtype) for i in held]
        + [pltpu.VMEM(results[i][0], results[i][1]) for i in given]
        + [pltpu.SemaphoreType.DMA((len(held) + len(given),))]
        + scratch,
        compiler_params=pltpu.CompilerParams(**params),
        name=name,
    )(*operands)


def place():
    dp = lax.axis_index("dp")
    return lax.axis_index("seq"), dp // 8, lax.rem(dp // 2, 4), lax.rem(dp, 2)


def at(x, y, z, core):
    return ((lax.rem(y, 4) * 4 + lax.rem(z, 4)) * 2 + core, lax.rem(x, 4))


def plane_peers():
    x, y, z, core = place()
    return [at(x, y + k, z, core) for k in (1, 2, 3)] + [at(x, y, z + k, core) for k in (1, 2, 3)]


def sibling():
    x, y, z, core = place()
    return at(x, y, z, 1 - core)


def remote(src, dst, send_sem, recv_sem, peer):
    return pltpu.make_async_remote_copy(
        src_ref=src, dst_ref=dst, send_sem=send_sem, recv_sem=recv_sem,
        device_id=peer, device_id_type=MESH,
    )


class PlaneGather:
    def __init__(self, own, buffer, send_sem, recv_sem):
        self.x, self.y, self.z, self.core = place()
        self.own, self.buffer, self.send, self.recv = own, buffer, send_sem, recv_sem

    def _copy(self, src, dst, slot, peer):
        return remote(src, dst, self.send.at[slot], self.recv.at[slot], peer)

    def _first(self, k):
        x, y, z, core = self.x, self.y, self.z, self.core
        peer = at(x, y + k * (1 - core), z + k * core, core)
        return self._copy(self.own, self.buffer.at[y, z, core], k - 1, peer)

    def _line(self, core, back):
        if core == 0:
            return self.buffer.at[:, lax.rem(self.z + 4 - back, 4), 0]
        return self.buffer.at[lax.rem(self.y + 4 - back, 4), :, 1]

    def _second(self, core, k):
        line = self._line(core, 0)
        peer = at(self.x, self.y + k * core, self.z + k * (1 - core), core)
        return self._copy(line, line, 2 + k, peer)

    def _pass(self, core, half):
        back, k = ((1, 1), (3, 3))[half]
        line = self._line(core, back).at[2 * half : 2 * half + 2]
        peer = at(self.x, self.y + k * core, self.z + k * (1 - core), core)
        return self._copy(line, line, (4, 10)[half], peer)

    def _swap(self, core, back):
        line = self._line(core, back)
        return self._copy(line, line, 6 + back, at(self.x, self.y, self.z, 1 - core))

    def _both(self, act):
        for core in (0, 1):
            pl.when(self.core == core)(functools.partial(act, core))

    def start(self):
        for k in (2, 1, 3):
            self._first(k).start()

    def middle(self):
        for k in (1, 3, 2):
            self._first(k).wait()

        def act(core):
            for k in (1, 3):
                self._second(core, k).start()
            self._swap(core, 0).start()

        self._both(act)

    def late(self):
        def act(core):
            for half, k in ((0, 1), (1, 3)):
                self._second(core, k).wait()
                self._pass(core, half).start()
                self._swap(core, k).start()

        self._both(act)

    def last(self):
        def act(core):
            for half in (0, 1):
                self._pass(core, half).wait()
            self._swap(core, 2).start()

        self._both(act)

    def finish(self):
        def act(core):
            for back in (0, 1, 3, 2):
                self._swap(core, back).wait()

        self._both(act)


def allowed_pairs(segment_rows, segment_column, me, chunk):
    keys = lax.broadcasted_iota(jnp.int32, (ROWS, ROWS), 1) + chunk * ROWS
    queries = lax.broadcasted_iota(jnp.int32, (ROWS, ROWS), 0) + me * ROWS
    return (segment_column[...] == segment_rows[chunk]) & (keys <= queries)


SCORE = 1.0 / 16.0


def attention_kernel(
    arrive, leave,
    layer_input, pack_qkv, pack_o, pack_gu, pack_down, segment_rows, segment_column, gains,
    first_qkv, second_q, second_kv, first_o, second_o,
    all_gu, all_down, all_tokens, out_qkv, out_kv_rows, out_o, out_kv,
    queries, totals, context, attn_proj, mixed, qkv_latent, o_latent,
    got_qkv, got_o, kv_rows, first_norm, kv_all, second_norm,
    sem_s, sem_r, kv_s, kv_r, tok_s, tok_r, loc,
):
    me, y, z, core = place()
    line = seq_peers()
    greet(line + plane_peers() + [sibling()])
    gathers = [
        PlaneGather(own, got, sem_s.at[i], sem_r.at[i])
        for i, (own, got) in enumerate(
            (
                (pack_qkv, got_qkv), (pack_o, got_o), (pack_gu, all_gu), (pack_down, all_down),
            )
        )
    ]
    g_qkv, g_o, g_gu, g_down = gathers
    own_copies = [
        pltpu.make_async_copy(g.own, g.buffer.at[y, z, core], loc.at[i])
        for i, g in enumerate(gathers)
    ]
    arrive(1)
    g_qkv.start()
    own_copies[0].start()
    arrive()
    for moving in own_copies[1:]:
        moving.start()
    gain_first, gain_second, gain_third = gains[0:1], gains[1:2], gains[2:3]
    values = layer_input[...].astype(f32)
    first_norm[...] = normed(values, gain_first).astype(bf16)
    latent = dot_nt(first_norm[...], first_qkv[...]).astype(bf16)
    qkv_latent[...] = latent
    for moving in own_copies:
        moving.wait()
    g_qkv.middle()
    g_o.start()
    g_qkv.late()
    g_gu.start()
    g_qkv.last()
    g_o.middle()
    g_qkv.finish()

    def unmix(i, _):
        pairs = got_qkv[i, :, :, 32:48].astype(f32).reshape(8, 2, 8, D)
        kv_rows[pl.ds(i * 64, 64)] = pairs[:, 0].reshape(64, D).astype(bf16)
        kv_rows[pl.ds(256 + i * 64, 64)] = pairs[:, 1].reshape(64, D).astype(bf16)
        return 0

    lax.fori_loop(0, 4, unmix, 0)
    kv = dot_nt(first_norm[...], kv_rows[...]) + dot(latent, second_kv[...])
    kv_all[me] = kv.astype(bf16)

    def kv_copy(shift):
        return remote(kv_all.at[me], kv_all.at[me], kv_s.at[shift - 1], kv_r.at[shift - 1], line[shift - 1])

    for shift in (1, 2, 3):
        pl.when(me + shift < SEQ)(lambda shift=shift: kv_copy(shift).start())

    def query(h, _):
        rows = got_qkv[h, :, :, 0:32].reshape(256, D)
        queries[h] = (dot_nt(first_norm[...], rows) + dot(latent, second_q[h])).astype(bf16)
        context[h] = jnp.zeros((ROWS, 256), f32)
        totals[h] = jnp.zeros((ROWS, 1), f32)
        return 0

    lax.fori_loop(0, 4, query, 0)
    g_gu.middle()
    g_down.start()

    def attend(chunk):
        keys, held = kv_all[chunk, :, 0:256], kv_all[chunk, :, 256:512]
        allowed = allowed_pairs(segment_rows, segment_column, me, chunk)

        def head(h, _):
            bent = jnp.tanh(dot_nt(queries[h], keys) * (SCORE / softcap))
            weight = jnp.where(allowed, jnp.exp(softcap * bent), 0.0).astype(bf16)
            totals[h] += jnp.sum(weight.astype(f32), -1, keepdims=True)
            context[h] += dot(weight, held)
            return 0

        lax.fori_loop(0, 4, head, 0)

    attend(me)
    g_o.late()
    g_o.last()
    for shift in (1, 2, 3):
        def arrived(shift=shift):
            kv_copy(shift).wait_recv()
            attend(me - shift)

        pl.when(me >= shift)(arrived)

    g_o.finish()
    keep = [
        pltpu.make_async_copy(got_qkv, out_qkv, loc.at[0]),
        pltpu.make_async_copy(got_o, out_o, loc.at[1]),
        pltpu.make_async_copy(kv_rows, out_kv_rows, loc.at[2]),
    ]
    for moving in keep:
        moving.start()
    g_gu.late()
    g_down.middle()
    total = jnp.zeros((ROWS, D), f32)
    thin = jnp.zeros((ROWS, 16), f32)
    for h in range(4):
        context[h] = context[h] / totals[h]
        low = context[h].astype(bf16)
        total = total + dot(low, got_o[h].reshape(256, D))
        thin = thin + dot_nt(low, first_o[h])
    o_latent[...] = thin.astype(bf16)
    proj = total + dot(o_latent[...], second_o[...])
    attn_proj[...] = proj
    mid = values + normed(proj, gain_second)
    mixed[...] = mid
    second_norm[...] = normed(mid, gain_third).astype(bf16)
    ahead, _, behind = line

    def passed(chunk, rows, slot, peer):
        block = all_tokens.at[chunk, rows]
        return remote(block, block, tok_s.at[slot], tok_r.at[slot], peer)

    to_ahead = remote(second_norm, all_tokens.at[me], tok_s.at[0], tok_r.at[0], ahead)
    to_behind = remote(second_norm, all_tokens.at[me], tok_s.at[1], tok_r.at[1], behind)
    to_ahead.start()
    to_behind.start()
    mine = pltpu.make_async_copy(second_norm, all_tokens.at[me], loc.at[3])
    mine.start()
    leave(7, 8, 9, 10, 11, 12, 13)
    kept_kv = pltpu.make_async_copy(kv_all, out_kv, loc.at[5])
    kept_kv.start()
    g_gu.last()
    g_down.late()
    to_ahead.wait()
    on_ahead = passed(lax.rem(me + 3, SEQ), slice(0, 128), 2, ahead)
    on_ahead.start()
    to_behind.wait()
    on_behind = passed(lax.rem(me + 1, SEQ), slice(128, 256), 3, behind)
    on_behind.start()
    g_gu.finish()
    g_down.last()
    g_down.finish()
    for moving in keep + [mine, kept_kv]:
        moving.wait()
    on_ahead.wait()
    on_behind.wait()
    for shift in (1, 2, 3):
        pl.when(me + shift < SEQ)(lambda shift=shift: kv_copy(shift).wait_send())


def attention_forward(*arrays):
    dma = pltpu.SemaphoreType.DMA
    return staged_call(
        attention_kernel, "attention_forward", arrays, "v" * len(arrays),
        [
            ((4, 4, 2, 2 * BLOCK, D), bf16, "h"),
            ((4, 4, 2, BLOCK, D), bf16, "h"),
            ((SEQ, ROWS, D), bf16, "h"),
            ((4, 4, 2, 48, D), bf16, "h"),
            ((512, D), bf16, "h"),
            ((4, 4, 2, 32, D), bf16, "h"),
            ((SEQ, ROWS, 512), bf16, "h"),
            ((4, ROWS, 256), bf16, "v"),
            ((4, ROWS, 1), f32, "v"),
            ((4, ROWS, 256), f32, "v"),
            ((ROWS, D), f32, "v"),
            ((ROWS, D), f32, "v"),
            ((ROWS, 48), bf16, "v"),
            ((ROWS, 16), bf16, "v"),
        ],
        [
            pltpu.VMEM((4, 4, 2, 48, D), bf16),
            pltpu.VMEM((4, 4, 2, 32, D), bf16),
            pltpu.VMEM((512, D), bf16),
            pltpu.VMEM((ROWS, D), bf16),
            pltpu.VMEM((SEQ, ROWS, 512), bf16),
            pltpu.VMEM((ROWS, D), bf16),
            dma((4, 11)), dma((4, 11)), dma((3,)), dma((3,)), dma((4,)), dma((4,)), dma((6,)),
        ],
        collective_id=2,
    )


WIDE = D + 128
HIDDEN = 32 * BLOCK
HALF = ROWS // 2
ROOT = 0.7978845608028654
CUBE = ROOT * 0.044715
FF_BLOCKS = 48


def mlp_kernel(
    arrive, leave,
    tokens, all_gu, all_down, ext_gu, ext_down, first_gu, second_down, mixed, out_grad, gains,
    layer_out, mixed_grad, early,
    w_gu, w_down, inputs, down_grads, hidden, act_gate, act_up, total,
    down_latents, gu_grads, hold_next, hold_back, packed,
    far, landed_half, near, landed, far_two, landed_half_two, near_two, landed_two,
    rs_s, rs_r, ag_s, ag_r, loc,
):
    me = lax.axis_index("seq")
    ahead, across, behind = seq_peers()
    slots = [me] + [lax.rem(me + k, SEQ) for k in (1, 3, 2)]
    copies = [
        pltpu.make_async_copy(src, dst, loc.at[i])
        for i, (src, dst) in enumerate(
            [(tokens.at[chunk], inputs.at[slot, :, 0:D]) for slot, chunk in enumerate(slots)]
            + [
                (all_gu, w_gu.at[:, :, :, :, 0:D]),
                (ext_gu, w_gu.at[:, :, :, :, D:WIDE]),
                (all_down, w_down.at[:, :, :, :, 0:D]),
                (ext_down, w_down.at[:, :, :, :, D:WIDE]),
            ]
        )
    ]
    for moving in copies:
        moving.start()
    greet([ahead, behind])
    arrive()
    gain_in, gain_out = gains[2:3], gains[3:4]

    def gate_rows(j):
        return w_gu[j // 2, pl.ds(2 * lax.rem(j, 2), 2), :, 0:64].reshape(TILE, WIDE)

    def up_rows(j):
        return w_gu[j // 2, pl.ds(2 * lax.rem(j, 2), 2), :, 64:128].reshape(TILE, WIDE)

    def down_rows(j):
        return w_down[j // 2, pl.ds(2 * lax.rem(j, 2), 2)].reshape(TILE, WIDE)

    def lanes(j, size=TILE):
        return pl.ds(pl.multiple_of(j * size, size), size)

    def forward(slot, many, before_down=None):
        size = many * ROWS
        part = slice(slot, slot + many)
        inputs[part, :, D:WIDE] = (
            dot_nt(inputs[part, :, 0:D].reshape(size, D), first_gu[...]).astype(bf16).reshape(many, ROWS, 128)
        )

        def step(j, _):
            rows = inputs[part].reshape(size, WIDE)
            gate = dot_nt(rows, gate_rows(j))
            upward = dot_nt(rows, up_rows(j))
            square = gate * gate
            bent = jnp.tanh(gate * (ROOT + CUBE * square))
            half = 0.5 * bent + 0.5
            gelu = gate * half
            slope = half + gelu * ((1.0 - bent) * (ROOT + 3.0 * CUBE * square))
            shape = (many, ROWS, TILE)
            hidden[part, :, lanes(j)] = (gelu * upward).astype(bf16).reshape(shape)
            act_gate[part, :, lanes(j)] = gelu.astype(bf16).reshape(shape)
            act_up[part, :, lanes(j)] = (upward * slope).astype(bf16).reshape(shape)
            return 0

        lax.fori_loop(0, 8, step, 0, unroll=2)
        if before_down is not None:
            before_down()

        def close(n, _):
            rows = hidden[part].reshape(size, HIDDEN)
            total[0:size, lanes(n)] = dot(rows, w_down[:, :, :, :, lanes(n)].reshape(HIDDEN, TILE))
            return 0

        lax.fori_loop(0, 5, close, 0)
        down_latent = total[0:size, D:WIDE].astype(bf16)
        down_latents[slot * ROWS : slot * ROWS + size] = down_latent
        total[0:size, 0:D] += dot(down_latent, second_down[...])

    def backward(slot, many):
        size = many * ROWS
        part = slice(slot, slot + many)
        latent_grad = dot_nt(down_grads[part, :, 0:D].reshape(size, D), second_down[...])
        down_grads[part, :, D:WIDE] = latent_grad.astype(bf16).reshape(many, ROWS, 128)

        def step(j, _):
            shape = (many, ROWS, TILE)
            hidden_grad = dot_nt(down_grads[part].reshape(size, WIDE), down_rows(j)).reshape(shape)
            gate_grad = (hidden_grad * act_up[part, :, lanes(j)].astype(f32)).astype(bf16)
            up_grad = (hidden_grad * act_gate[part, :, lanes(j)].astype(f32)).astype(bf16)
            act_up[part, :, lanes(j)] = gate_grad
            act_gate[part, :, lanes(j)] = up_grad
            return 0

        lax.fori_loop(0, 8, step, 0, unroll=2)

        def close(n, _):
            total[0:size, lanes(n)] = dot(
                act_up[part].reshape(size, HIDDEN), w_gu[:, :, :, 0:64, lanes(n)].reshape(HIDDEN, TILE)
            ) + dot(
                act_gate[part].reshape(size, HIDDEN), w_gu[:, :, :, 64:128, lanes(n)].reshape(HIDDEN, TILE)
            )
            return 0

        lax.fori_loop(0, 5, close, 0)
        gu_grad = total[0:size, D:WIDE].astype(bf16)
        gu_grads[slot * ROWS : slot * ROWS + size] = gu_grad
        total[0:size, 0:D] += dot(gu_grad, first_gu[...])

    def factors():
        latent = inputs[:, :, D:WIDE].reshape(SEQ * ROWS, 128)[:, 0:32]
        latent_grad = down_grads[:, :, D:WIDE].reshape(SEQ * ROWS, 128)[:, 32:48]

        def piece(j, _):
            gate_part = dot_tn(latent, act_up[:, :, lanes(j)].reshape(SEQ * ROWS, TILE))
            up_part = dot_tn(latent, act_gate[:, :, lanes(j)].reshape(SEQ * ROWS, TILE))
            down_part = dot_tn(latent_grad, hidden[:, :, lanes(j)].reshape(SEQ * ROWS, TILE))
            packed[0:16, lanes(j)] = gate_part[0:16].astype(bf16)
            packed[16:32, lanes(j)] = up_part[16:32].astype(bf16)
            packed[32:48, lanes(j)] = down_part.astype(bf16)
            return 0

        lax.fori_loop(0, 8, piece, 0)

    low, high = slice(0, HALF), slice(HALF, ROWS)

    def scatter_far(buffer, into, base):
        buffer[...] = total[0:ROWS, 0:D].astype(bf16)
        moves = [
            remote(buffer.at[low], into.at[0], rs_s.at[base], rs_r.at[base], behind),
            remote(buffer.at[high], into.at[1], rs_s.at[base + 1], rs_r.at[base + 1], ahead),
        ]
        for moving in moves:
            moving.start()
        return moves

    def scatter_near(buffer, into, base):
        return [
            remote(buffer.at[0, low], into.at[0, low], rs_s.at[base], rs_r.at[base], ahead),
            remote(buffer.at[0, high], into.at[0, high], rs_s.at[base + 1], rs_r.at[base + 1], ahead),
            remote(buffer.at[1, high], into.at[1, high], rs_s.at[base + 2], rs_r.at[base + 2], behind),
            remote(buffer.at[1, low], into.at[1, low], rs_s.at[base + 3], rs_r.at[base + 3], behind),
        ]

    def keep_near(buffer, moves):
        buffer[0, low] = total[0:HALF, 0:D].astype(bf16)
        moves[0].start()
        buffer[1, high] = total[ROWS + HALF : 2 * ROWS, 0:D].astype(bf16)
        moves[2].start()
        hold_next[...] = total[HALF:ROWS, 0:D]
        hold_back[...] = total[ROWS : ROWS + HALF, 0:D]

    def merge(buffer, half, far_moves, moves):
        far_moves[1].wait()
        buffer[0, high] = (hold_next[...] + half[1].astype(f32)).astype(bf16)
        moves[1].start()
        far_moves[0].wait()
        buffer[1, low] = (hold_back[...] + half[0].astype(f32)).astype(bf16)
        moves[3].start()

    for moving in copies[:6]:
        moving.wait()

    def down_here():
        for moving in copies[6:]:
            moving.wait()

    forward(3, 1, down_here)
    far_moves = scatter_far(far, landed_half, 0)
    near_moves = scatter_near(near, landed, 2)
    forward(1, 2)
    keep_near(near, near_moves)
    merge(near, landed_half, far_moves, near_moves)
    forward(0, 1)
    for moving in near_moves:
        moving.wait()
    down_proj = total[0:ROWS, 0:D] + landed[0].astype(f32) + landed[1].astype(f32)
    layer_out[...] = (mixed[...] + normed(down_proj, gain_out)).astype(bf16)
    leave(0)
    down_grads[0, :, 0:D] = norm_back(down_proj, gain_out, out_grad[...].astype(f32)).astype(bf16)

    def passed(from_slot, to_slot, rows, index, peer):
        return remote(
            down_grads.at[from_slot, rows, 0:D], down_grads.at[to_slot, rows, 0:D],
            ag_s.at[index], ag_r.at[index], peer,
        )

    whole = slice(0, ROWS)
    to_ahead, to_behind = passed(0, 2, whole, 0, ahead), passed(0, 1, whole, 1, behind)
    to_ahead.start()
    to_behind.start()
    backward(0, 1)
    mixed_grad[...] = total[0:ROWS, 0:D]
    to_ahead.wait()
    on_ahead = passed(2, 3, low, 2, ahead)
    on_ahead.start()
    to_behind.wait()
    on_behind = passed(1, 3, high, 3, behind)
    on_behind.start()
    near_moves = scatter_near(near_two, landed_two, 8)
    backward(1, 2)
    keep_near(near_two, near_moves)
    on_ahead.wait()
    on_behind.wait()
    backward(3, 1)
    far_moves = scatter_far(far_two, landed_half_two, 6)
    factors()
    merge(near_two, landed_half_two, far_moves, near_moves)

    def unpad(j, _):
        start = jnp.minimum((j * 128 // 216) // 2 * 128, HIDDEN // 2 - 256)
        lane = start + lax.broadcasted_iota(jnp.int32, (256, 128), 0)
        within = lane & 63
        unit = (lane >> 6) * 216 + me * UNITS + within
        goal = j * 128 + lax.broadcasted_iota(jnp.int32, (256, 128), 1)
        chosen = jnp.where((unit == goal) & (within < UNITS), 1.0, 0.0).astype(bf16)
        for half in (0, 1):
            rows = packed[:, pl.ds(pl.multiple_of(start + half * HIDDEN // 2, 128), 256)]
            moved = dot(rows, chosen).astype(bf16)
            for i in range(3):
                early[54 * i + 27 * half + j] = moved[16 * i : 16 * i + 16]
        return 0

    lax.fori_loop(0, 27, unpad, 0)
    all_gu_grads = gu_grads[...]
    gu_part = dot_tn(all_gu_grads[:, 0:32], inputs[:, :, 0:D].reshape(SEQ * ROWS, D))
    down_part = dot_tn(down_latents[:, 32:48], down_grads[:, :, 0:D].reshape(SEQ * ROWS, D))

    def put(start, rows):
        for i in range(9):
            early[start + i] = rows[:, i * 128 : (i + 1) * 128].astype(bf16)

    put(162, gu_part[0:16])
    put(171, gu_part[16:32])
    put(180, down_part)
    for i in range(189, 192):
        early[i] = jnp.zeros((16, 128), bf16)
    for moving in near_moves:
        moving.wait()
    own = mixed_grad[...] + landed_two[0].astype(f32) + landed_two[1].astype(f32)
    mixed_grad[...] = out_grad[...].astype(f32) + norm_back(mixed[...], gain_in, own)


def feed_forward(*arrays):
    dma = pltpu.SemaphoreType.DMA
    exchange = [
        pltpu.VMEM((ROWS, D), bf16),
        pltpu.VMEM((2, HALF, D), bf16),
        pltpu.VMEM((2, ROWS, D), bf16),
        pltpu.VMEM((2, ROWS, D), bf16),
    ]
    return staged_call(
        mlp_kernel, "feed_forward", arrays, "hhhhh" + "v" * (len(arrays) - 5),
        [((ROWS, D), bf16, "v"), ((ROWS, D), f32, "v"), ((SEQ * FF_BLOCKS, 16, 128), bf16, "v")],
        [
            pltpu.VMEM((4, 4, 2, 2 * BLOCK, WIDE), bf16),
            pltpu.VMEM((4, 4, 2, BLOCK, WIDE), bf16),
            pltpu.VMEM((SEQ, ROWS, WIDE), bf16),
            pltpu.VMEM((SEQ, ROWS, WIDE), bf16),
            pltpu.VMEM((SEQ, ROWS, HIDDEN), bf16),
            pltpu.VMEM((SEQ, ROWS, HIDDEN), bf16),
            pltpu.VMEM((SEQ, ROWS, HIDDEN), bf16),
            pltpu.VMEM((2 * ROWS, WIDE), f32),
            pltpu.VMEM((SEQ * ROWS, 128), bf16),
            pltpu.VMEM((SEQ * ROWS, 128), bf16),
            pltpu.VMEM((HALF, D), f32),
            pltpu.VMEM((HALF, D), f32),
            pltpu.VMEM((48, HIDDEN), bf16),
        ]
        + exchange
        + exchange
        + [dma((12,)), dma((12,)), dma((4,)), dma((4,)), dma((8,))],
        collective_id=1,
    )


LATE = 14


class LineSum:
    def __init__(self, parts, landed, send_sem, recv_sem):
        self.me, self.peers = lax.axis_index("seq"), seq_peers()
        self.parts, self.landed, self.send, self.recv = parts, landed, send_sem, recv_sem

    def _copy(self, shift):
        return remote(
            self.parts.at[lax.rem(self.me + shift, SEQ)], self.landed.at[shift - 1],
            self.send.at[shift - 1], self.recv.at[shift - 1], self.peers[shift - 1],
        )

    def start(self):
        for shift in (2, 1, 3):
            self._copy(shift).start()

    def finish(self):
        for shift in (1, 3, 2):
            self._copy(shift).wait()


class PlaneExchange:
    def __init__(self, first, second, third, fourth, send_sem, recv_sem):
        self.x, self.y, self.z, self.core = place()
        self.first, self.second, self.third, self.fourth = first, second, third, fourth
        self.send, self.recv = send_sem, recv_sem

    def _copy(self, src, dst, slot, peer):
        return remote(src, dst, self.send.at[slot], self.recv.at[slot], peer)

    def _along_y(self, k):
        y = lax.rem(self.y + k, 4)
        return self._copy(self.first.at[y], self.second.at[k], k - 1, at(self.x, y, self.z, self.core))

    def _along_z(self, k):
        z = lax.rem(self.z + k, 4)
        return self._copy(self.second.at[:, z], self.third.at[k], 2 + k, at(self.x, self.y, z, self.core))

    def _across(self):
        return self._copy(self.third, self.fourth, 6, sibling())

    def start(self):
        for k in (2, 1, 3):
            self._along_y(k).start()
        self.second[0] = self.first[self.y]

    def middle(self):
        for k in (1, 3, 2):
            self._along_y(k).wait()
        for k in (2, 1, 3):
            self._along_z(k).start()
        self.third[0] = self.second[:, self.z]

    def late(self):
        for k in (1, 3, 2):
            self._along_z(k).wait()
        self._across().start()

    def finish(self):
        self._across().wait()

    def total(self, marks, out):
        slots = self.first.shape[2]
        out[...] = jnp.zeros_like(out)

        def add(i, _):
            kz, ky = i // 4, lax.rem(i, 4)
            for held, known in ((self.third, marks.third), (self.fourth, marks.fourth)):
                weights = known[kz, ky, 0, self.core]
                for slot in range(slots):
                    rows = held[kz, ky, slot].astype(f32)
                    for a in range(4):
                        out[slot, a] += weights[a : a + 1] * rows
            return 0

        lax.fori_loop(0, 16, add, 0)


class LineGather:
    def __init__(self, buffer, send_sem, recv_sem):
        self.me, self.peers = lax.axis_index("seq"), seq_peers()
        self.buffer, self.send, self.recv = buffer, send_sem, recv_sem

    def _copy(self, shift):
        mine = self.buffer.at[self.me]
        return remote(mine, mine, self.send.at[shift - 1], self.recv.at[shift - 1], self.peers[shift - 1])

    def start(self):
        for shift in (2, 1, 3):
            self._copy(shift).start()

    def finish(self):
        for shift in (1, 3, 2):
            self._copy(shift).wait()


def attention_back_kernel(
    arrive, leave,
    layer_input, mixed_grad, attn_proj, context, totals, queries, kv_all,
    segment_rows, segment_column, gains,
    first_qkv, second_q, second_kv, first_o, second_o, qkv_latent, o_latent,
    got_qkv, kv_rows, got_o,
    early, own_marks,
    input_grad, all_early, all_late,
    m1, m2, m3, m4, attn_grad, head_grads, query_grads, centre, key_part, value_part, kv_send, kv_landed, kv_own,
    early_landed, early_sum, e2, e3, e4, early_total, early_line,
    late, late_landed, late_sum, l2, l3, l4, late_total, late_line,
    line_s, line_r, kv_s, kv_r, plane_s, plane_r, spread_s, spread_r, out_s, out_r, loc,
):
    me, y, z, core = place()
    line = seq_peers()
    greet(line + plane_peers() + [sibling()])
    arrive(20)
    early_parts = early.reshape(SEQ, FF_BLOCKS, 16, 128)
    e_line = LineSum(early_parts, early_landed, line_s.at[0], line_r.at[0])
    e_line.start()
    arrive(21)
    for i in range(4):
        for k in range(4):
            m1[i, k, 0] = own_marks[...]
    m_plane = PlaneExchange(m1, m2, m3, m4, plane_s.at[2], plane_r.at[2])
    m_plane.start()
    arrive(*range(17))
    gain_first, gain_second = gains[0:1], gains[1:2]

    attn_grad[...] = norm_back(attn_proj[...], gain_second, mixed_grad[...]).astype(bf16)
    o_grad = dot_nt(attn_grad[...], second_o[...]).astype(bf16)

    def put(start, rows, buffer):
        for i in range(rows.shape[1] // 128):
            buffer[start + i] = rows[:, i * 128 : (i + 1) * 128].astype(bf16)

    m_plane.middle()
    arrive(19)
    for h in range(4):
        low = (dot_nt(attn_grad[...], got_o[h].reshape(256, D)) + dot(o_grad, first_o[h])).astype(bf16)
        head_grads[h] = low
        centre[h] = jnp.sum(low.astype(f32) * context[h], -1, keepdims=True)
        query_grads[h] = jnp.zeros((ROWS, 256), f32)
        put(39 + 2 * h, dot_tn(o_grad, context[h].astype(bf16)), late)
    put(47, dot_tn(o_latent[...], attn_grad[...]), late)

    def attend_back(chunk):
        keys, held = kv_all[chunk, :, 0:256], kv_all[chunk, :, 256:512]
        allowed = allowed_pairs(segment_rows, segment_column, me, chunk)
        key_part[...] = jnp.zeros_like(key_part)
        value_part[...] = jnp.zeros_like(value_part)

        def head(h, _):
            bent = jnp.tanh(dot_nt(queries[h], keys) * (SCORE / softcap))
            weight = jnp.where(allowed, jnp.exp(softcap * bent), 0.0).astype(bf16).astype(f32)
            probs = weight / totals[h]
            prob_grad = dot_nt(head_grads[h], held)
            raw_grad = (probs * (prob_grad - centre[h]) * ((1.0 - bent * bent) * SCORE)).astype(bf16)
            query_grads[h] += dot(raw_grad, keys)
            key_part[...] += dot_tn(raw_grad, queries[h])
            value_part[...] += dot_tn(probs.astype(bf16), head_grads[h])
            return 0

        lax.fori_loop(0, 4, head, 0)

    def kv_copy(shift):
        peer = line[3 - shift]
        return remote(kv_send.at[shift - 1], kv_landed.at[shift - 1], kv_s.at[shift - 1], kv_r.at[shift - 1], peer)

    for shift in (3, 2, 1):
        def earlier(shift=shift):
            attend_back(me - shift)
            kv_send[shift - 1, :, 0:256] = key_part[...].astype(bf16)
            kv_send[shift - 1, :, 256:512] = value_part[...].astype(bf16)
            kv_copy(shift).start()

        pl.when(me >= shift)(earlier)

    attend_back(me)
    kv_own[:, 0:256] = key_part[...]
    kv_own[:, 256:512] = value_part[...]
    m_plane.late()

    e_line.finish()

    def add_early(i, _):
        for k in range(3):
            own = early_parts[me, 3 * i + k].astype(f32)
            for s in range(3):
                own = own + early_landed[s, 3 * i + k].astype(f32)
            low = own.astype(bf16)
            early_sum[i // 4, lax.rem(i, 4), k] = low
        return 0

    lax.fori_loop(0, 16, add_early, 0)
    e_plane = PlaneExchange(early_sum, e2, e3, e4, plane_s.at[0], plane_r.at[0])
    e_plane.start()

    m_plane.finish()
    e_plane.middle()
    e_plane.late()
    e_plane.finish()
    e_plane.total(m_plane, early_total)
    early_line[me] = early_total[...].astype(bf16)
    e_spread = LineGather(early_line, spread_s.at[0], spread_r.at[0])
    e_spread.start()
    for shift in (1, 2, 3):
        def landed(shift=shift):
            kv_copy(shift).wait_recv()
            kv_own[...] += kv_landed[shift - 1].astype(f32)

        pl.when(me + shift < SEQ)(landed)

    arrive(17, 18)
    key_value = kv_own[...].astype(bf16)
    values = layer_input[...].astype(f32)
    first_norm = normed(values, gain_first).astype(bf16)
    thin = dot_nt(key_value, second_kv[...])
    total = dot(key_value, kv_rows[...])
    for h in range(4):
        low = query_grads[h].astype(bf16)
        total = total + dot(low, got_qkv[h, :, :, 0:32].reshape(256, D))
        thin = thin + dot_nt(low, second_q[h])
        put(27 + 2 * h, dot_tn(qkv_latent[...], low)[0:16], late)
    qkv_grad = thin.astype(bf16)
    total = total + dot(qkv_grad, first_qkv[...])
    e_spread.finish()
    own_early = pltpu.make_async_copy(early_line, all_early.at[y, z, core], loc.at[0])
    own_early.start()
    e_out = PlaneGather(early_line, all_early, out_s.at[0], out_r.at[0])
    e_out.start()

    in_grad = dot_tn(qkv_grad, first_norm)
    for i in range(3):
        put(9 * i, in_grad[16 * i : 16 * i + 16], late)
    kv_out_grad = dot_tn(qkv_latent[...], key_value)
    put(35, kv_out_grad[16:32, 0:256], late)
    put(37, kv_out_grad[32:48, 256:512], late)
    late_parts = late.reshape(SEQ, LATE, 16, 128)
    l_line = LineSum(late_parts, late_landed, line_s.at[1], line_r.at[1])
    l_line.start()
    input_grad[...] = (mixed_grad[...] + norm_back(values, gain_first, total)).astype(bf16)

    leave(0)

    l_line.finish()
    for i in range(16):
        low = jnp.zeros((16, 128), bf16)
        if i < LATE:
            own = late_parts[me, i].astype(f32)
            for s in range(3):
                own = own + late_landed[s, i].astype(f32)
            low = own.astype(bf16)
        late_sum[i // 4, i % 4, 0] = low
    l_plane = PlaneExchange(late_sum, l2, l3, l4, plane_s.at[1], plane_r.at[1])
    l_plane.start()
    own_early.wait()
    e_out.middle()
    l_plane.middle()
    l_plane.late()
    l_plane.finish()
    l_plane.total(m_plane, late_total)
    late_line[me] = late_total[...].astype(bf16)
    l_spread = LineGather(late_line, spread_s.at[1], spread_r.at[1])
    l_spread.start()
    l_spread.finish()
    own_late = pltpu.make_async_copy(late_line, all_late.at[y, z, core], loc.at[1])
    own_late.start()
    l_out = PlaneGather(late_line, all_late, out_s.at[1], out_r.at[1])
    l_out.start()
    e_out.late()
    own_late.wait()
    l_out.middle()
    l_out.late()
    e_out.last()
    l_out.last()
    e_out.finish()
    l_out.finish()
    for shift in (1, 2, 3):
        pl.when(me >= shift)(lambda shift=shift: kv_copy(shift).wait_send())


def attention_back(*arrays):
    dma = pltpu.SemaphoreType.DMA
    marks = pltpu.VMEM((4, 4, 1, 2, 8, 128), f32)

    def reduction(blocks, slots):
        whole = pltpu.VMEM((4, 4, slots, 16, 128), bf16)
        return [
            pltpu.VMEM((3, blocks, 16, 128), bf16), whole, whole, whole, whole,
            pltpu.VMEM((slots, 4, 16, 128), f32),
            pltpu.VMEM((SEQ, slots, 4, 16, 128), bf16),
        ]

    return staged_call(
        attention_back_kernel, "attention_back", arrays, "v" * len(arrays),
        [
            ((ROWS, D), bf16, "v"),
            ((4, 4, 2, SEQ, 3, 4, 16, 128), bf16, "h"),
            ((4, 4, 2, SEQ, 1, 4, 16, 128), bf16, "h"),
        ],
        [
            marks, marks, marks, marks,
            pltpu.VMEM((ROWS, D), bf16),
            pltpu.VMEM((4, ROWS, 256), bf16),
            pltpu.VMEM((4, ROWS, 256), f32),
            pltpu.VMEM((4, ROWS, 1), f32),
            pltpu.VMEM((ROWS, 256), f32),
            pltpu.VMEM((ROWS, 256), f32),
            pltpu.VMEM((3, ROWS, 512), bf16),
            pltpu.VMEM((3, ROWS, 512), bf16),
            pltpu.VMEM((ROWS, 512), f32),
        ]
        + reduction(FF_BLOCKS, 3)
        + [pltpu.VMEM((SEQ * LATE, 16, 128), bf16)]
        + reduction(LATE, 1)
        + [dma((2, 3))] * 2
        + [dma((3,))] * 2
        + [dma((3, 7))] * 2
        + [dma((2, 3))] * 2
        + [dma((2, 11))] * 2
        + [dma((2,))],
        collective_id=3,
    )


def tables_kernel(
    early, late, qkv_in, q_out, kv_out, o_in, o_out, mlp_in, mlp_out, down_in, down_out
):
    def copy(source, start, count, out):
        for i in range(count):
            x, place = divmod(start + i, FF_BLOCKS if source is early else LATE)
            owner, slot = divmod(place, 3 if source is early else 1)
            out[:, i * 128 : (i + 1) * 128] = source[owner // 4, owner % 4, 0, x, slot, 0].astype(f32)

    for i in range(2):
        copy(early, 54 * i, 54, mlp_out.at[0, i])
        copy(early, 162 + 9 * i, 9, mlp_in.at[0, i])
        copy(late, 35 + 2 * i, 2, kv_out.at[0, i])
    copy(early, 108, 54, down_in.at[0])
    copy(early, 180, 9, down_out.at[0])
    for i in range(3):
        copy(late, 9 * i, 9, qkv_in.at[0, i])
    copy(late, 27, 8, q_out.at[0])
    copy(late, 39, 8, o_in.at[0])
    copy(late, 47, 9, o_out.at[0])


def put_tables(early, late):
    shapes = (
        (3, 16, D), (16, 1024), (2, 16, 256), (16, 1024), (16, D),
        (2, 16, D), (2, 16, 6912), (16, 6912), (16, D),
    )

    def one(shape):
        rest = len(shape)
        return pl.BlockSpec((1,) + shape, lambda a, rest=rest: (a,) + (0,) * rest)

    def blocks(slots):
        return pl.BlockSpec(
            (4, 4, 1, SEQ, slots, 1, 16, 128), lambda a: (0, 0, a // 4, 0, 0, a % 4, 0, 0)
        )

    return pl.pallas_call(
        tables_kernel,
        grid=(8,),
        out_shape=[jax.ShapeDtypeStruct((8,) + shape, f32) for shape in shapes],
        in_specs=[blocks(3), blocks(1)],
        out_specs=[one(shape) for shape in shapes],
        compiler_params=pltpu.CompilerParams(vmem_limit_bytes=62 * MIB),
        name="tables",
    )(early, late)


def prepare_kernel(
    arrive, leave, ids, place_x, segments, w_query, w_key, w_value, w_gate, w_up, w_down,
    qkv_adapt_in, q_adapt_out, kv_adapt_out, o_adapt_in, o_adapt_out,
    mlp_adapt_in, mlp_adapt_out, down_adapt_in, down_adapt_out,
    pack_qkv, pack_gu, pack_down, own_marks, segment_rows, segment_column,
    first_qkv, second_q, second_kv, first_o, second_o, first_gu, second_down, ext_gu, ext_down,
    table, q_held, kv_held, o_held, in_held, out_held, sem,
):
    chosen, me = ids[0], place_x[0]
    mlp_out, down_in = mlp_adapt_out.at[chosen], down_adapt_in.at[chosen]
    moves = [
        (mlp_out.at[0], table.at[0:16]),
        (mlp_out.at[1], table.at[16:32]),
        (down_in, table.at[32:48]),
        (q_adapt_out.at[chosen], q_held),
        (kv_adapt_out.at[chosen], kv_held),
        (o_adapt_in.at[chosen], o_held),
        (o_adapt_out.at[chosen], second_o),
        (mlp_adapt_in.at[chosen], in_held),
        (down_adapt_out.at[chosen], out_held),
        (qkv_adapt_in.at[chosen], first_qkv),
    ]
    moves = [pltpu.make_async_copy(src, dst, sem.at[i]) for i, (src, dst) in enumerate(moves)]
    for moving in moves:
        moving.start()
    iota = lambda shape, axis: lax.broadcasted_iota(jnp.int32, shape, axis)
    ones = lambda where: jnp.where(where, 1.0, 0.0).astype(bf16)

    def placed(count, first):
        return ones(iota((48, count), 0) == iota((48, count), 1) + first)

    table[48:128] = jnp.zeros((80, 6912), bf16)
    arrive()
    rows = dot(placed(32, 0), w_query[...]) + dot(placed(8, 32), w_key[...])
    pack_qkv[...] = (rows + dot(placed(8, 40), w_value[...])).astype(bf16)
    row, unit = iota((BLOCK, 216), 0), iota((BLOCK, 216), 1)
    quarter = ones((unit == me * UNITS + row) & (row < UNITS))
    pack_gu[0:64] = dot(quarter, w_gate[...]).astype(bf16)
    pack_gu[64:128] = dot(quarter, w_up[...]).astype(bf16)
    pack_down[...] = dot(quarter, w_down[...]).astype(bf16)

    leave(0, 1, 2)
    adapter = iota((8, 128), 0)
    for half in (0, 1):
        own_marks[half] = jnp.where((adapter + 4 * half == chosen) & (adapter < 4), 1.0, 0.0)
    for i in range(SEQ):
        segment_rows[i] = segments[:, i * ROWS : (i + 1) * ROWS]
    square = iota((ROWS, ROWS), 0) == iota((ROWS, ROWS), 1)
    segment_column[...] = jnp.sum(jnp.where(square, segment_rows[me], 0), -1, keepdims=True)

    for moving in moves:
        moving.wait()
    second_q[...] = jnp.zeros_like(second_q)
    for h in range(4):
        second_q[h, 0:16] = q_held[:, h * 256 : (h + 1) * 256]
        first_o[h] = o_held[:, h * 256 : (h + 1) * 256]
    second_kv[...] = jnp.zeros_like(second_kv)
    second_kv[16:32, 0:256] = kv_held[0]
    second_kv[32:48, 256:512] = kv_held[1]
    first_gu[0:16] = in_held[0]
    first_gu[16:32] = in_held[1]
    first_gu[32:128] = jnp.zeros((96, D), bf16)
    second_down[0:32] = jnp.zeros((32, D), bf16)
    second_down[32:48] = out_held[...]
    second_down[48:128] = jnp.zeros((80, D), bf16)

    def spread(p, _):
        first = 432 * p + me * UNITS
        start = jnp.minimum(first // 128 * 128, 6912 - 512)
        row = iota((128, 512), 0)
        within = row & 63
        unit = first + (row >> 6) * 216 + within
        picked = ones((unit == start + iota((128, 512), 1)) & (within < UNITS))
        held = dot_nt(picked, table[:, pl.ds(pl.multiple_of(start, 128), 512)])
        lane = iota((128, 128), 1)
        gate = jnp.where(lane < 16, held, 0.0).astype(bf16)
        upward = jnp.where((lane >= 16) & (lane < 32), held, 0.0).astype(bf16)
        down = jnp.where(lane >= 32, held, 0.0).astype(bf16)
        for i in (0, 1):
            half = slice(64 * i, 64 * i + 64)
            ext_gu[2 * p + i, 0:64] = gate[half]
            ext_gu[2 * p + i, 64:128] = upward[half]
            ext_down[2 * p + i] = down[half]
        return 0

    lax.fori_loop(0, 16, spread, 0)


def prepare(*arrays):
    shapes = [
        ((48, D), bf16), ((128, D), bf16), ((64, D), bf16), ((2, 8, 128), f32),
        ((SEQ, 1, ROWS), jnp.int32), ((ROWS, 1), jnp.int32),
        ((3, 16, D), bf16), ((4, 48, 256), bf16), ((48, 512), bf16), ((4, 16, 256), bf16), ((16, D), bf16),
        ((128, D), bf16), ((128, D), bf16), ((32, 2 * BLOCK, 128), bf16), ((32, BLOCK, 128), bf16),
    ]
    return staged_call(
        prepare_kernel, "prepare", arrays, "ss" + "v" * 7 + "h" * 9,
        [shape + ("v",) for shape in shapes],
        [
            pltpu.VMEM((128, 6912), bf16),
            pltpu.VMEM((16, 1024), bf16),
            pltpu.VMEM((2, 16, 256), bf16),
            pltpu.VMEM((16, 1024), bf16),
            pltpu.VMEM((2, 16, D), bf16),
            pltpu.VMEM((16, D), bf16),
            pltpu.SemaphoreType.DMA((10,)),
        ],
    )


def body(
    layer_input, out_grad, segment_ids, adapter_ids,
    gain_attn_in, gain_attn_out, gain_mlp_in, gain_mlp_out,
    w_query, w_key, w_value, w_out, w_gate, w_up, w_down,
    qkv_adapt_in, q_adapt_out, kv_adapt_out, o_adapt_in, o_adapt_out,
    mlp_adapt_in, mlp_adapt_out, down_adapt_in, down_adapt_out,
):
    me = lax.axis_index("seq").astype(jnp.int32)
    (
        pack_qkv, pack_gu, pack_down, own_marks, segment_rows, segment_column,
        first_qkv, second_q, second_kv, first_o, second_o, first_gu, second_down, ext_gu, ext_down,
    ) = prepare(
        adapter_ids, me.reshape(1), segment_ids, w_query.T, w_key.T, w_value.T, w_gate.T, w_up.T, w_down,
        qkv_adapt_in, q_adapt_out, kv_adapt_out, o_adapt_in, o_adapt_out,
        mlp_adapt_in, mlp_adapt_out, down_adapt_in, down_adapt_out,
    )
    first_qkv = first_qkv.reshape(48, D)
    gains = jnp.stack([gain_attn_in, gain_attn_out, gain_mlp_in, gain_mlp_out])
    (
        w_gu_all, w_down_all, tokens, qkv_all, kv_rows, o_all, kv_all,
        q, totals, context, attn_proj, mixed, qkv_latent, o_latent,
    ) = attention_forward(
        layer_input[0], pack_qkv, w_out, pack_gu, pack_down, segment_rows, segment_column, gains,
        first_qkv, second_q, second_kv, first_o, second_o,
    )
    layer_out, mixed_grad, early = feed_forward(
        tokens, w_gu_all, w_down_all,
        ext_gu.reshape(4, 4, 2, 2 * BLOCK, 128), ext_down.reshape(4, 4, 2, BLOCK, 128),
        first_gu, second_down, mixed, out_grad[0], gains,
    )
    input_grad, all_early, all_late = attention_back(
        layer_input[0], mixed_grad, attn_proj, context, totals, q, kv_all,
        segment_rows, segment_column, gains,
        first_qkv, second_q, second_kv, first_o, second_o, qkv_latent, o_latent,
        qkv_all, kv_rows, o_all, early, own_marks,
    )
    return (layer_out[None], input_grad[None]) + tuple(put_tables(all_early, all_late))


def solution(mesh):
    tokens = P("dp", "seq", None)
    columns, rows = P(None, "dp"), P("dp", None)
    placed = (
        (tokens, tokens, P("dp", None), P("dp"))
        + (P(),) * 4
        + (columns, columns, columns, rows, columns, columns, rows)
        + (P(),) * 9
    )
    return jax.shard_map(
        body,
        mesh=mesh,
        in_specs=placed,
        out_specs=(tokens, tokens) + (P(),) * 9,
        check_vma=False,
    )
```

```python
import functools

import jax
import jax.numpy as jnp
from jax import lax
from jax.experimental import pallas as pl
from jax.experimental.pallas import tpu as pltpu
from jax.sharding import PartitionSpec as P

epsilon = 1e-06
softcap = 50.0
MESH = pl.DeviceIdType.MESH
bf16 = jnp.bfloat16
f32 = jnp.float32

D = 1152
SEQ = 4
ROWS = 256
UNITS = 54
BLOCK = 64
TILE = 256
MIB = 1 << 20


def dot(a, b):
    return lax.dot_general(a, b, (((1,), (0,)), ((), ())), preferred_element_type=f32)


def dot_nt(a, b):
    return lax.dot_general(a, b, (((1,), (1,)), ((), ())), preferred_element_type=f32)


def dot_tn(a, b):
    return lax.dot_general(a, b, (((0,), (0,)), ((), ())), preferred_element_type=f32)


def normed(values, gain_vector):
    return values * lax.rsqrt(jnp.mean(values * values, -1, keepdims=True) + epsilon) * gain_vector


def norm_back(values, gain_vector, cotangent):
    inverse = lax.rsqrt(jnp.mean(values * values, -1, keepdims=True) + epsilon)
    scaled = cotangent * gain_vector
    mean_part = jnp.mean(scaled * values, -1, keepdims=True)
    return inverse * (scaled - values * (inverse * inverse * mean_part))


def seq_peers():
    dp, me = lax.axis_index("dp"), lax.axis_index("seq")
    return [(dp, lax.rem(me + shift, SEQ)) for shift in (1, 2, 3)]


def greet(peers):
    barrier = pltpu.get_barrier_semaphore()
    for peer in peers:
        pl.semaphore_signal(barrier, inc=1, device_id=peer, device_id_type=MESH)
    pl.semaphore_wait(barrier, len(peers))


def staged_call(kernel, name, operands, kinds, results, scratch, collective_id=None):
    count, made = len(operands), len(results)
    held = [i for i in range(count) if kinds[i] == "v"]
    given = [i for i in range(made) if results[i][2] == "v"]

    def body(*refs):
        outer = list(refs[: count + made])
        inner = list(outer)
        rest = refs[count + made :]
        for n, i in enumerate(held):
            inner[i] = rest[n]
        for n, i in enumerate(given):
            inner[count + i] = rest[len(held) + n]
        sems, rest = rest[len(held) + len(given)], rest[len(held) + len(given) + 1 :]
        ins = {i: pltpu.make_async_copy(outer[i], inner[i], sems.at[n]) for n, i in enumerate(held)}
        outs = {
            i: pltpu.make_async_copy(inner[count + i], outer[count + i], sems.at[len(held) + n])
            for n, i in enumerate(given)
        }
        waiting, leaving = set(ins), []
        for moving in ins.values():
            moving.start()

        def arrive(*which):
            for i in which or sorted(waiting):
                if i in waiting:
                    waiting.discard(i)
                    ins[i].wait()

        def leave(*which):
            for i in which:
                outs[i].start()
                leaving.append(i)

        kernel(arrive, leave, *inner, *rest)
        leave(*[i for i in given if i not in leaving])
        for i in given:
            outs[i].wait()

    spaces = {"v": pl.ANY, "h": pl.ANY, "s": pltpu.SMEM}
    params = dict(vmem_limit_bytes=63 * MIB)
    if collective_id is not None:
        params.update(collective_id=collective_id, has_side_effects=True)
    return pl.pallas_call(
        body,
        out_shape=[jax.ShapeDtypeStruct(shape, dtype) for shape, dtype, _ in results],
        in_specs=[pl.BlockSpec(memory_space=spaces[k]) for k in kinds],
        out_specs=[pl.BlockSpec(memory_space=pl.ANY)] * made,
        scratch_shapes=[pltpu.VMEM(operands[i].shape, operands[i].dtype) for i in held]
        + [pltpu.VMEM(results[i][0], results[i][1]) for i in given]
        + [pltpu.SemaphoreType.DMA((len(held) + len(given),))]
        + scratch,
        compiler_params=pltpu.CompilerParams(**params),
        name=name,
    )(*operands)


def place():
    dp = lax.axis_index("dp")
    return lax.axis_index("seq"), dp // 8, lax.rem(dp // 2, 4), lax.rem(dp, 2)


def at(x, y, z, core):
    return ((lax.rem(y, 4) * 4 + lax.rem(z, 4)) * 2 + core, lax.rem(x, 4))


def plane_peers():
    x, y, z, core = place()
    return [at(x, y + k, z, core) for k in (1, 2, 3)] + [at(x, y, z + k, core) for k in (1, 2, 3)]


def sibling():
    x, y, z, core = place()
    return at(x, y, z, 1 - core)


def remote(src, dst, send_sem, recv_sem, peer):
    return pltpu.make_async_remote_copy(
        src_ref=src, dst_ref=dst, send_sem=send_sem, recv_sem=recv_sem,
        device_id=peer, device_id_type=MESH,
    )


class PlaneGather:
    def __init__(self, own, buffer, send_sem, recv_sem):
        self.x, self.y, self.z, self.core = place()
        self.own, self.buffer, self.send, self.recv = own, buffer, send_sem, recv_sem

    def _copy(self, src, dst, slot, peer):
        return remote(src, dst, self.send.at[slot], self.recv.at[slot], peer)

    def _first(self, k):
        x, y, z, core = self.x, self.y, self.z, self.core
        peer = at(x, y + k * (1 - core), z + k * core, core)
        return self._copy(self.own, self.buffer.at[y, z, core], k - 1, peer)

    def _line(self, core, back):
        if core == 0:
            return self.buffer.at[:, lax.rem(self.z + 4 - back, 4), 0]
        return self.buffer.at[lax.rem(self.y + 4 - back, 4), :, 1]

    def _second(self, core, k):
        line = self._line(core, 0)
        peer = at(self.x, self.y + k * core, self.z + k * (1 - core), core)
        return self._copy(line, line, 2 + k, peer)

    def _pass(self, core, half):
        back, k = ((1, 1), (3, 3))[half]
        line = self._line(core, back).at[2 * half : 2 * half + 2]
        peer = at(self.x, self.y + k * core, self.z + k * (1 - core), core)
        return self._copy(line, line, (4, 10)[half], peer)

    def _swap(self, core, back):
        line = self._line(core, back)
        return self._copy(line, line, 6 + back, at(self.x, self.y, self.z, 1 - core))

    def _both(self, act):
        for core in (0, 1):
            pl.when(self.core == core)(functools.partial(act, core))

    def start(self):
        for k in (2, 1, 3):
            self._first(k).start()

    def middle(self):
        for k in (1, 3, 2):
            self._first(k).wait()

        def act(core):
            for k in (1, 3):
                self._second(core, k).start()
            self._swap(core, 0).start()

        self._both(act)

    def late(self):
        def act(core):
            for half, k in ((0, 1), (1, 3)):
                self._second(core, k).wait()
                self._pass(core, half).start()
                self._swap(core, k).start()

        self._both(act)

    def last(self):
        def act(core):
            for half in (0, 1):
                self._pass(core, half).wait()
            self._swap(core, 2).start()

        self._both(act)

    def finish(self):
        def act(core):
            for back in (0, 1, 3, 2):
                self._swap(core, back).wait()

        self._both(act)


class LineSum:
    def __init__(self, parts, landed, send_sem, recv_sem):
        self.me, self.peers = lax.axis_index("seq"), seq_peers()
        self.parts, self.landed, self.send, self.recv = parts, landed, send_sem, recv_sem

    def _copy(self, shift):
        return remote(
            self.parts.at[lax.rem(self.me + shift, SEQ)], self.landed.at[shift - 1],
            self.send.at[shift - 1], self.recv.at[shift - 1], self.peers[shift - 1],
        )

    def start(self):
        for shift in (2, 1, 3):
            self._copy(shift).start()

    def finish(self):
        for shift in (1, 3, 2):
            self._copy(shift).wait()


class PlaneExchange:
    def __init__(self, first, second, third, fourth, send_sem, recv_sem):
        self.x, self.y, self.z, self.core = place()
        self.first, self.second, self.third, self.fourth = first, second, third, fourth
        self.send, self.recv = send_sem, recv_sem

    def _copy(self, src, dst, slot, peer):
        return remote(src, dst, self.send.at[slot], self.recv.at[slot], peer)

    def _along_y(self, k):
        y = lax.rem(self.y + k, 4)
        return self._copy(self.first.at[y], self.second.at[k], k - 1, at(self.x, y, self.z, self.core))

    def _along_z(self, k):
        z = lax.rem(self.z + k, 4)
        return self._copy(self.second.at[:, z], self.third.at[k], 2 + k, at(self.x, self.y, z, self.core))

    def _across(self):
        return self._copy(self.third, self.fourth, 6, sibling())

    def start(self):
        for k in (2, 1, 3):
            self._along_y(k).start()
        self.second[0] = self.first[self.y]

    def middle(self):
        for k in (1, 3, 2):
            self._along_y(k).wait()
        for k in (2, 1, 3):
            self._along_z(k).start()
        self.third[0] = self.second[:, self.z]

    def late(self):
        for k in (1, 3, 2):
            self._along_z(k).wait()
        self._across().start()

    def finish(self):
        self._across().wait()

    def total(self, marks, out):
        slots = self.first.shape[2]
        out[...] = jnp.zeros_like(out)

        def add(i, _):
            kz, ky = i // 4, lax.rem(i, 4)
            for held, known in ((self.third, marks.third), (self.fourth, marks.fourth)):
                weights = known[kz, ky, 0, self.core]
                for slot in range(slots):
                    rows = held[kz, ky, slot].astype(f32)
                    for a in range(4):
                        out[slot, a] += weights[a : a + 1] * rows
            return 0

        lax.fori_loop(0, 16, add, 0)


class LineGather:
    def __init__(self, buffer, send_sem, recv_sem):
        self.me, self.peers = lax.axis_index("seq"), seq_peers()
        self.buffer, self.send, self.recv = buffer, send_sem, recv_sem

    def _copy(self, shift):
        mine = self.buffer.at[self.me]
        return remote(mine, mine, self.send.at[shift - 1], self.recv.at[shift - 1], self.peers[shift - 1])

    def start(self):
        for shift in (2, 1, 3):
            self._copy(shift).start()

    def finish(self):
        for shift in (1, 3, 2):
            self._copy(shift).wait()


WIDE = D + 128
HIDDEN = 32 * BLOCK
HALF = ROWS // 2
ROOT = 0.7978845608028654
CUBE = ROOT * 0.044715
FF_BLOCKS = 48
LATE = 14
SCORE = 1.0 / 16.0


def allowed_pairs(segment_rows, segment_column, me, chunk):
    keys = lax.broadcasted_iota(jnp.int32, (ROWS, ROWS), 1) + chunk * ROWS
    queries = lax.broadcasted_iota(jnp.int32, (ROWS, ROWS), 0) + me * ROWS
    return (segment_column[...] == segment_rows[chunk]) & (keys <= queries)


def layer_kernel(
    arrive, leave,
    layer_input, pack_qkv, pack_o, pack_gu, pack_down, segment_rows, segment_column, gains,
    first_qkv, second_q, second_kv, first_o, second_o,
    ext_gu, ext_down, first_gu, second_down, out_grad, own_marks,
    layer_out, input_grad, all_early, all_late,
    queries, totals, context, attn_proj, qkv_latent, o_latent, mixed_grad, early_sum,
    got_qkv, got_o, first_norm, kv_all, mixed,
    w_gu, w_down, inputs, down_grads, hidden, act_gate, act_up, total,
    down_latents, gu_grads, packed, early, early_landed,
    far, landed_half, near, landed,
    m1, m2, m3, m4, e2, e3, e4, early_total, early_line,
    late, late_landed, late_sum, l2, l3, l4, late_total, late_line,
    sem_s, sem_r, kv_s, kv_r, tok_s, tok_r, rs_s, rs_r, ag_s, ag_r, line_s, line_r, loc,
    back_s, back_r, plane_s, plane_r, spread_s, spread_r, out_s, out_r,
):
    me, y, z, core = place()
    line = seq_peers()
    ahead, _, behind = line
    greet(line + plane_peers() + [sibling()])

    all_gu, all_down = w_gu.at[:, :, :, :, 0:D], w_down.at[:, :, :, :, 0:D]
    gathers = [
        PlaneGather(own, got, sem_s.at[i], sem_r.at[i])
        for i, (own, got) in enumerate(
            ((pack_qkv, got_qkv), (pack_o, got_o), (pack_gu, all_gu), (pack_down, all_down))
        )
    ]
    g_qkv, g_o, g_gu, g_down = gathers
    own_copies = [
        pltpu.make_async_copy(g.own, g.buffer.at[y, z, core], loc.at[i]) for i, g in enumerate(gathers)
    ]
    ext_copies = [
        pltpu.make_async_copy(ext_gu, w_gu.at[:, :, :, :, D:WIDE], loc.at[4]),
        pltpu.make_async_copy(ext_down, w_down.at[:, :, :, :, D:WIDE], loc.at[5]),
    ]
    arrive(1)
    g_qkv.start()
    own_copies[0].start()
    arrive()
    for moving in own_copies[1:] + ext_copies:
        moving.start()
    gain_first, gain_second, gain_third, gain_fourth = [gains[i : i + 1] for i in range(4)]
    first_norm[...] = normed(layer_input[...].astype(f32), gain_first).astype(bf16)
    latent = dot_nt(first_norm[...], first_qkv[...]).astype(bf16)
    qkv_latent[...] = latent
    for moving in own_copies:
        moving.wait()
    g_qkv.middle()
    g_o.start()
    g_qkv.late()
    g_gu.start()
    g_down.start()
    g_qkv.last()
    g_o.middle()
    g_qkv.finish()

    def unmix(i, _):
        pairs = got_qkv[i, :, :, 32:48].astype(f32).reshape(8, 2, 8, D)
        got_qkv[i, 0:2, :, 32:48] = pairs[:, 0].reshape(2, 2, 16, D).astype(bf16)
        got_qkv[i, 2:4, :, 32:48] = pairs[:, 1].reshape(2, 2, 16, D).astype(bf16)
        return 0

    lax.fori_loop(0, 4, unmix, 0)
    key_rows = lambda: got_qkv[:, 0:2, :, 32:48].reshape(256, D)
    value_rows = lambda: got_qkv[:, 2:4, :, 32:48].reshape(256, D)
    kv_low = dot(latent, second_kv[...])
    kv_all[me, :, 0:256] = (dot_nt(first_norm[...], key_rows()) + kv_low[:, 0:256]).astype(bf16)
    kv_all[me, :, 256:512] = (dot_nt(first_norm[...], value_rows()) + kv_low[:, 256:512]).astype(bf16)

    def kv_copy(shift):
        return remote(kv_all.at[me], kv_all.at[me], kv_s.at[shift - 1], kv_r.at[shift - 1], line[shift - 1])

    for shift in (1, 2, 3):
        pl.when(me + shift < SEQ)(lambda shift=shift: kv_copy(shift).start())

    def query(h, _):
        rows = got_qkv[h, :, :, 0:32].reshape(256, D)
        queries[h] = (dot_nt(first_norm[...], rows) + dot(latent, second_q[h])).astype(bf16)
        context[h] = jnp.zeros((ROWS, 256), f32)
        return 0

    lax.fori_loop(0, 4, query, 0)
    totals[...] = jnp.zeros_like(totals)
    head_lane = lax.broadcasted_iota(jnp.int32, (ROWS, 128), 1)

    def total_of(h):
        return jnp.sum(jnp.where(head_lane == h, totals[...], 0.0), -1, keepdims=True)

    g_gu.middle()
    g_down.middle()

    def attend(chunk):
        keys, held = kv_all[chunk, :, 0:256], kv_all[chunk, :, 256:512]
        allowed = allowed_pairs(segment_rows, segment_column, me, chunk)

        def head(h, _):
            bent = jnp.tanh(dot_nt(queries[h], keys) * (SCORE / softcap))
            weight = jnp.where(allowed, jnp.exp(softcap * bent), 0.0).astype(bf16)
            totals[...] += jnp.where(head_lane == h, jnp.sum(weight.astype(f32), -1, keepdims=True), 0.0)
            context[h] += dot(weight, held)
            return 0

        lax.fori_loop(0, 4, head, 0)

    attend(me)
    g_o.late()
    g_o.last()
    for shift in (1, 2, 3):
        def arrived(shift=shift):
            kv_copy(shift).wait_recv()
            attend(me - shift)

        pl.when(me >= shift)(arrived)

    g_o.finish()
    proj = jnp.zeros((ROWS, D), f32)
    thin = jnp.zeros((ROWS, 16), f32)
    for h in range(4):
        context[h] = context[h] / total_of(h)
        low = context[h].astype(bf16)
        proj = proj + dot(low, got_o[h].reshape(256, D))
        thin = thin + dot_nt(low, first_o[h])
    o_latent[...] = thin.astype(bf16)
    proj = proj + dot(o_latent[...], second_o[...])
    attn_proj[...] = proj
    mid = layer_input[...].astype(f32) + normed(proj, gain_second)
    mixed[...] = mid
    inputs[0, :, 0:D] = normed(mid, gain_third).astype(bf16)

    low, high = slice(0, HALF), slice(HALF, ROWS)

    def passing(buffer, send, recv):
        def move(from_slot, to_slot, rows, index, peer):
            src, dst = buffer.at[from_slot, rows, 0:D], buffer.at[to_slot, rows, 0:D]
            return remote(src, dst, send.at[index], recv.at[index], peer)

        return [
            move(0, 2, low, 0, ahead), move(0, 1, high, 1, behind),
            move(0, 2, high, 2, ahead), move(0, 1, low, 3, behind),
            move(2, 3, low, 4, ahead), move(1, 3, high, 5, behind),
        ]

    token_moves = passing(inputs, tok_s, tok_r)
    for i in range(4):
        token_moves[i].start()
    g_gu.late()
    for i in range(4):
        for k in range(4):
            m1[i, k, 0] = own_marks[...]
    m_plane = PlaneExchange(m1, m2, m3, m4, plane_s.at[2], plane_r.at[2])
    g_down.late()
    g_gu.last()
    for moving in ext_copies:
        moving.wait()
    g_gu.finish()

    def gate_rows(j):
        return w_gu[j // 2, pl.ds(2 * lax.rem(j, 2), 2), :, 0:64].reshape(TILE, WIDE)

    def up_rows(j):
        return w_gu[j // 2, pl.ds(2 * lax.rem(j, 2), 2), :, 64:128].reshape(TILE, WIDE)

    def down_rows(j):
        return w_down[j // 2, pl.ds(2 * lax.rem(j, 2), 2)].reshape(TILE, WIDE)

    def lanes(j, size=TILE):
        return pl.ds(pl.multiple_of(j * size, size), size)

    def forward_open(slot, many):
        size = many * ROWS
        part = slice(slot, slot + many)
        inputs[part, :, D:WIDE] = (
            dot_nt(inputs[part, :, 0:D].reshape(size, D), first_gu[...]).astype(bf16).reshape(many, ROWS, 128)
        )

        def step(j, _):
            rows = inputs[part].reshape(size, WIDE)
            gate = dot_nt(rows, gate_rows(j))
            upward = dot_nt(rows, up_rows(j))
            square = gate * gate
            bent = jnp.tanh(gate * (ROOT + CUBE * square))
            half = 0.5 * bent + 0.5
            gelu = gate * half
            slope = half + gelu * ((1.0 - bent) * (ROOT + 3.0 * CUBE * square))
            shape = (many, ROWS, TILE)
            hidden[part, :, lanes(j)] = (gelu * upward).astype(bf16).reshape(shape)
            act_gate[part, :, lanes(j)] = gelu.astype(bf16).reshape(shape)
            act_up[part, :, lanes(j)] = (upward * slope).astype(bf16).reshape(shape)
            return 0

        lax.fori_loop(0, 8, step, 0, unroll=2)

    def forward_close(slot, many):
        size = many * ROWS
        part = slice(slot, slot + many)

        def close(n, _):
            rows = hidden[part].reshape(size, HIDDEN)
            total[0:size, lanes(n)] = dot(rows, w_down[:, :, :, :, lanes(n)].reshape(HIDDEN, TILE))
            return 0

        lax.fori_loop(0, 5, close, 0)
        down_latent = total[0:size, D:WIDE].astype(bf16)
        down_latents[slot * ROWS : slot * ROWS + size] = down_latent
        total[0:size, 0:D] += dot(down_latent, second_down[...])

    def backward_open(slot, many):
        size = many * ROWS
        part = slice(slot, slot + many)
        latent_grad = dot_nt(down_grads[part, :, 0:D].reshape(size, D), second_down[...])
        down_grads[part, :, D:WIDE] = latent_grad.astype(bf16).reshape(many, ROWS, 128)

        def step(j, _):
            shape = (many, ROWS, TILE)
            hidden_grad = dot_nt(down_grads[part].reshape(size, WIDE), down_rows(j)).reshape(shape)
            gate_grad = (hidden_grad * act_up[part, :, lanes(j)].astype(f32)).astype(bf16)
            up_grad = (hidden_grad * act_gate[part, :, lanes(j)].astype(f32)).astype(bf16)
            act_up[part, :, lanes(j)] = gate_grad
            act_gate[part, :, lanes(j)] = up_grad
            return 0

        lax.fori_loop(0, 8, step, 0, unroll=2)

    def backward_close(slot, many):
        size = many * ROWS
        part = slice(slot, slot + many)

        def close(n, _):
            total[0:size, lanes(n)] = dot(
                act_up[part].reshape(size, HIDDEN), w_gu[:, :, :, 0:64, lanes(n)].reshape(HIDDEN, TILE)
            ) + dot(
                act_gate[part].reshape(size, HIDDEN), w_gu[:, :, :, 64:128, lanes(n)].reshape(HIDDEN, TILE)
            )
            return 0

        lax.fori_loop(0, 5, close, 0)
        gu_grad = total[0:size, D:WIDE].astype(bf16)
        gu_grads[slot * ROWS : slot * ROWS + size] = gu_grad
        total[0:size, 0:D] += dot(gu_grad, first_gu[...])

    def factors():
        latent = inputs[:, :, D:WIDE].reshape(SEQ * ROWS, 128)[:, 0:32]
        latent_grad = down_grads[:, :, D:WIDE].reshape(SEQ * ROWS, 128)[:, 32:48]

        def piece(j, _):
            gate_part = dot_tn(latent, act_up[:, :, lanes(j)].reshape(SEQ * ROWS, TILE))
            up_part = dot_tn(latent, act_gate[:, :, lanes(j)].reshape(SEQ * ROWS, TILE))
            down_part = dot_tn(latent_grad, hidden[:, :, lanes(j)].reshape(SEQ * ROWS, TILE))
            packed[0:16, lanes(j)] = gate_part[0:16].astype(bf16)
            packed[16:32, lanes(j)] = up_part[16:32].astype(bf16)
            packed[32:48, lanes(j)] = down_part.astype(bf16)
            return 0

        lax.fori_loop(0, 8, piece, 0, unroll=2)

    def scatter(base, finish, others, own=None):
        finish(3, 1)
        far[...] = total[0:ROWS, 0:D].astype(bf16)
        far_moves = [
            remote(far.at[low], landed_half.at[0], rs_s.at[base + 4], rs_r.at[base + 4], behind),
            remote(far.at[high], landed_half.at[1], rs_s.at[base + 5], rs_r.at[base + 5], ahead),
        ]
        for moving in far_moves:
            moving.start()
        finish(1, 2)
        near_moves = [
            remote(near.at[0, low], landed.at[0, low], rs_s.at[base], rs_r.at[base], ahead),
            remote(near.at[0, high], landed.at[0, high], rs_s.at[base + 1], rs_r.at[base + 1], ahead),
            remote(near.at[1, high], landed.at[1, high], rs_s.at[base + 2], rs_r.at[base + 2], behind),
            remote(near.at[1, low], landed.at[1, low], rs_s.at[base + 3], rs_r.at[base + 3], behind),
        ]
        near[0, low] = total[0:HALF, 0:D].astype(bf16)
        near_moves[0].start()
        near[1, high] = total[ROWS + HALF : 2 * ROWS, 0:D].astype(bf16)
        near_moves[2].start()
        near[0, high] = total[HALF:ROWS, 0:D].astype(bf16)
        near[1, low] = total[ROWS : ROWS + HALF, 0:D].astype(bf16)
        if own is not None:
            own()
        far_moves[1].wait()
        near[0, high] = (near[0, high].astype(f32) + landed_half[1].astype(f32)).astype(bf16)
        near_moves[1].start()
        far_moves[0].wait()
        near[1, low] = (near[1, low].astype(f32) + landed_half[0].astype(f32)).astype(bf16)
        near_moves[3].start()
        others()
        for moving in near_moves:
            moving.wait()

    def forward_own():
        forward_close(0, 1)
        mixed_grad[...] = total[0:ROWS, 0:D]

    m_plane.start()
    forward_open(0, 1)
    token_moves[0].wait()
    token_moves[4].start()
    token_moves[1].wait()
    token_moves[5].start()
    token_moves[2].wait()
    token_moves[3].wait()
    forward_open(1, 2)
    g_down.last()
    token_moves[4].wait()
    token_moves[5].wait()
    forward_open(3, 1)
    g_down.finish()
    scatter(0, forward_close, forward_own)
    m_plane.middle()
    down_proj = mixed_grad[...] + landed[0].astype(f32) + landed[1].astype(f32)
    layer_out[...] = (mixed[...] + normed(down_proj, gain_fourth)).astype(bf16)
    leave(0)
    down_grads[0, :, 0:D] = norm_back(down_proj, gain_fourth, out_grad[...].astype(f32)).astype(bf16)
    grad_moves = passing(down_grads, ag_s, ag_r)
    for i in range(4):
        grad_moves[i].start()

    early_parts = early.reshape(SEQ, FF_BLOCKS, 16, 128)
    e_line = LineSum(early_parts, early_landed, line_s.at[0], line_r.at[0])

    def unpad(j, _):
        start = jnp.minimum((j * 128 // 216) // 2 * 128, HIDDEN // 2 - 256)
        lane = start + lax.broadcasted_iota(jnp.int32, (256, 128), 0)
        within = lane & 63
        unit = (lane >> 6) * 216 + me * UNITS + within
        goal = j * 128 + lax.broadcasted_iota(jnp.int32, (256, 128), 1)
        chosen = jnp.where((unit == goal) & (within < UNITS), 1.0, 0.0).astype(bf16)
        for half in (0, 1):
            rows = packed[:, pl.ds(pl.multiple_of(start + half * HIDDEN // 2, 128), 256)]
            moved = dot(rows, chosen).astype(bf16)
            for i in range(3):
                early[54 * i + 27 * half + j] = moved[16 * i : 16 * i + 16]
        return 0

    def put(start, rows, buffer):
        for i in range(rows.shape[1] // 128):
            buffer[start + i] = rows[:, i * 128 : (i + 1) * 128].astype(bf16)

    def spread_factors():
        lax.fori_loop(0, 27, unpad, 0, unroll=3)
        all_gu_grads = gu_grads[...]
        gu_part = dot_tn(all_gu_grads[:, 0:32], inputs[:, :, 0:D].reshape(SEQ * ROWS, D))
        put(162, gu_part[0:16], early)
        put(171, gu_part[16:32], early)
        put(180, dot_tn(down_latents[:, 32:48], down_grads[:, :, 0:D].reshape(SEQ * ROWS, D)), early)
        for i in range(189, 192):
            early[i] = jnp.zeros((16, 128), bf16)
        e_line.start()

    backward_open(0, 1)
    backward_close(0, 1)
    mixed_grad[...] = total[0:ROWS, 0:D]
    m_plane.late()
    grad_moves[0].wait()
    grad_moves[4].start()
    grad_moves[1].wait()
    grad_moves[5].start()
    grad_moves[2].wait()
    grad_moves[3].wait()
    backward_open(1, 2)
    grad_moves[4].wait()
    grad_moves[5].wait()
    backward_open(3, 1)

    def all_factors():
        factors()
        spread_factors()

    scatter(6, backward_close, all_factors)
    m_plane.finish()
    own_sum = mixed_grad[...] + landed[0].astype(f32) + landed[1].astype(f32)
    mixed_grad[...] = out_grad[...].astype(f32) + norm_back(mixed[...], gain_third, own_sum)

    head_grads = [down_grads.at[3, :, 256 * h : 256 * h + 256] for h in range(4)]
    key_part, value_part = total.at[0:ROWS, 512:768], total.at[0:ROWS, 768:1024]
    kv_own = total.at[ROWS : 2 * ROWS, 512:1024]

    def query_part(h):
        row, lane = h // 2, lax.rem(h, 2)
        return total.at[pl.ds(pl.multiple_of(row * ROWS, ROWS), ROWS), pl.ds(pl.multiple_of(lane * 256, 256), 256)]

    def head_grad(h):
        return down_grads[3, :, pl.ds(pl.multiple_of(h * 256, 256), 256)]

    far[...] = norm_back(attn_proj[...], gain_second, mixed_grad[...]).astype(bf16)
    o_grad = dot_nt(far[...], second_o[...]).astype(bf16)

    for h in range(4):
        low = (dot_nt(far[...], got_o[h].reshape(256, D)) + dot(o_grad, first_o[h])).astype(bf16)
        head_grads[h][...] = low
        query_part(h)[...] = jnp.zeros((ROWS, 256), f32)

    def attend_back(chunk):
        keys, held = kv_all[chunk, :, 0:256], kv_all[chunk, :, 256:512]
        allowed = allowed_pairs(segment_rows, segment_column, me, chunk)
        key_part[...] = jnp.zeros_like(key_part)
        value_part[...] = jnp.zeros_like(value_part)

        def head(h, _):
            bent = jnp.tanh(dot_nt(queries[h], keys) * (SCORE / softcap))
            weight = jnp.where(allowed, jnp.exp(softcap * bent), 0.0).astype(bf16).astype(f32)
            probs = weight / total_of(h)
            grads = head_grad(h)
            centre = jnp.sum(grads.astype(f32) * context[h], -1, keepdims=True)
            prob_grad = dot_nt(grads, held)
            raw_grad = (probs * (prob_grad - centre) * ((1.0 - bent * bent) * SCORE)).astype(bf16)
            query_part(h)[...] += dot(raw_grad, keys)
            key_part[...] += dot_tn(raw_grad, queries[h])
            value_part[...] += dot_tn(probs.astype(bf16), grads)
            return 0

        lax.fori_loop(0, 4, head, 0)

    def back_copy(shift):
        peer = line[3 - shift]
        return remote(w_down.at[shift - 1, 2:4, :, :, 0:512], w_down.at[shift - 1, 0:2, :, :, 0:512], back_s.at[shift - 1], back_r.at[shift - 1], peer)

    for shift in (3, 2, 1):
        def earlier(shift=shift):
            attend_back(me - shift)
            w_down[shift - 1, 2:4, :, :, 0:256] = key_part[...].astype(bf16).reshape(2, 2, BLOCK, 256)
            w_down[shift - 1, 2:4, :, :, 256:512] = value_part[...].astype(bf16).reshape(2, 2, BLOCK, 256)
            back_copy(shift).start()

        pl.when(me >= shift)(earlier)

    e_line.finish()

    def add_early(i, _):
        for k in range(3):
            own = early_parts[me, 3 * i + k].astype(f32)
            for s in range(3):
                own = own + early_landed[s, 3 * i + k].astype(f32)
            early_sum[i // 4, lax.rem(i, 4), k] = own.astype(bf16)
        return 0

    lax.fori_loop(0, 16, add_early, 0)
    e_plane = PlaneExchange(early_sum, e2, e3, e4, plane_s.at[0], plane_r.at[0])
    e_plane.start()

    attend_back(me)
    for h in range(4):
        put(39 + 2 * h, dot_tn(o_grad, context[h].astype(bf16)), late)
    put(47, dot_tn(o_latent[...], far[...]), late)
    kv_own[:, 0:256] = key_part[...]
    kv_own[:, 256:512] = value_part[...]

    e_plane.middle()
    e_plane.late()
    e_plane.finish()
    e_plane.total(m_plane, early_total)
    early_line[me] = early_total[...].astype(bf16)
    e_spread = LineGather(early_line, spread_s.at[0], spread_r.at[0])
    e_spread.start()
    for shift in (1, 2, 3):
        def collect(shift=shift):
            back_copy(shift).wait_recv()
            kv_own[...] += w_down[shift - 1, 0:2, :, :, 0:512].reshape(ROWS, 512).astype(f32)

        pl.when(me + shift < SEQ)(collect)

    e_spread.finish()
    own_early = pltpu.make_async_copy(early_line, all_early.at[y, z, core], loc.at[0])
    own_early.start()
    e_out = PlaneGather(early_line, all_early, out_s.at[0], out_r.at[0])
    e_out.start()

    key_value = kv_own[...].astype(bf16)
    thin = dot_nt(key_value, second_kv[...])
    back = dot(key_value[:, 0:256], key_rows()) + dot(key_value[:, 256:512], value_rows())
    for h in range(4):
        low = query_part(h)[...].astype(bf16)
        back = back + dot(low, got_qkv[h, :, :, 0:32].reshape(256, D))
        thin = thin + dot_nt(low, second_q[h])
        put(27 + 2 * h, dot_tn(qkv_latent[...], low)[0:16], late)
    qkv_grad = thin.astype(bf16)
    back = back + dot(qkv_grad, first_qkv[...])
    in_grad = dot_tn(qkv_grad, first_norm[...])
    for i in range(3):
        put(9 * i, in_grad[16 * i : 16 * i + 16], late)
    kv_out_grad = dot_tn(qkv_latent[...], key_value)
    put(35, kv_out_grad[16:32, 0:256], late)
    put(37, kv_out_grad[32:48, 256:512], late)
    late_parts = late.reshape(SEQ, LATE, 16, 128)
    l_line = LineSum(late_parts, late_landed, line_s.at[1], line_r.at[1])
    l_line.start()
    near[0] = (mixed_grad[...] + norm_back(layer_input[...].astype(f32), gain_first, back)).astype(bf16)
    result = pltpu.make_async_copy(near.at[0], input_grad, loc.at[2])
    result.start()

    own_early.wait()
    e_out.middle()
    l_line.finish()
    for i in range(16):
        low = jnp.zeros((16, 128), bf16)
        if i < LATE:
            own = late_parts[me, i].astype(f32)
            for s in range(3):
                own = own + late_landed[s, i].astype(f32)
            low = own.astype(bf16)
        late_sum[i // 4, i % 4, 0] = low
    l_plane = PlaneExchange(late_sum, l2, l3, l4, plane_s.at[1], plane_r.at[1])
    l_plane.start()
    l_plane.middle()
    l_plane.late()
    l_plane.finish()
    l_plane.total(m_plane, late_total)
    late_line[me] = late_total[...].astype(bf16)
    l_spread = LineGather(late_line, spread_s.at[1], spread_r.at[1])
    l_spread.start()
    e_out.late()
    l_spread.finish()
    own_late = pltpu.make_async_copy(late_line, all_late.at[y, z, core], loc.at[1])
    own_late.start()
    l_out = PlaneGather(late_line, all_late, out_s.at[1], out_r.at[1])
    l_out.start()
    own_late.wait()
    l_out.middle()
    e_out.last()
    l_out.late()
    e_out.finish()
    l_out.last()
    l_out.finish()
    result.wait()
    for shift in (1, 2, 3):
        pl.when(me >= shift)(lambda shift=shift: back_copy(shift).wait_send())
    for shift in (1, 2, 3):
        pl.when(me + shift < SEQ)(lambda shift=shift: kv_copy(shift).wait_send())


def layer(*arrays):
    dma = pltpu.SemaphoreType.DMA
    vmem = pltpu.VMEM

    def reduction(slots):
        whole = vmem((4, 4, slots, 16, 128), bf16)
        return [
            whole, whole, whole,
            vmem((slots, 4, 16, 128), f32),
            vmem((SEQ, slots, 4, 16, 128), bf16),
        ]

    return staged_call(
        layer_kernel, "layer", arrays, "v" * 13 + "hhvvvv",
        [
            ((ROWS, D), bf16, "v"),
            ((ROWS, D), bf16, "h"),
            ((4, 4, 2, SEQ, 3, 4, 16, 128), bf16, "h"),
            ((4, 4, 2, SEQ, 1, 4, 16, 128), bf16, "h"),
        ],
        [
            vmem((4, ROWS, 256), bf16),
            vmem((ROWS, 128), f32),
            vmem((4, ROWS, 256), f32),
            vmem((ROWS, D), f32),
            vmem((ROWS, 48), bf16),
            vmem((ROWS, 16), bf16),
            vmem((ROWS, D), f32),
            vmem((4, 4, 3, 16, 128), bf16),
            vmem((4, 4, 2, 48, D), bf16),
            vmem((4, 4, 2, 32, D), bf16),
            vmem((ROWS, D), bf16),
            vmem((SEQ, ROWS, 512), bf16),
            vmem((ROWS, D), f32),
            vmem((4, 4, 2, 2 * BLOCK, WIDE), bf16),
            vmem((4, 4, 2, BLOCK, WIDE), bf16),
            vmem((SEQ, ROWS, WIDE), bf16),
            vmem((SEQ, ROWS, WIDE), bf16),
            vmem((SEQ, ROWS, HIDDEN), bf16),
            vmem((SEQ, ROWS, HIDDEN), bf16),
            vmem((SEQ, ROWS, HIDDEN), bf16),
            vmem((2 * ROWS, WIDE), f32),
            vmem((SEQ * ROWS, 128), bf16),
            vmem((SEQ * ROWS, 128), bf16),
            vmem((48, HIDDEN), bf16),
            vmem((SEQ * FF_BLOCKS, 16, 128), bf16),
            vmem((3, FF_BLOCKS, 16, 128), bf16),
            vmem((ROWS, D), bf16),
            vmem((2, HALF, D), bf16),
            vmem((2, ROWS, D), bf16),
            vmem((2, ROWS, D), bf16),
        ]
        + [vmem((4, 4, 1, 2, 8, 128), f32)] * 4
        + reduction(3)
        + [
            vmem((SEQ * LATE, 16, 128), bf16),
            vmem((3, LATE, 16, 128), bf16),
            vmem((4, 4, 1, 16, 128), bf16),
        ]
        + reduction(1)
        + [
            dma((4, 11)), dma((4, 11)), dma((3,)), dma((3,)), dma((6,)), dma((6,)),
            dma((12,)), dma((12,)), dma((6,)), dma((6,)), dma((2, 3)), dma((2, 3)), dma((6,)),
            dma((3,)), dma((3,)), dma((3, 7)), dma((3, 7)), dma((2, 3)), dma((2, 3)), dma((2, 11)), dma((2, 11)),
        ],
        collective_id=1,
    )


def tables_kernel(
    early, late, done_out, done_grad,
    qkv_in, q_out, kv_out, o_in, o_out, mlp_in, mlp_out, down_in, down_out, layer_out, input_grad,
):
    def copy(source, start, count, out):
        for i in range(count):
            x, place = divmod(start + i, FF_BLOCKS if source is early else LATE)
            owner, slot = divmod(place, 3 if source is early else 1)
            out[:, i * 128 : (i + 1) * 128] = source[owner // 4, owner % 4, 0, x, slot, 0].astype(f32)

    layer_out[...] = done_out[...]
    input_grad[...] = done_grad[...]
    for i in range(2):
        copy(early, 54 * i, 54, mlp_out.at[0, i])
        copy(early, 162 + 9 * i, 9, mlp_in.at[0, i])
        copy(late, 35 + 2 * i, 2, kv_out.at[0, i])
    copy(early, 108, 54, down_in.at[0])
    copy(early, 180, 9, down_out.at[0])
    for i in range(3):
        copy(late, 9 * i, 9, qkv_in.at[0, i])
    copy(late, 27, 8, q_out.at[0])
    copy(late, 39, 8, o_in.at[0])
    copy(late, 47, 9, o_out.at[0])


def put_tables(early, late, done_out, done_grad):
    shapes = (
        (3, 16, D), (16, 1024), (2, 16, 256), (16, 1024), (16, D),
        (2, 16, D), (2, 16, 6912), (16, 6912), (16, D),
    )

    def one(shape):
        rest = len(shape)
        return pl.BlockSpec((1,) + shape, lambda a, rest=rest: (a,) + (0,) * rest)

    rows = pl.BlockSpec((ROWS // 8, D), lambda a: (a, 0))

    def blocks(slots):
        return pl.BlockSpec(
            (4, 4, 1, SEQ, slots, 1, 16, 128), lambda a: (0, 0, a // 4, 0, 0, a % 4, 0, 0)
        )

    return pl.pallas_call(
        tables_kernel,
        grid=(8,),
        out_shape=[jax.ShapeDtypeStruct((8,) + shape, f32) for shape in shapes]
        + [jax.ShapeDtypeStruct((ROWS, D), bf16)] * 2,
        in_specs=[blocks(3), blocks(1), rows, rows],
        out_specs=[one(shape) for shape in shapes] + [rows, rows],
        compiler_params=pltpu.CompilerParams(vmem_limit_bytes=63 * MIB),
        name="tables",
    )(early, late, done_out, done_grad)


def prepare_kernel(
    arrive, leave, ids, place_x, segments, w_query, w_key, w_value, w_gate, w_up, w_down,
    qkv_adapt_in, q_adapt_out, kv_adapt_out, o_adapt_in, o_adapt_out,
    mlp_adapt_in, mlp_adapt_out, down_adapt_in, down_adapt_out,
    gain_one, gain_two, gain_three, gain_four,
    pack_qkv, pack_gu, pack_down, own_marks, segment_rows, segment_column,
    first_qkv, second_q, second_kv, first_o, second_o, first_gu, second_down, ext_gu, ext_down, gains,
    table, q_held, kv_held, o_held, in_held, out_held, sem,
):
    chosen, me = ids[0], place_x[0]
    mlp_out, down_in = mlp_adapt_out.at[chosen], down_adapt_in.at[chosen]
    moves = [
        (mlp_out.at[0], table.at[0:16]),
        (mlp_out.at[1], table.at[16:32]),
        (down_in, table.at[32:48]),
        (q_adapt_out.at[chosen], q_held),
        (kv_adapt_out.at[chosen], kv_held),
        (o_adapt_in.at[chosen], o_held),
        (o_adapt_out.at[chosen], second_o),
        (mlp_adapt_in.at[chosen], in_held),
        (down_adapt_out.at[chosen], out_held),
        (qkv_adapt_in.at[chosen], first_qkv),
    ]
    moves = [pltpu.make_async_copy(src, dst, sem.at[i]) for i, (src, dst) in enumerate(moves)]
    for moving in moves:
        moving.start()
    iota = lambda shape, axis: lax.broadcasted_iota(jnp.int32, shape, axis)
    ones = lambda where: jnp.where(where, 1.0, 0.0).astype(bf16)

    def placed(count, first):
        return ones(iota((48, count), 0) == iota((48, count), 1) + first)

    table[48:128] = jnp.zeros((80, 6912), bf16)
    arrive()
    rows = dot(placed(32, 0), w_query[...]) + dot(placed(8, 32), w_key[...])
    pack_qkv[...] = (rows + dot(placed(8, 40), w_value[...])).astype(bf16)
    row, unit = iota((BLOCK, 216), 0), iota((BLOCK, 216), 1)
    quarter = ones((unit == me * UNITS + row) & (row < UNITS))
    pack_gu[0:64] = dot(quarter, w_gate[...]).astype(bf16)
    pack_gu[64:128] = dot(quarter, w_up[...]).astype(bf16)
    pack_down[...] = dot(quarter, w_down[...]).astype(bf16)

    for i, gain in enumerate((gain_one, gain_two, gain_three, gain_four)):
        gains[i : i + 1] = gain[...].reshape(1, D)
    leave(0, 1, 2)
    adapter = iota((8, 128), 0)
    for half in (0, 1):
        own_marks[half] = jnp.where((adapter + 4 * half == chosen) & (adapter < 4), 1.0, 0.0)
    for i in range(SEQ):
        segment_rows[i] = segments[:, i * ROWS : (i + 1) * ROWS]
    square = iota((ROWS, ROWS), 0) == iota((ROWS, ROWS), 1)
    segment_column[...] = jnp.sum(jnp.where(square, segment_rows[me], 0), -1, keepdims=True)

    for moving in moves:
        moving.wait()
    second_q[...] = jnp.zeros_like(second_q)
    for h in range(4):
        second_q[h, 0:16] = q_held[:, h * 256 : (h + 1) * 256]
        first_o[h] = o_held[:, h * 256 : (h + 1) * 256]
    second_kv[...] = jnp.zeros_like(second_kv)
    second_kv[16:32, 0:256] = kv_held[0]
    second_kv[32:48, 256:512] = kv_held[1]
    first_gu[0:16] = in_held[0]
    first_gu[16:32] = in_held[1]
    first_gu[32:128] = jnp.zeros((96, D), bf16)
    second_down[0:32] = jnp.zeros((32, D), bf16)
    second_down[32:48] = out_held[...]
    second_down[48:128] = jnp.zeros((80, D), bf16)

    def spread(d, _):
        first = 216 * d + me * UNITS
        start = jnp.minimum(first // 128 * 128, 6912 - 256)
        row = iota((BLOCK, 256), 0)
        picked = ones((first + row == start + iota((BLOCK, 256), 1)) & (row < UNITS))
        held = dot_nt(picked, table[:, pl.ds(pl.multiple_of(start, 128), 256)])
        lane = iota((BLOCK, 128), 1)
        ext_gu[d, 0:64] = jnp.where(lane < 16, held, 0.0).astype(bf16)
        ext_gu[d, 64:128] = jnp.where((lane >= 16) & (lane < 32), held, 0.0).astype(bf16)
        ext_down[d] = jnp.where(lane >= 32, held, 0.0).astype(bf16)
        return 0

    lax.fori_loop(0, 32, spread, 0, unroll=4)


def prepare(*arrays):
    shapes = [
        ((48, D), bf16), ((128, D), bf16), ((64, D), bf16), ((2, 8, 128), f32),
        ((SEQ, 1, ROWS), jnp.int32), ((ROWS, 1), jnp.int32),
        ((3, 16, D), bf16), ((4, 48, 256), bf16), ((48, 512), bf16), ((4, 16, 256), bf16), ((16, D), bf16),
        ((128, D), bf16), ((128, D), bf16), ((32, 2 * BLOCK, 128), bf16), ((32, BLOCK, 128), bf16),
        ((4, D), f32),
    ]
    return staged_call(
        prepare_kernel, "prepare", arrays, "ss" + "v" * 7 + "h" * 9 + "v" * 4,
        [shape + ("v",) for shape in shapes],
        [
            pltpu.VMEM((128, 6912), bf16),
            pltpu.VMEM((16, 1024), bf16),
            pltpu.VMEM((2, 16, 256), bf16),
            pltpu.VMEM((16, 1024), bf16),
            pltpu.VMEM((2, 16, D), bf16),
            pltpu.VMEM((16, D), bf16),
            pltpu.SemaphoreType.DMA((10,)),
        ],
    )


def body(
    layer_input, out_grad, segment_ids, adapter_ids,
    gain_attn_in, gain_attn_out, gain_mlp_in, gain_mlp_out,
    w_query, w_key, w_value, w_out, w_gate, w_up, w_down,
    qkv_adapt_in, q_adapt_out, kv_adapt_out, o_adapt_in, o_adapt_out,
    mlp_adapt_in, mlp_adapt_out, down_adapt_in, down_adapt_out,
):
    me = lax.axis_index("seq").astype(jnp.int32)
    (
        pack_qkv, pack_gu, pack_down, own_marks, segment_rows, segment_column,
        first_qkv, second_q, second_kv, first_o, second_o, first_gu, second_down, ext_gu, ext_down, gains,
    ) = prepare(
        adapter_ids, me.reshape(1), segment_ids, w_query.T, w_key.T, w_value.T, w_gate.T, w_up.T, w_down,
        qkv_adapt_in, q_adapt_out, kv_adapt_out, o_adapt_in, o_adapt_out,
        mlp_adapt_in, mlp_adapt_out, down_adapt_in, down_adapt_out,
        gain_attn_in, gain_attn_out, gain_mlp_in, gain_mlp_out,
    )
    first_qkv = first_qkv.reshape(48, D)
    layer_out, input_grad, all_early, all_late = layer(
        layer_input[0], pack_qkv, w_out, pack_gu, pack_down, segment_rows, segment_column, gains,
        first_qkv, second_q, second_kv, first_o, second_o,
        ext_gu.reshape(4, 4, 2, 2 * BLOCK, 128), ext_down.reshape(4, 4, 2, BLOCK, 128),
        first_gu, second_down, out_grad[0], own_marks,
    )
    *tables, layer_out, input_grad = put_tables(all_early, all_late, layer_out, input_grad)
    return (layer_out[None], input_grad[None], *tables)


def solution(mesh):
    tokens = P("dp", "seq", None)
    columns, rows = P(None, "dp"), P("dp", None)
    placed = (
        (tokens, tokens, P("dp", None), P("dp"))
        + (P(),) * 4
        + (columns, columns, columns, rows, columns, columns, rows)
        + (P(),) * 9
    )
    return jax.shard_map(
        body,
        mesh=mesh,
        in_specs=placed,
        out_specs=(tokens, tokens) + (P(),) * 9,
        check_vma=False,
    )
```

```python
import functools

import jax
import jax.numpy as jnp
from jax import lax
from jax.experimental import pallas as pl
from jax.experimental.pallas import tpu as pltpu
from jax.sharding import PartitionSpec as P

epsilon = 1e-06
softcap = 50.0
MESH = pl.DeviceIdType.MESH
bf16 = jnp.bfloat16
f32 = jnp.float32

D = 1152
SEQ = 4
ROWS = 256
UNITS = 54
BLOCK = 64
TILE = 256
MIB = 1 << 20


def dot(a, b):
    return lax.dot_general(a, b, (((1,), (0,)), ((), ())), preferred_element_type=f32)


def dot_nt(a, b):
    return lax.dot_general(a, b, (((1,), (1,)), ((), ())), preferred_element_type=f32)


def dot_tn(a, b):
    return lax.dot_general(a, b, (((0,), (0,)), ((), ())), preferred_element_type=f32)


def normed(values, gain_vector):
    return values * lax.rsqrt(jnp.mean(values * values, -1, keepdims=True) + epsilon) * gain_vector


def norm_back(values, gain_vector, cotangent):
    inverse = lax.rsqrt(jnp.mean(values * values, -1, keepdims=True) + epsilon)
    scaled = cotangent * gain_vector
    mean_part = jnp.mean(scaled * values, -1, keepdims=True)
    return inverse * (scaled - values * (inverse * inverse * mean_part))


def seq_peers():
    dp, me = lax.axis_index("dp"), lax.axis_index("seq")
    return [(dp, lax.rem(me + shift, SEQ)) for shift in (1, 2, 3)]


def greet(peers):
    barrier = pltpu.get_barrier_semaphore()
    for peer in peers:
        pl.semaphore_signal(barrier, inc=1, device_id=peer, device_id_type=MESH)
    pl.semaphore_wait(barrier, len(peers))


def staged_call(kernel, name, operands, kinds, results, scratch, collective_id=None):
    count, made = len(operands), len(results)
    held = [i for i in range(count) if kinds[i] == "v"]
    given = [i for i in range(made) if results[i][2] == "v"]

    def body(*refs):
        outer = list(refs[: count + made])
        inner = list(outer)
        rest = refs[count + made :]
        for n, i in enumerate(held):
            inner[i] = rest[n]
        for n, i in enumerate(given):
            inner[count + i] = rest[len(held) + n]
        sems, rest = rest[len(held) + len(given)], rest[len(held) + len(given) + 1 :]
        ins = {i: pltpu.make_async_copy(outer[i], inner[i], sems.at[n]) for n, i in enumerate(held)}
        outs = {
            i: pltpu.make_async_copy(inner[count + i], outer[count + i], sems.at[len(held) + n])
            for n, i in enumerate(given)
        }
        waiting, leaving = set(ins), []
        for moving in ins.values():
            moving.start()

        def arrive(*which):
            for i in which or sorted(waiting):
                if i in waiting:
                    waiting.discard(i)
                    ins[i].wait()

        def leave(*which):
            for i in which:
                outs[i].start()
                leaving.append(i)

        kernel(arrive, leave, *inner, *rest)
        leave(*[i for i in given if i not in leaving])
        for i in given:
            outs[i].wait()

    spaces = {"v": pl.ANY, "h": pl.ANY, "s": pltpu.SMEM}
    params = dict(vmem_limit_bytes=63 * MIB)
    if collective_id is not None:
        params.update(collective_id=collective_id, has_side_effects=True)
    return pl.pallas_call(
        body,
        out_shape=[jax.ShapeDtypeStruct(shape, dtype) for shape, dtype, _ in results],
        in_specs=[pl.BlockSpec(memory_space=spaces[k]) for k in kinds],
        out_specs=[pl.BlockSpec(memory_space=pl.ANY)] * made,
        scratch_shapes=[pltpu.VMEM(operands[i].shape, operands[i].dtype) for i in held]
        + [pltpu.VMEM(results[i][0], results[i][1]) for i in given]
        + [pltpu.SemaphoreType.DMA((len(held) + len(given),))]
        + scratch,
        compiler_params=pltpu.CompilerParams(**params),
        name=name,
    )(*operands)


def place():
    dp = lax.axis_index("dp")
    return lax.axis_index("seq"), dp // 8, lax.rem(dp // 2, 4), lax.rem(dp, 2)


def at(x, y, z, core):
    return ((lax.rem(y, 4) * 4 + lax.rem(z, 4)) * 2 + core, lax.rem(x, 4))


def plane_peers():
    x, y, z, core = place()
    return [at(x, y + k, z, core) for k in (1, 2, 3)] + [at(x, y, z + k, core) for k in (1, 2, 3)]


def far_siblings():
    x, y, z, core = place()
    return [at(x, y, z + k, 1 - core) for k in (1, 2, 3)]


def sibling():
    x, y, z, core = place()
    return at(x, y, z, 1 - core)


def remote(src, dst, send_sem, recv_sem, peer):
    return pltpu.make_async_remote_copy(
        src_ref=src, dst_ref=dst, send_sem=send_sem, recv_sem=recv_sem,
        device_id=peer, device_id_type=MESH,
    )


class PlaneGather:
    def __init__(self, own, buffer, send_sem, recv_sem, direct=False):
        self.x, self.y, self.z, self.core = place()
        self.own, self.buffer, self.send, self.recv = own, buffer, send_sem, recv_sem
        self.direct = direct

    def _copy(self, src, dst, slot, peer):
        return remote(src, dst, self.send.at[slot], self.recv.at[slot], peer)

    def _first(self, k):
        x, y, z, core = self.x, self.y, self.z, self.core
        peer = at(x, y + k * (1 - core), z + k * core, core)
        return self._copy(self.own, self.buffer.at[y, z, core], k - 1, peer)

    def _line(self, core, back):
        if core == 0:
            return self.buffer.at[:, lax.rem(self.z + 4 - back, 4), 0]
        return self.buffer.at[lax.rem(self.y + 4 - back, 4), :, 1]

    def _second(self, core, k):
        line = self._line(core, 0)
        peer = at(self.x, self.y + k * core, self.z + k * (1 - core), core)
        return self._copy(line, line, 2 + k, peer)

    def _pass(self, core, half):
        back, k = ((1, 1), (3, 3))[half]
        line = self._line(core, back).at[2 * half : 2 * half + 2]
        peer = at(self.x, self.y + k * core, self.z + k * (1 - core), core)
        return self._copy(line, line, (4, 10)[half], peer)

    def _swap(self, core, back):
        line = self._line(core, back)
        return self._copy(line, line, 6 + back, at(self.x, self.y, self.z, 1 - core))

    def _both(self, act):
        for core in (0, 1):
            pl.when(self.core == core)(functools.partial(act, core))

    def start(self):
        for k in (2, 1, 3):
            self._first(k).start()

    def middle(self):
        for k in (1, 3, 2):
            self._first(k).wait()

        def act(core):
            for k in (2, 1, 3) if self.direct else (1, 3):
                self._second(core, k).start()
            self._swap(core, 0).start()

        self._both(act)

    def late(self):
        def act(core):
            for half, k in ((0, 1), (1, 3)):
                self._second(core, k).wait()
                if not self.direct:
                    self._pass(core, half).start()
                self._swap(core, k).start()

        self._both(act)

    def last(self):
        def act(core):
            if self.direct:
                self._second(core, 2).wait()
            else:
                for half in (0, 1):
                    self._pass(core, half).wait()
            self._swap(core, 2).start()

        self._both(act)

    def finish(self):
        def act(core):
            for back in (0, 1, 3, 2):
                self._swap(core, back).wait()

        self._both(act)


class LineSum:
    def __init__(self, parts, landed, send_sem, recv_sem):
        self.me, self.peers = lax.axis_index("seq"), seq_peers()
        self.parts, self.landed, self.send, self.recv = parts, landed, send_sem, recv_sem

    def _copy(self, shift):
        return remote(
            self.parts.at[lax.rem(self.me + shift, SEQ)], self.landed.at[shift - 1],
            self.send.at[shift - 1], self.recv.at[shift - 1], self.peers[shift - 1],
        )

    def start(self):
        for shift in (2, 1, 3):
            self._copy(shift).start()

    def finish(self):
        for shift in (1, 3, 2):
            self._copy(shift).wait()


class PlaneExchange:
    def __init__(self, first, second, third, fourth, send_sem, recv_sem):
        self.x, self.y, self.z, self.core = place()
        self.first, self.second, self.third, self.fourth = first, second, third, fourth
        self.send, self.recv = send_sem, recv_sem

    def _copy(self, src, dst, slot, peer):
        return remote(src, dst, self.send.at[slot], self.recv.at[slot], peer)

    def _along_y(self, k):
        y = lax.rem(self.y + k, 4)
        return self._copy(self.first.at[y], self.second.at[k], k - 1, at(self.x, y, self.z, self.core))

    def _along_z(self, k):
        z = lax.rem(self.z + k, 4)
        return self._copy(self.second.at[:, z], self.third.at[k], 2 + k, at(self.x, self.y, z, self.core))

    def _other(self, k):
        z = lax.rem(self.z + k, 4)
        return self._copy(self.second.at[:, z], self.fourth.at[k], 6 + k, at(self.x, self.y, z, 1 - self.core))

    def start(self):
        for k in (2, 1, 3):
            self._along_y(k).start()
        self.second[0] = self.first[self.y]

    def middle(self):
        for k in (1, 3, 2):
            self._along_y(k).wait()
        for k in (2, 1, 3):
            self._along_z(k).start()
        for k in (2, 1, 3, 0):
            self._other(k).start()
        self.third[0] = self.second[:, self.z]

    def late(self):
        for k in (1, 3, 2):
            self._along_z(k).wait()
        for k in (0, 1, 3, 2):
            self._other(k).wait()

    def total(self, marks, out):
        slots = self.first.shape[2]
        out[...] = jnp.zeros_like(out)

        def add(i, _):
            kz, ky = i // 4, lax.rem(i, 4)
            for held, known in ((self.third, marks.third), (self.fourth, marks.fourth)):
                weights = known[kz, ky, 0, self.core]
                for slot in range(slots):
                    rows = held[kz, ky, slot].astype(f32)
                    for a in range(4):
                        out[slot, a] += weights[a : a + 1] * rows
            return 0

        lax.fori_loop(0, 16, add, 0)


class LineGather:
    def __init__(self, buffer, send_sem, recv_sem):
        self.me, self.peers = lax.axis_index("seq"), seq_peers()
        self.buffer, self.send, self.recv = buffer, send_sem, recv_sem

    def _copy(self, shift):
        mine = self.buffer.at[self.me]
        return remote(mine, mine, self.send.at[shift - 1], self.recv.at[shift - 1], self.peers[shift - 1])

    def start(self):
        for shift in (2, 1, 3):
            self._copy(shift).start()

    def finish(self):
        for shift in (1, 3, 2):
            self._copy(shift).wait()


WIDE = D + 128
HIDDEN = 32 * BLOCK
HALF = ROWS // 2
ROOT = 0.7978845608028654
CUBE = ROOT * 0.044715
FF_BLOCKS = 48
LATE = 14
SCORE = 1.0 / 16.0


def allowed_pairs(segment_rows, segment_column, me, chunk):
    keys = lax.broadcasted_iota(jnp.int32, (ROWS, ROWS), 1) + chunk * ROWS
    queries = lax.broadcasted_iota(jnp.int32, (ROWS, ROWS), 0) + me * ROWS
    return (segment_column[...] == segment_rows[chunk]) & (keys <= queries)


def layer_kernel(
    arrive, leave,
    layer_input, pack_qkv, pack_o, pack_gu, pack_down, segment_rows, segment_column, gains,
    first_qkv, second_q, second_kv, first_o, second_o,
    ext_gu, ext_down, first_gu, second_down, out_grad, own_marks,
    layer_out, input_grad, all_early, all_late,
    queries, totals, context, attn_proj, qkv_latent, o_latent, mixed_grad, early_sum,
    got_qkv, got_o, first_norm, kv_all, mixed,
    w_gu, w_down, inputs, down_grads, hidden, act_gate, act_up, total,
    down_latents, gu_grads, packed, early, early_landed,
    far, landed_half, near, landed,
    m1, m2, m3, m4, e2, e3, e4, early_total, early_line,
    late, late_landed, late_sum, l2, l3, l4, late_total, late_line,
    sem_s, sem_r, kv_s, kv_r, tok_s, tok_r, rs_s, rs_r, ag_s, ag_r, line_s, line_r, loc,
    back_s, back_r, plane_s, plane_r, spread_s, spread_r, out_s, out_r,
):
    me, y, z, core = place()
    line = seq_peers()
    ahead, _, behind = line
    greet(line + plane_peers() + far_siblings() + [sibling()])

    all_gu, all_down = w_gu.at[:, :, :, :, 0:D], w_down.at[:, :, :, :, 0:D]
    gathers = [
        PlaneGather(own, got, sem_s.at[i], sem_r.at[i])
        for i, (own, got) in enumerate(
            ((pack_qkv, got_qkv), (pack_o, got_o), (pack_gu, all_gu), (pack_down, all_down))
        )
    ]
    g_qkv, g_o, g_gu, g_down = gathers
    own_copies = [
        pltpu.make_async_copy(g.own, g.buffer.at[y, z, core], loc.at[i]) for i, g in enumerate(gathers)
    ]
    ext_copies = [
        pltpu.make_async_copy(ext_gu, w_gu.at[:, :, :, :, D:WIDE], loc.at[4]),
        pltpu.make_async_copy(ext_down, w_down.at[:, :, :, :, D:WIDE], loc.at[5]),
    ]
    arrive(1)
    g_qkv.start()
    own_copies[0].start()
    arrive()
    for moving in own_copies[1:] + ext_copies:
        moving.start()
    gain_first, gain_second, gain_third, gain_fourth = [gains[i : i + 1] for i in range(4)]
    first_norm[...] = normed(layer_input[...].astype(f32), gain_first).astype(bf16)
    latent = dot_nt(first_norm[...], first_qkv[...]).astype(bf16)
    qkv_latent[...] = latent
    for moving in own_copies:
        moving.wait()
    g_qkv.middle()
    g_o.start()
    g_qkv.late()
    g_gu.start()
    g_down.start()
    g_qkv.last()
    g_o.middle()
    g_qkv.finish()

    def unmix(i, _):
        pairs = got_qkv[i, :, :, 32:48].astype(f32).reshape(8, 2, 8, D)
        got_qkv[i, 0:2, :, 32:48] = pairs[:, 0].reshape(2, 2, 16, D).astype(bf16)
        got_qkv[i, 2:4, :, 32:48] = pairs[:, 1].reshape(2, 2, 16, D).astype(bf16)
        return 0

    lax.fori_loop(0, 4, unmix, 0)
    key_rows = lambda: got_qkv[:, 0:2, :, 32:48].reshape(256, D)
    value_rows = lambda: got_qkv[:, 2:4, :, 32:48].reshape(256, D)
    kv_low = dot(latent, second_kv[...])
    kv_all[me, :, 0:256] = (dot_nt(first_norm[...], key_rows()) + kv_low[:, 0:256]).astype(bf16)
    kv_all[me, :, 256:512] = (dot_nt(first_norm[...], value_rows()) + kv_low[:, 256:512]).astype(bf16)

    def kv_copy(shift):
        return remote(kv_all.at[me], kv_all.at[me], kv_s.at[shift - 1], kv_r.at[shift - 1], line[shift - 1])

    for shift in (1, 2, 3):
        pl.when(me + shift < SEQ)(lambda shift=shift: kv_copy(shift).start())

    def query(h, _):
        rows = got_qkv[h, :, :, 0:32].reshape(256, D)
        queries[h] = (dot_nt(first_norm[...], rows) + dot(latent, second_q[h])).astype(bf16)
        context[h] = jnp.zeros((ROWS, 256), f32)
        return 0

    lax.fori_loop(0, 4, query, 0)
    totals[...] = jnp.zeros_like(totals)
    head_lane = lax.broadcasted_iota(jnp.int32, (ROWS, 128), 1)

    def total_of(h):
        return jnp.sum(jnp.where(head_lane == h, totals[...], 0.0), -1, keepdims=True)

    g_gu.middle()
    g_down.middle()

    def attend(chunk):
        keys, held = kv_all[chunk, :, 0:256], kv_all[chunk, :, 256:512]
        allowed = allowed_pairs(segment_rows, segment_column, me, chunk)

        def head(h, _):
            bent = jnp.tanh(dot_nt(queries[h], keys) * (SCORE / softcap))
            weight = jnp.where(allowed, jnp.exp(softcap * bent), 0.0).astype(bf16)
            totals[...] += jnp.where(head_lane == h, jnp.sum(weight.astype(f32), -1, keepdims=True), 0.0)
            context[h] += dot(weight, held)
            return 0

        lax.fori_loop(0, 4, head, 0)

    attend(me)
    g_o.late()
    g_o.last()
    for shift in (1, 2, 3):
        def arrived(shift=shift):
            kv_copy(shift).wait_recv()
            attend(me - shift)

        pl.when(me >= shift)(arrived)

    g_o.finish()
    proj = jnp.zeros((ROWS, D), f32)
    thin = jnp.zeros((ROWS, 16), f32)
    for h in range(4):
        context[h] = context[h] / total_of(h)
        low = context[h].astype(bf16)
        proj = proj + dot(low, got_o[h].reshape(256, D))
        thin = thin + dot_nt(low, first_o[h])
    o_latent[...] = thin.astype(bf16)
    proj = proj + dot(o_latent[...], second_o[...])
    attn_proj[...] = proj
    mid = layer_input[...].astype(f32) + normed(proj, gain_second)
    mixed[...] = mid
    inputs[0, :, 0:D] = normed(mid, gain_third).astype(bf16)

    low, high = slice(0, HALF), slice(HALF, ROWS)

    def passing(buffer, send, recv):
        def move(from_slot, to_slot, rows, index, peer):
            src, dst = buffer.at[from_slot, rows, 0:D], buffer.at[to_slot, rows, 0:D]
            return remote(src, dst, send.at[index], recv.at[index], peer)

        return [
            move(0, 2, low, 0, ahead), move(0, 1, high, 1, behind),
            move(0, 2, high, 2, ahead), move(0, 1, low, 3, behind),
            move(2, 3, low, 4, ahead), move(1, 3, high, 5, behind),
        ]

    token_moves = passing(inputs, tok_s, tok_r)
    for i in range(4):
        token_moves[i].start()
    g_gu.late()
    for i in range(4):
        for k in range(4):
            m1[i, k, 0] = own_marks[...]
    m_plane = PlaneExchange(m1, m2, m3, m4, plane_s.at[2], plane_r.at[2])
    g_down.late()
    g_gu.last()
    token_moves[0].wait()
    token_moves[4].start()
    token_moves[1].wait()
    token_moves[5].start()
    for moving in ext_copies:
        moving.wait()
    g_gu.finish()

    def gate_rows(j):
        return w_gu[j // 2, pl.ds(2 * lax.rem(j, 2), 2), :, 0:64].reshape(TILE, WIDE)

    def up_rows(j):
        return w_gu[j // 2, pl.ds(2 * lax.rem(j, 2), 2), :, 64:128].reshape(TILE, WIDE)

    def down_rows(j):
        return w_down[j // 2, pl.ds(2 * lax.rem(j, 2), 2)].reshape(TILE, WIDE)

    def lanes(j, size=TILE):
        return pl.ds(pl.multiple_of(j * size, size), size)

    def forward_open(slot, many):
        size = many * ROWS
        part = slice(slot, slot + many)
        inputs[part, :, D:WIDE] = (
            dot_nt(inputs[part, :, 0:D].reshape(size, D), first_gu[...]).astype(bf16).reshape(many, ROWS, 128)
        )

        def step(j, _):
            rows = inputs[part].reshape(size, WIDE)
            gate = dot_nt(rows, gate_rows(j))
            upward = dot_nt(rows, up_rows(j))
            square = gate * gate
            bent = jnp.tanh(gate * (ROOT + CUBE * square))
            half = 0.5 * bent + 0.5
            gelu = gate * half
            slope = half + gelu * ((1.0 - bent) * (ROOT + 3.0 * CUBE * square))
            shape = (many, ROWS, TILE)
            hidden[part, :, lanes(j)] = (gelu * upward).astype(bf16).reshape(shape)
            act_gate[part, :, lanes(j)] = gelu.astype(bf16).reshape(shape)
            act_up[part, :, lanes(j)] = (upward * slope).astype(bf16).reshape(shape)
            return 0

        lax.fori_loop(0, 8, step, 0, unroll=4)

    def forward_close(slot, many):
        size = many * ROWS
        part = slice(slot, slot + many)

        def close(n, _):
            rows = hidden[part].reshape(size, HIDDEN)
            total[0:size, lanes(n)] = dot(rows, w_down[:, :, :, :, lanes(n)].reshape(HIDDEN, TILE))
            return 0

        lax.fori_loop(0, 5, close, 0)
        down_latent = total[0:size, D:WIDE].astype(bf16)
        down_latents[slot * ROWS : slot * ROWS + size] = down_latent
        total[0:size, 0:D] += dot(down_latent, second_down[...])

    def backward_open(slot, many):
        size = many * ROWS
        part = slice(slot, slot + many)
        latent_grad = dot_nt(down_grads[part, :, 0:D].reshape(size, D), second_down[...])
        down_grads[part, :, D:WIDE] = latent_grad.astype(bf16).reshape(many, ROWS, 128)

        def step(j, _):
            shape = (many, ROWS, TILE)
            hidden_grad = dot_nt(down_grads[part].reshape(size, WIDE), down_rows(j)).reshape(shape)
            gate_grad = (hidden_grad * act_up[part, :, lanes(j)].astype(f32)).astype(bf16)
            up_grad = (hidden_grad * act_gate[part, :, lanes(j)].astype(f32)).astype(bf16)
            act_up[part, :, lanes(j)] = gate_grad
            act_gate[part, :, lanes(j)] = up_grad
            return 0

        lax.fori_loop(0, 8, step, 0, unroll=4)

    def backward_close(slot, many):
        size = many * ROWS
        part = slice(slot, slot + many)

        def close(n, _):
            total[0:size, lanes(n)] = dot(
                act_up[part].reshape(size, HIDDEN), w_gu[:, :, :, 0:64, lanes(n)].reshape(HIDDEN, TILE)
            ) + dot(
                act_gate[part].reshape(size, HIDDEN), w_gu[:, :, :, 64:128, lanes(n)].reshape(HIDDEN, TILE)
            )
            return 0

        lax.fori_loop(0, 5, close, 0)
        gu_grad = total[0:size, D:WIDE].astype(bf16)
        gu_grads[slot * ROWS : slot * ROWS + size] = gu_grad
        total[0:size, 0:D] += dot(gu_grad, first_gu[...])

    def factors():
        latent = inputs[:, :, D:WIDE].reshape(SEQ * ROWS, 128)[:, 0:32]
        latent_grad = down_grads[:, :, D:WIDE].reshape(SEQ * ROWS, 128)[:, 32:48]

        def piece(j, _):
            gate_part = dot_tn(latent, act_up[:, :, lanes(j)].reshape(SEQ * ROWS, TILE))
            up_part = dot_tn(latent, act_gate[:, :, lanes(j)].reshape(SEQ * ROWS, TILE))
            down_part = dot_tn(latent_grad, hidden[:, :, lanes(j)].reshape(SEQ * ROWS, TILE))
            packed[0:16, lanes(j)] = gate_part[0:16].astype(bf16)
            packed[16:32, lanes(j)] = up_part[16:32].astype(bf16)
            packed[32:48, lanes(j)] = down_part.astype(bf16)
            return 0

        lax.fori_loop(0, 8, piece, 0, unroll=2)

    def scatter(base, finish, others, own=None):
        finish(3, 1)
        far[...] = total[0:ROWS, 0:D].astype(bf16)
        far_moves = [
            remote(far.at[low], landed_half.at[0], rs_s.at[base + 4], rs_r.at[base + 4], behind),
            remote(far.at[high], landed_half.at[1], rs_s.at[base + 5], rs_r.at[base + 5], ahead),
        ]
        for moving in far_moves:
            moving.start()
        finish(1, 2)
        near_moves = [
            remote(near.at[0, low], landed.at[0, low], rs_s.at[base], rs_r.at[base], ahead),
            remote(near.at[0, high], landed.at[0, high], rs_s.at[base + 1], rs_r.at[base + 1], ahead),
            remote(near.at[1, high], landed.at[1, high], rs_s.at[base + 2], rs_r.at[base + 2], behind),
            remote(near.at[1, low], landed.at[1, low], rs_s.at[base + 3], rs_r.at[base + 3], behind),
        ]
        near[0, low] = total[0:HALF, 0:D].astype(bf16)
        near_moves[0].start()
        near[1, high] = total[ROWS + HALF : 2 * ROWS, 0:D].astype(bf16)
        near_moves[2].start()
        near[0, high] = total[HALF:ROWS, 0:D].astype(bf16)
        near[1, low] = total[ROWS : ROWS + HALF, 0:D].astype(bf16)
        if own is not None:
            own()
        far_moves[1].wait()
        near[0, high] = (near[0, high].astype(f32) + landed_half[1].astype(f32)).astype(bf16)
        near_moves[1].start()
        far_moves[0].wait()
        near[1, low] = (near[1, low].astype(f32) + landed_half[0].astype(f32)).astype(bf16)
        near_moves[3].start()
        others()
        for moving in near_moves:
            moving.wait()

    def forward_own():
        forward_close(0, 1)
        mixed_grad[...] = total[0:ROWS, 0:D]

    m_plane.start()
    forward_open(0, 1)
    g_down.last()
    token_moves[2].wait()
    token_moves[3].wait()
    forward_open(1, 2)
    token_moves[4].wait()
    token_moves[5].wait()
    forward_open(3, 1)
    g_down.finish()
    scatter(0, forward_close, forward_own)
    m_plane.middle()
    down_proj = mixed_grad[...] + landed[0].astype(f32) + landed[1].astype(f32)
    layer_out[...] = (mixed[...] + normed(down_proj, gain_fourth)).astype(bf16)
    leave(0)
    down_grads[0, :, 0:D] = norm_back(down_proj, gain_fourth, out_grad[...].astype(f32)).astype(bf16)
    grad_moves = passing(down_grads, ag_s, ag_r)
    for i in range(4):
        grad_moves[i].start()

    early_parts = early.reshape(SEQ, FF_BLOCKS, 16, 128)
    e_line = LineSum(early_parts, early_landed, line_s.at[0], line_r.at[0])

    def unpad(j, _):
        start = jnp.minimum((j * 128 // 216) // 2 * 128, HIDDEN // 2 - 256)
        lane = start + lax.broadcasted_iota(jnp.int32, (256, 128), 0)
        within = lane & 63
        unit = (lane >> 6) * 216 + me * UNITS + within
        goal = j * 128 + lax.broadcasted_iota(jnp.int32, (256, 128), 1)
        chosen = jnp.where((unit == goal) & (within < UNITS), 1.0, 0.0).astype(bf16)
        for half in (0, 1):
            rows = packed[:, pl.ds(pl.multiple_of(start + half * HIDDEN // 2, 128), 256)]
            moved = dot(rows, chosen).astype(bf16)
            for i in range(3):
                early[54 * i + 27 * half + j] = moved[16 * i : 16 * i + 16]
        return 0

    def put(start, rows, buffer):
        for i in range(rows.shape[1] // 128):
            buffer[start + i] = rows[:, i * 128 : (i + 1) * 128].astype(bf16)

    def spread_factors():
        lax.fori_loop(0, 27, unpad, 0, unroll=3)
        all_gu_grads = gu_grads[...]
        gu_part = dot_tn(all_gu_grads[:, 0:32], inputs[:, :, 0:D].reshape(SEQ * ROWS, D))
        put(162, gu_part[0:16], early)
        put(171, gu_part[16:32], early)
        put(180, dot_tn(down_latents[:, 32:48], down_grads[:, :, 0:D].reshape(SEQ * ROWS, D)), early)
        for i in range(189, 192):
            early[i] = jnp.zeros((16, 128), bf16)
        e_line.start()

    backward_open(0, 1)
    backward_close(0, 1)
    mixed_grad[...] = total[0:ROWS, 0:D]
    m_plane.late()
    grad_moves[0].wait()
    grad_moves[4].start()
    grad_moves[1].wait()
    grad_moves[5].start()
    grad_moves[2].wait()
    grad_moves[3].wait()
    backward_open(1, 2)
    grad_moves[4].wait()
    grad_moves[5].wait()
    backward_open(3, 1)

    def all_factors():
        factors()
        spread_factors()

    scatter(6, backward_close, all_factors)
    own_sum = mixed_grad[...] + landed[0].astype(f32) + landed[1].astype(f32)
    mixed_grad[...] = out_grad[...].astype(f32) + norm_back(mixed[...], gain_third, own_sum)

    head_grads = [down_grads.at[3, :, 256 * h : 256 * h + 256] for h in range(4)]
    key_part, value_part = total.at[0:ROWS, 512:768], total.at[0:ROWS, 768:1024]
    kv_own = total.at[ROWS : 2 * ROWS, 512:1024]

    def query_part(h):
        row, lane = h // 2, lax.rem(h, 2)
        return total.at[pl.ds(pl.multiple_of(row * ROWS, ROWS), ROWS), pl.ds(pl.multiple_of(lane * 256, 256), 256)]

    def head_grad(h):
        return down_grads[3, :, pl.ds(pl.multiple_of(h * 256, 256), 256)]

    far[...] = norm_back(attn_proj[...], gain_second, mixed_grad[...]).astype(bf16)
    o_grad = dot_nt(far[...], second_o[...]).astype(bf16)

    for h in range(4):
        low = (dot_nt(far[...], got_o[h].reshape(256, D)) + dot(o_grad, first_o[h])).astype(bf16)
        head_grads[h][...] = low
        query_part(h)[...] = jnp.zeros((ROWS, 256), f32)

    def attend_back(chunk):
        keys, held = kv_all[chunk, :, 0:256], kv_all[chunk, :, 256:512]
        allowed = allowed_pairs(segment_rows, segment_column, me, chunk)
        key_part[...] = jnp.zeros_like(key_part)
        value_part[...] = jnp.zeros_like(value_part)

        def head(h, _):
            bent = jnp.tanh(dot_nt(queries[h], keys) * (SCORE / softcap))
            weight = jnp.where(allowed, jnp.exp(softcap * bent), 0.0).astype(bf16).astype(f32)
            probs = weight / total_of(h)
            grads = head_grad(h)
            centre = jnp.sum(grads.astype(f32) * context[h], -1, keepdims=True)
            prob_grad = dot_nt(grads, held)
            raw_grad = (probs * (prob_grad - centre) * ((1.0 - bent * bent) * SCORE)).astype(bf16)
            query_part(h)[...] += dot(raw_grad, keys)
            key_part[...] += dot_tn(raw_grad, queries[h])
            value_part[...] += dot_tn(probs.astype(bf16), grads)
            return 0

        lax.fori_loop(0, 4, head, 0)

    def back_copy(shift):
        peer = line[3 - shift]
        return remote(w_down.at[shift - 1, 2:4, :, :, 0:512], w_down.at[shift - 1, 0:2, :, :, 0:512], back_s.at[shift - 1], back_r.at[shift - 1], peer)

    for shift in (3, 2, 1):
        def earlier(shift=shift):
            attend_back(me - shift)
            w_down[shift - 1, 2:4, :, :, 0:256] = key_part[...].astype(bf16).reshape(2, 2, BLOCK, 256)
            w_down[shift - 1, 2:4, :, :, 256:512] = value_part[...].astype(bf16).reshape(2, 2, BLOCK, 256)
            back_copy(shift).start()

        pl.when(me >= shift)(earlier)

    e_line.finish()

    def add_early(i, _):
        for k in range(3):
            own = early_parts[me, 3 * i + k].astype(f32)
            for s in range(3):
                own = own + early_landed[s, 3 * i + k].astype(f32)
            early_sum[i // 4, lax.rem(i, 4), k] = own.astype(bf16)
        return 0

    lax.fori_loop(0, 16, add_early, 0)
    e_plane = PlaneExchange(early_sum, e2, e3, e4, plane_s.at[0], plane_r.at[0])
    e_plane.start()

    attend_back(me)
    for h in range(4):
        put(39 + 2 * h, dot_tn(o_grad, context[h].astype(bf16)), late)
    put(47, dot_tn(o_latent[...], far[...]), late)
    kv_own[:, 0:256] = key_part[...]
    kv_own[:, 256:512] = value_part[...]

    e_plane.middle()
    e_plane.late()
    e_plane.total(m_plane, early_total)
    early_line[me] = early_total[...].astype(bf16)
    e_spread = LineGather(early_line, spread_s.at[0], spread_r.at[0])
    e_spread.start()
    for shift in (1, 2, 3):
        def collect(shift=shift):
            back_copy(shift).wait_recv()
            kv_own[...] += w_down[shift - 1, 0:2, :, :, 0:512].reshape(ROWS, 512).astype(f32)

        pl.when(me + shift < SEQ)(collect)

    key_value = kv_own[...].astype(bf16)
    thin = dot_nt(key_value, second_kv[...])
    back = dot(key_value[:, 0:256], key_rows()) + dot(key_value[:, 256:512], value_rows())
    for h in range(4):
        low = query_part(h)[...].astype(bf16)
        back = back + dot(low, got_qkv[h, :, :, 0:32].reshape(256, D))
        thin = thin + dot_nt(low, second_q[h])
        put(27 + 2 * h, dot_tn(qkv_latent[...], low)[0:16], late)
    qkv_grad = thin.astype(bf16)
    back = back + dot(qkv_grad, first_qkv[...])
    in_grad = dot_tn(qkv_grad, first_norm[...])
    for i in range(3):
        put(9 * i, in_grad[16 * i : 16 * i + 16], late)
    kv_out_grad = dot_tn(qkv_latent[...], key_value)
    put(35, kv_out_grad[16:32, 0:256], late)
    put(37, kv_out_grad[32:48, 256:512], late)
    late_parts = late.reshape(SEQ, LATE, 16, 128)
    l_line = LineSum(late_parts, late_landed, line_s.at[1], line_r.at[1])
    l_line.start()
    e_spread.finish()
    own_early = pltpu.make_async_copy(early_line, all_early.at[y, z, core], loc.at[0])
    own_early.start()
    e_out = PlaneGather(early_line, all_early, out_s.at[0], out_r.at[0])
    e_out.start()
    near[0] = (mixed_grad[...] + norm_back(layer_input[...].astype(f32), gain_first, back)).astype(bf16)
    result = pltpu.make_async_copy(near.at[0], input_grad, loc.at[2])
    result.start()

    l_line.finish()
    for i in range(16):
        low = jnp.zeros((16, 128), bf16)
        if i < LATE:
            own = late_parts[me, i].astype(f32)
            for s in range(3):
                own = own + late_landed[s, i].astype(f32)
            low = own.astype(bf16)
        late_sum[i // 4, i % 4, 0] = low
    l_plane = PlaneExchange(late_sum, l2, l3, l4, plane_s.at[1], plane_r.at[1])
    l_plane.start()
    own_early.wait()
    e_out.middle()
    l_plane.middle()
    l_plane.late()
    l_plane.total(m_plane, late_total)
    late_line[me] = late_total[...].astype(bf16)
    l_spread = LineGather(late_line, spread_s.at[1], spread_r.at[1])
    l_spread.start()
    e_out.late()
    l_spread.finish()
    own_late = pltpu.make_async_copy(late_line, all_late.at[y, z, core], loc.at[1])
    own_late.start()
    l_out = PlaneGather(late_line, all_late, out_s.at[1], out_r.at[1], direct=True)
    l_out.start()
    own_late.wait()
    l_out.middle()
    e_out.last()
    l_out.late()
    e_out.finish()
    l_out.last()
    l_out.finish()
    result.wait()
    for shift in (1, 2, 3):
        pl.when(me >= shift)(lambda shift=shift: back_copy(shift).wait_send())
    for shift in (1, 2, 3):
        pl.when(me + shift < SEQ)(lambda shift=shift: kv_copy(shift).wait_send())


def layer(*arrays):
    dma = pltpu.SemaphoreType.DMA
    vmem = pltpu.VMEM

    def reduction(slots):
        whole = vmem((4, 4, slots, 16, 128), bf16)
        return [
            whole, whole, whole,
            vmem((slots, 4, 16, 128), f32),
            vmem((SEQ, slots, 4, 16, 128), bf16),
        ]

    return staged_call(
        layer_kernel, "layer", arrays, "v" * 13 + "hhvvvv",
        [
            ((ROWS, D), bf16, "v"),
            ((ROWS, D), bf16, "h"),
            ((4, 4, 2, SEQ, 3, 4, 16, 128), bf16, "h"),
            ((4, 4, 2, SEQ, 1, 4, 16, 128), bf16, "h"),
        ],
        [
            vmem((4, ROWS, 256), bf16),
            vmem((ROWS, 128), f32),
            vmem((4, ROWS, 256), f32),
            vmem((ROWS, D), f32),
            vmem((ROWS, 48), bf16),
            vmem((ROWS, 16), bf16),
            vmem((ROWS, D), f32),
            vmem((4, 4, 3, 16, 128), bf16),
            vmem((4, 4, 2, 48, D), bf16),
            vmem((4, 4, 2, 32, D), bf16),
            vmem((ROWS, D), bf16),
            vmem((SEQ, ROWS, 512), bf16),
            vmem((ROWS, D), f32),
            vmem((4, 4, 2, 2 * BLOCK, WIDE), bf16),
            vmem((4, 4, 2, BLOCK, WIDE), bf16),
            vmem((SEQ, ROWS, WIDE), bf16),
            vmem((SEQ, ROWS, WIDE), bf16),
            vmem((SEQ, ROWS, HIDDEN), bf16),
            vmem((SEQ, ROWS, HIDDEN), bf16),
            vmem((SEQ, ROWS, HIDDEN), bf16),
            vmem((2 * ROWS, WIDE), f32),
            vmem((SEQ * ROWS, 128), bf16),
            vmem((SEQ * ROWS, 128), bf16),
            vmem((48, HIDDEN), bf16),
            vmem((SEQ * FF_BLOCKS, 16, 128), bf16),
            vmem((3, FF_BLOCKS, 16, 128), bf16),
            vmem((ROWS, D), bf16),
            vmem((2, HALF, D), bf16),
            vmem((2, ROWS, D), bf16),
            vmem((2, ROWS, D), bf16),
        ]
        + [vmem((4, 4, 1, 2, 8, 128), f32)] * 4
        + reduction(3)
        + [
            vmem((SEQ * LATE, 16, 128), bf16),
            vmem((3, LATE, 16, 128), bf16),
            vmem((4, 4, 1, 16, 128), bf16),
        ]
        + reduction(1)
        + [
            dma((4, 11)), dma((4, 11)), dma((3,)), dma((3,)), dma((6,)), dma((6,)),
            dma((12,)), dma((12,)), dma((6,)), dma((6,)), dma((2, 3)), dma((2, 3)), dma((6,)),
            dma((3,)), dma((3,)), dma((3, 10)), dma((3, 10)), dma((2, 3)), dma((2, 3)), dma((2, 11)), dma((2, 11)),
        ],
        collective_id=1,
    )


def tables_kernel(
    early, late, done_out, done_grad,
    qkv_in, q_out, kv_out, o_in, o_out, mlp_in, mlp_out, down_in, down_out, layer_out, input_grad,
):
    def copy(source, start, count, out):
        for i in range(count):
            x, place = divmod(start + i, FF_BLOCKS if source is early else LATE)
            owner, slot = divmod(place, 3 if source is early else 1)
            out[:, i * 128 : (i + 1) * 128] = source[owner // 4, owner % 4, 0, x, slot, 0].astype(f32)

    layer_out[...] = done_out[...]
    input_grad[...] = done_grad[...]
    for i in range(2):
        copy(early, 54 * i, 54, mlp_out.at[0, i])
        copy(early, 162 + 9 * i, 9, mlp_in.at[0, i])
        copy(late, 35 + 2 * i, 2, kv_out.at[0, i])
    copy(early, 108, 54, down_in.at[0])
    copy(early, 180, 9, down_out.at[0])
    for i in range(3):
        copy(late, 9 * i, 9, qkv_in.at[0, i])
    copy(late, 27, 8, q_out.at[0])
    copy(late, 39, 8, o_in.at[0])
    copy(late, 47, 9, o_out.at[0])


def put_tables(early, late, done_out, done_grad):
    shapes = (
        (3, 16, D), (16, 1024), (2, 16, 256), (16, 1024), (16, D),
        (2, 16, D), (2, 16, 6912), (16, 6912), (16, D),
    )

    def one(shape):
        rest = len(shape)
        return pl.BlockSpec((1,) + shape, lambda a, rest=rest: (a,) + (0,) * rest)

    rows = pl.BlockSpec((ROWS // 8, D), lambda a: (a, 0))

    def blocks(slots):
        return pl.BlockSpec(
            (4, 4, 1, SEQ, slots, 1, 16, 128), lambda a: (0, 0, a // 4, 0, 0, a % 4, 0, 0)
        )

    return pl.pallas_call(
        tables_kernel,
        grid=(8,),
        out_shape=[jax.ShapeDtypeStruct((8,) + shape, f32) for shape in shapes]
        + [jax.ShapeDtypeStruct((ROWS, D), bf16)] * 2,
        in_specs=[blocks(3), blocks(1), rows, rows],
        out_specs=[one(shape) for shape in shapes] + [rows, rows],
        compiler_params=pltpu.CompilerParams(vmem_limit_bytes=63 * MIB),
        name="tables",
    )(early, late, done_out, done_grad)


def prepare_kernel(
    arrive, leave, ids, place_x, segments, w_query, w_key, w_value, w_gate, w_up, w_down,
    qkv_adapt_in, q_adapt_out, kv_adapt_out, o_adapt_in, o_adapt_out,
    mlp_adapt_in, mlp_adapt_out, down_adapt_in, down_adapt_out,
    gain_one, gain_two, gain_three, gain_four,
    pack_qkv, pack_gu, pack_down, own_marks, segment_rows, segment_column,
    first_qkv, second_q, second_kv, first_o, second_o, first_gu, second_down, ext_gu, ext_down, gains,
    table, q_held, kv_held, o_held, in_held, out_held, sem,
):
    chosen, me = ids[0], place_x[0]
    mlp_out, down_in = mlp_adapt_out.at[chosen], down_adapt_in.at[chosen]
    moves = [
        (mlp_out.at[0], table.at[0:16]),
        (mlp_out.at[1], table.at[16:32]),
        (down_in, table.at[32:48]),
        (q_adapt_out.at[chosen], q_held),
        (kv_adapt_out.at[chosen], kv_held),
        (o_adapt_in.at[chosen], o_held),
        (o_adapt_out.at[chosen], second_o),
        (mlp_adapt_in.at[chosen], in_held),
        (down_adapt_out.at[chosen], out_held),
        (qkv_adapt_in.at[chosen], first_qkv),
    ]
    moves = [pltpu.make_async_copy(src, dst, sem.at[i]) for i, (src, dst) in enumerate(moves)]
    for moving in moves:
        moving.start()
    iota = lambda shape, axis: lax.broadcasted_iota(jnp.int32, shape, axis)
    ones = lambda where: jnp.where(where, 1.0, 0.0).astype(bf16)

    def placed(count, first):
        return ones(iota((48, count), 0) == iota((48, count), 1) + first)

    table[48:128] = jnp.zeros((80, 6912), bf16)
    arrive()
    rows = dot(placed(32, 0), w_query[...]) + dot(placed(8, 32), w_key[...])
    pack_qkv[...] = (rows + dot(placed(8, 40), w_value[...])).astype(bf16)
    row, unit = iota((BLOCK, 216), 0), iota((BLOCK, 216), 1)
    quarter = ones((unit == me * UNITS + row) & (row < UNITS))
    pack_gu[0:64] = dot(quarter, w_gate[...]).astype(bf16)
    pack_gu[64:128] = dot(quarter, w_up[...]).astype(bf16)
    pack_down[...] = dot(quarter, w_down[...]).astype(bf16)

    for i, gain in enumerate((gain_one, gain_two, gain_three, gain_four)):
        gains[i : i + 1] = gain[...].reshape(1, D)
    leave(0, 1, 2)
    adapter = iota((8, 128), 0)
    for half in (0, 1):
        own_marks[half] = jnp.where((adapter + 4 * half == chosen) & (adapter < 4), 1.0, 0.0)
    for i in range(SEQ):
        segment_rows[i] = segments[:, i * ROWS : (i + 1) * ROWS]
    square = iota((ROWS, ROWS), 0) == iota((ROWS, ROWS), 1)
    segment_column[...] = jnp.sum(jnp.where(square, segment_rows[me], 0), -1, keepdims=True)

    for moving in moves:
        moving.wait()
    second_q[...] = jnp.zeros_like(second_q)
    for h in range(4):
        second_q[h, 0:16] = q_held[:, h * 256 : (h + 1) * 256]
        first_o[h] = o_held[:, h * 256 : (h + 1) * 256]
    second_kv[...] = jnp.zeros_like(second_kv)
    second_kv[16:32, 0:256] = kv_held[0]
    second_kv[32:48, 256:512] = kv_held[1]
    first_gu[0:16] = in_held[0]
    first_gu[16:32] = in_held[1]
    first_gu[32:128] = jnp.zeros((96, D), bf16)
    second_down[0:32] = jnp.zeros((32, D), bf16)
    second_down[32:48] = out_held[...]
    second_down[48:128] = jnp.zeros((80, D), bf16)

    def spread(d, _):
        first = 216 * d + me * UNITS
        start = jnp.minimum(first // 128 * 128, 6912 - 256)
        row = iota((BLOCK, 256), 0)
        picked = ones((first + row == start + iota((BLOCK, 256), 1)) & (row < UNITS))
        held = dot_nt(picked, table[:, pl.ds(pl.multiple_of(start, 128), 256)])
        lane = iota((BLOCK, 128), 1)
        ext_gu[d, 0:64] = jnp.where(lane < 16, held, 0.0).astype(bf16)
        ext_gu[d, 64:128] = jnp.where((lane >= 16) & (lane < 32), held, 0.0).astype(bf16)
        ext_down[d] = jnp.where(lane >= 32, held, 0.0).astype(bf16)
        return 0

    lax.fori_loop(0, 32, spread, 0, unroll=4)


def prepare(*arrays):
    shapes = [
        ((48, D), bf16), ((128, D), bf16), ((64, D), bf16), ((2, 8, 128), f32),
        ((SEQ, 1, ROWS), jnp.int32), ((ROWS, 1), jnp.int32),
        ((3, 16, D), bf16), ((4, 48, 256), bf16), ((48, 512), bf16), ((4, 16, 256), bf16), ((16, D), bf16),
        ((128, D), bf16), ((128, D), bf16), ((32, 2 * BLOCK, 128), bf16), ((32, BLOCK, 128), bf16),
        ((4, D), f32),
    ]
    return staged_call(
        prepare_kernel, "prepare", arrays, "ss" + "v" * 7 + "h" * 9 + "v" * 4,
        [shape + ("v",) for shape in shapes],
        [
            pltpu.VMEM((128, 6912), bf16),
            pltpu.VMEM((16, 1024), bf16),
            pltpu.VMEM((2, 16, 256), bf16),
            pltpu.VMEM((16, 1024), bf16),
            pltpu.VMEM((2, 16, D), bf16),
            pltpu.VMEM((16, D), bf16),
            pltpu.SemaphoreType.DMA((10,)),
        ],
    )


def body(
    layer_input, out_grad, segment_ids, adapter_ids,
    gain_attn_in, gain_attn_out, gain_mlp_in, gain_mlp_out,
    w_query, w_key, w_value, w_out, w_gate, w_up, w_down,
    qkv_adapt_in, q_adapt_out, kv_adapt_out, o_adapt_in, o_adapt_out,
    mlp_adapt_in, mlp_adapt_out, down_adapt_in, down_adapt_out,
):
    me = lax.axis_index("seq").astype(jnp.int32)
    (
        pack_qkv, pack_gu, pack_down, own_marks, segment_rows, segment_column,
        first_qkv, second_q, second_kv, first_o, second_o, first_gu, second_down, ext_gu, ext_down, gains,
    ) = prepare(
        adapter_ids, me.reshape(1), segment_ids, w_query.T, w_key.T, w_value.T, w_gate.T, w_up.T, w_down,
        qkv_adapt_in, q_adapt_out, kv_adapt_out, o_adapt_in, o_adapt_out,
        mlp_adapt_in, mlp_adapt_out, down_adapt_in, down_adapt_out,
        gain_attn_in, gain_attn_out, gain_mlp_in, gain_mlp_out,
    )
    first_qkv = first_qkv.reshape(48, D)
    layer_out, input_grad, all_early, all_late = layer(
        layer_input[0], pack_qkv, w_out, pack_gu, pack_down, segment_rows, segment_column, gains,
        first_qkv, second_q, second_kv, first_o, second_o,
        ext_gu.reshape(4, 4, 2, 2 * BLOCK, 128), ext_down.reshape(4, 4, 2, BLOCK, 128),
        first_gu, second_down, out_grad[0], own_marks,
    )
    *tables, layer_out, input_grad = put_tables(all_early, all_late, layer_out, input_grad)
    return (layer_out[None], input_grad[None], *tables)


def solution(mesh):
    tokens = P("dp", "seq", None)
    columns, rows = P(None, "dp"), P("dp", None)
    placed = (
        (tokens, tokens, P("dp", None), P("dp"))
        + (P(),) * 4
        + (columns, columns, columns, rows, columns, columns, rows)
        + (P(),) * 9
    )
    return jax.shard_map(
        body,
        mesh=mesh,
        in_specs=placed,
        out_specs=(tokens, tokens) + (P(),) * 9,
        check_vma=False,
    )
```

```python
import functools

import jax
import jax.numpy as jnp
from jax import lax
from jax.experimental import pallas as pl
from jax.experimental.pallas import tpu as pltpu
from jax.sharding import PartitionSpec as P

epsilon = 1e-06
softcap = 50.0
MESH = pl.DeviceIdType.MESH
bf16 = jnp.bfloat16
f32 = jnp.float32

D = 1152
SEQ = 4
ROWS = 256
UNITS = 54
BLOCK = 64
TILE = 256
MIB = 1 << 20


def dot(a, b):
    return lax.dot_general(a, b, (((1,), (0,)), ((), ())), preferred_element_type=f32)


def dot_nt(a, b):
    return lax.dot_general(a, b, (((1,), (1,)), ((), ())), preferred_element_type=f32)


def dot_tn(a, b):
    return lax.dot_general(a, b, (((0,), (0,)), ((), ())), preferred_element_type=f32)


def normed(values, gain_vector):
    return values * lax.rsqrt(jnp.mean(values * values, -1, keepdims=True) + epsilon) * gain_vector


def norm_back(values, gain_vector, cotangent):
    inverse = lax.rsqrt(jnp.mean(values * values, -1, keepdims=True) + epsilon)
    scaled = cotangent * gain_vector
    mean_part = jnp.mean(scaled * values, -1, keepdims=True)
    return inverse * (scaled - values * (inverse * inverse * mean_part))


def seq_peers():
    dp, me = lax.axis_index("dp"), lax.axis_index("seq")
    return [(dp, lax.rem(me + shift, SEQ)) for shift in (1, 2, 3)]


def greet(peers):
    barrier = pltpu.get_barrier_semaphore()
    for peer in peers:
        pl.semaphore_signal(barrier, inc=1, device_id=peer, device_id_type=MESH)
    pl.semaphore_wait(barrier, len(peers))


def staged_call(kernel, name, operands, kinds, results, scratch, collective_id=None):
    count, made = len(operands), len(results)
    held = [i for i in range(count) if kinds[i] == "v"]
    given = [i for i in range(made) if results[i][2] == "v"]

    def body(*refs):
        outer = list(refs[: count + made])
        inner = list(outer)
        rest = refs[count + made :]
        for n, i in enumerate(held):
            inner[i] = rest[n]
        for n, i in enumerate(given):
            inner[count + i] = rest[len(held) + n]
        sems, rest = rest[len(held) + len(given)], rest[len(held) + len(given) + 1 :]
        ins = {i: pltpu.make_async_copy(outer[i], inner[i], sems.at[n]) for n, i in enumerate(held)}
        outs = {
            i: pltpu.make_async_copy(inner[count + i], outer[count + i], sems.at[len(held) + n])
            for n, i in enumerate(given)
        }
        waiting, leaving = set(ins), []
        for moving in ins.values():
            moving.start()

        def arrive(*which):
            for i in which or sorted(waiting):
                if i in waiting:
                    waiting.discard(i)
                    ins[i].wait()

        def leave(*which):
            for i in which:
                outs[i].start()
                leaving.append(i)

        kernel(arrive, leave, *inner, *rest)
        leave(*[i for i in given if i not in leaving])
        for i in given:
            outs[i].wait()

    spaces = {"v": pl.ANY, "h": pl.ANY, "s": pltpu.SMEM}
    params = dict(vmem_limit_bytes=63 * MIB)
    if collective_id is not None:
        params.update(collective_id=collective_id, has_side_effects=True)
    return pl.pallas_call(
        body,
        out_shape=[jax.ShapeDtypeStruct(shape, dtype) for shape, dtype, _ in results],
        in_specs=[pl.BlockSpec(memory_space=spaces[k]) for k in kinds],
        out_specs=[pl.BlockSpec(memory_space=pl.ANY)] * made,
        scratch_shapes=[pltpu.VMEM(operands[i].shape, operands[i].dtype) for i in held]
        + [pltpu.VMEM(results[i][0], results[i][1]) for i in given]
        + [pltpu.SemaphoreType.DMA((len(held) + len(given),))]
        + scratch,
        compiler_params=pltpu.CompilerParams(**params),
        name=name,
    )(*operands)


def place():
    dp = lax.axis_index("dp")
    return lax.axis_index("seq"), dp // 8, lax.rem(dp // 2, 4), lax.rem(dp, 2)


def at(x, y, z, core):
    return ((lax.rem(y, 4) * 4 + lax.rem(z, 4)) * 2 + core, lax.rem(x, 4))


def plane_peers():
    x, y, z, core = place()
    return [at(x, y + k, z, core) for k in (1, 2, 3)] + [at(x, y, z + k, core) for k in (1, 2, 3)]


def far_siblings():
    x, y, z, core = place()
    return [at(x, y, z + k, 1 - core) for k in (1, 2, 3)]


def sibling():
    x, y, z, core = place()
    return at(x, y, z, 1 - core)


def remote(src, dst, send_sem, recv_sem, peer):
    return pltpu.make_async_remote_copy(
        src_ref=src, dst_ref=dst, send_sem=send_sem, recv_sem=recv_sem,
        device_id=peer, device_id_type=MESH,
    )


class PlaneGather:
    def __init__(self, own, buffer, send_sem, recv_sem, direct=False):
        self.x, self.y, self.z, self.core = place()
        self.own, self.buffer, self.send, self.recv = own, buffer, send_sem, recv_sem
        self.direct = direct

    def _copy(self, src, dst, slot, peer):
        return remote(src, dst, self.send.at[slot], self.recv.at[slot], peer)

    def _first(self, k):
        x, y, z, core = self.x, self.y, self.z, self.core
        peer = at(x, y + k * (1 - core), z + k * core, core)
        return self._copy(self.own, self.buffer.at[y, z, core], k - 1, peer)

    def _line(self, core, back):
        if core == 0:
            return self.buffer.at[:, lax.rem(self.z + 4 - back, 4), 0]
        return self.buffer.at[lax.rem(self.y + 4 - back, 4), :, 1]

    def _second(self, core, k):
        line = self._line(core, 0)
        peer = at(self.x, self.y + k * core, self.z + k * (1 - core), core)
        return self._copy(line, line, 2 + k, peer)

    def _pass(self, core, half):
        back, k = ((1, 1), (3, 3))[half]
        line = self._line(core, back).at[2 * half : 2 * half + 2]
        peer = at(self.x, self.y + k * core, self.z + k * (1 - core), core)
        return self._copy(line, line, (4, 10)[half], peer)

    def _swap(self, core, back):
        line = self._line(core, back)
        return self._copy(line, line, 6 + back, at(self.x, self.y, self.z, 1 - core))

    def _both(self, act):
        for core in (0, 1):
            pl.when(self.core == core)(functools.partial(act, core))

    def start(self):
        for k in (2, 1, 3):
            self._first(k).start()

    def middle(self):
        for k in (1, 3, 2):
            self._first(k).wait()

        def act(core):
            for k in (2, 1, 3) if self.direct else (1, 3):
                self._second(core, k).start()
            self._swap(core, 0).start()

        self._both(act)

    def late(self):
        def act(core):
            for half, k in ((0, 1), (1, 3)):
                self._second(core, k).wait()
                if not self.direct:
                    self._pass(core, half).start()
                self._swap(core, k).start()

        self._both(act)

    def last(self):
        def act(core):
            if self.direct:
                self._second(core, 2).wait()
            else:
                for half in (0, 1):
                    self._pass(core, half).wait()
            self._swap(core, 2).start()

        self._both(act)

    def finish(self):
        def act(core):
            for back in (0, 1, 3, 2):
                self._swap(core, back).wait()

        self._both(act)


class LineSum:
    def __init__(self, parts, landed, send_sem, recv_sem):
        self.me, self.peers = lax.axis_index("seq"), seq_peers()
        self.parts, self.landed, self.send, self.recv = parts, landed, send_sem, recv_sem

    def _copy(self, shift):
        return remote(
            self.parts.at[lax.rem(self.me + shift, SEQ)], self.landed.at[shift - 1],
            self.send.at[shift - 1], self.recv.at[shift - 1], self.peers[shift - 1],
        )

    def start(self):
        for shift in (2, 1, 3):
            self._copy(shift).start()

    def finish(self):
        for shift in (1, 3, 2):
            self._copy(shift).wait()


class PlaneExchange:
    def __init__(self, first, second, third, fourth, send_sem, recv_sem):
        self.x, self.y, self.z, self.core = place()
        self.first, self.second, self.third, self.fourth = first, second, third, fourth
        self.send, self.recv = send_sem, recv_sem

    def _copy(self, src, dst, slot, peer):
        return remote(src, dst, self.send.at[slot], self.recv.at[slot], peer)

    def _along_y(self, k):
        y = lax.rem(self.y + k, 4)
        return self._copy(self.first.at[y], self.second.at[k], k - 1, at(self.x, y, self.z, self.core))

    def _along_z(self, k):
        z = lax.rem(self.z + k, 4)
        return self._copy(self.second.at[:, z], self.third.at[k], 2 + k, at(self.x, self.y, z, self.core))

    def _other(self, k):
        z = lax.rem(self.z + k, 4)
        return self._copy(self.second.at[:, z], self.fourth.at[k], 6 + k, at(self.x, self.y, z, 1 - self.core))

    def start(self):
        for k in (2, 1, 3):
            self._along_y(k).start()
        self.second[0] = self.first[self.y]

    def middle(self):
        for k in (1, 3, 2):
            self._along_y(k).wait()
        for k in (2, 1, 3):
            self._along_z(k).start()
        for k in (2, 1, 3, 0):
            self._other(k).start()
        self.third[0] = self.second[:, self.z]

    def late(self):
        for k in (1, 3, 2):
            self._along_z(k).wait()
        for k in (0, 1, 3, 2):
            self._other(k).wait()

    def total(self, marks, out):
        slots = self.first.shape[2]
        out[...] = jnp.zeros_like(out)

        def add(i, _):
            kz, ky = i // 4, lax.rem(i, 4)
            for held, known in ((self.third, marks.third), (self.fourth, marks.fourth)):
                weights = known[kz, ky, 0, self.core]
                for slot in range(slots):
                    rows = held[kz, ky, slot].astype(f32)
                    for a in range(4):
                        out[slot, a] += weights[a : a + 1] * rows
            return 0

        lax.fori_loop(0, 16, add, 0)


class LineGather:
    def __init__(self, buffer, send_sem, recv_sem):
        self.me, self.peers = lax.axis_index("seq"), seq_peers()
        self.buffer, self.send, self.recv = buffer, send_sem, recv_sem

    def _copy(self, shift):
        mine = self.buffer.at[self.me]
        return remote(mine, mine, self.send.at[shift - 1], self.recv.at[shift - 1], self.peers[shift - 1])

    def start(self):
        for shift in (2, 1, 3):
            self._copy(shift).start()

    def finish(self):
        for shift in (1, 3, 2):
            self._copy(shift).wait()


WIDE = D + 128
HIDDEN = 32 * BLOCK
HALF = ROWS // 2
ROOT = 0.7978845608028654
CUBE = ROOT * 0.044715
FF_BLOCKS = 48
LATE = 14
SCORE = 1.0 / 16.0


def allowed_pairs(segment_rows, segment_column, me, chunk):
    keys = lax.broadcasted_iota(jnp.int32, (ROWS, ROWS), 1) + chunk * ROWS
    queries = lax.broadcasted_iota(jnp.int32, (ROWS, ROWS), 0) + me * ROWS
    return (segment_column[...] == segment_rows[chunk]) & (keys <= queries)


def layer_kernel(
    arrive, leave,
    layer_input, pack_qkv, pack_o, pack_gu, pack_down, segment_rows, segment_column, gains,
    first_qkv, second_q, second_kv, first_o, second_o,
    ext_gu, ext_down, first_gu, second_down, out_grad, own_marks,
    layer_out, input_grad, all_early, all_late,
    queries, totals, context, attn_proj, qkv_latent, o_latent, mixed_grad, early_sum,
    got_qkv, got_o, first_norm, kv_all, mixed,
    w_gu, w_down, inputs, down_grads, hidden, act_gate, act_up, total,
    down_latents, gu_grads, packed, early, early_landed,
    far, landed_half, near, landed,
    m1, m2, m3, m4, e2, e3, e4, early_total, early_line,
    late, late_landed, late_sum, l2, l3, l4, late_total, late_line,
    sem_s, sem_r, kv_s, kv_r, tok_s, tok_r, rs_s, rs_r, ag_s, ag_r, line_s, line_r, loc,
    back_s, back_r, plane_s, plane_r, spread_s, spread_r, out_s, out_r,
):
    me, y, z, core = place()
    line = seq_peers()
    ahead, _, behind = line
    greet(line + plane_peers() + far_siblings() + [sibling()])

    all_gu, all_down = w_gu.at[:, :, :, :, 0:D], w_down.at[:, :, :, :, 0:D]
    gathers = [
        PlaneGather(own, got, sem_s.at[i], sem_r.at[i], direct=i < 2)
        for i, (own, got) in enumerate(
            ((pack_qkv, got_qkv), (pack_o, got_o), (pack_gu, all_gu), (pack_down, all_down))
        )
    ]
    g_qkv, g_o, g_gu, g_down = gathers
    own_copies = [
        pltpu.make_async_copy(g.own, g.buffer.at[y, z, core], loc.at[i]) for i, g in enumerate(gathers)
    ]
    ext_copies = [
        pltpu.make_async_copy(ext_gu, w_gu.at[:, :, :, :, D:WIDE], loc.at[4]),
        pltpu.make_async_copy(ext_down, w_down.at[:, :, :, :, D:WIDE], loc.at[5]),
    ]
    arrive(1)
    g_qkv.start()
    own_copies[0].start()
    arrive()
    for moving in own_copies[1:] + ext_copies:
        moving.start()
    gain_first, gain_second, gain_third, gain_fourth = [gains[i : i + 1] for i in range(4)]
    first_norm[...] = normed(layer_input[...].astype(f32), gain_first).astype(bf16)
    latent = dot_nt(first_norm[...], first_qkv[...]).astype(bf16)
    qkv_latent[...] = latent
    for moving in own_copies:
        moving.wait()
    g_qkv.middle()
    g_o.start()
    g_qkv.late()
    g_gu.start()
    g_down.start()
    g_qkv.last()
    g_o.middle()
    g_qkv.finish()

    def unmix(i, _):
        pairs = got_qkv[i, :, :, 32:48].astype(f32).reshape(8, 2, 8, D)
        got_qkv[i, 0:2, :, 32:48] = pairs[:, 0].reshape(2, 2, 16, D).astype(bf16)
        got_qkv[i, 2:4, :, 32:48] = pairs[:, 1].reshape(2, 2, 16, D).astype(bf16)
        return 0

    lax.fori_loop(0, 4, unmix, 0)
    key_rows = lambda: got_qkv[:, 0:2, :, 32:48].reshape(256, D)
    value_rows = lambda: got_qkv[:, 2:4, :, 32:48].reshape(256, D)
    kv_low = dot(latent, second_kv[...])
    kv_all[me, :, 0:256] = (dot_nt(first_norm[...], key_rows()) + kv_low[:, 0:256]).astype(bf16)
    kv_all[me, :, 256:512] = (dot_nt(first_norm[...], value_rows()) + kv_low[:, 256:512]).astype(bf16)

    def kv_copy(shift):
        return remote(kv_all.at[me], kv_all.at[me], kv_s.at[shift - 1], kv_r.at[shift - 1], line[shift - 1])

    for shift in (1, 2, 3):
        pl.when(me + shift < SEQ)(lambda shift=shift: kv_copy(shift).start())

    def query(h, _):
        rows = got_qkv[h, :, :, 0:32].reshape(256, D)
        queries[h] = (dot_nt(first_norm[...], rows) + dot(latent, second_q[h])).astype(bf16)
        context[h] = jnp.zeros((ROWS, 256), f32)
        return 0

    lax.fori_loop(0, 4, query, 0)
    totals[...] = jnp.zeros_like(totals)
    head_lane = lax.broadcasted_iota(jnp.int32, (ROWS, 128), 1)

    def total_of(h):
        return jnp.sum(jnp.where(head_lane == h, totals[...], 0.0), -1, keepdims=True)

    g_gu.middle()
    g_down.middle()

    def attend(chunk):
        keys, held = kv_all[chunk, :, 0:256], kv_all[chunk, :, 256:512]
        allowed = allowed_pairs(segment_rows, segment_column, me, chunk)

        def head(h, _):
            bent = jnp.tanh(dot_nt(queries[h], keys) * (SCORE / softcap))
            weight = jnp.where(allowed, jnp.exp(softcap * bent), 0.0).astype(bf16)
            totals[...] += jnp.where(head_lane == h, jnp.sum(weight.astype(f32), -1, keepdims=True), 0.0)
            context[h] += dot(weight, held)
            return 0

        lax.fori_loop(0, 4, head, 0)

    attend(me)
    g_o.late()
    g_o.last()
    for shift in (1, 2, 3):
        def arrived(shift=shift):
            kv_copy(shift).wait_recv()
            attend(me - shift)

        pl.when(me >= shift)(arrived)

    g_o.finish()
    proj = jnp.zeros((ROWS, D), f32)
    thin = jnp.zeros((ROWS, 16), f32)
    for h in range(4):
        context[h] = context[h] / total_of(h)
        low = context[h].astype(bf16)
        proj = proj + dot(low, got_o[h].reshape(256, D))
        thin = thin + dot_nt(low, first_o[h])
    o_latent[...] = thin.astype(bf16)
    proj = proj + dot(o_latent[...], second_o[...])
    attn_proj[...] = proj
    mid = layer_input[...].astype(f32) + normed(proj, gain_second)
    mixed[...] = mid
    inputs[0, :, 0:D] = normed(mid, gain_third).astype(bf16)

    low, high = slice(0, HALF), slice(HALF, ROWS)

    def passing(buffer, send, recv):
        def move(from_slot, to_slot, rows, index, peer):
            src, dst = buffer.at[from_slot, rows, 0:D], buffer.at[to_slot, rows, 0:D]
            return remote(src, dst, send.at[index], recv.at[index], peer)

        return [
            move(0, 2, low, 0, ahead), move(0, 1, high, 1, behind),
            move(0, 2, high, 2, ahead), move(0, 1, low, 3, behind),
            move(2, 3, low, 4, ahead), move(1, 3, high, 5, behind),
        ]

    token_moves = passing(inputs, tok_s, tok_r)
    for i in range(4):
        token_moves[i].start()
    g_gu.late()
    for i in range(4):
        for k in range(4):
            m1[i, k, 0] = own_marks[...]
    m_plane = PlaneExchange(m1, m2, m3, m4, plane_s.at[2], plane_r.at[2])
    g_down.late()
    g_gu.last()
    token_moves[0].wait()
    token_moves[4].start()
    token_moves[1].wait()
    token_moves[5].start()
    for moving in ext_copies:
        moving.wait()
    g_gu.finish()

    def gate_rows(j):
        return w_gu[j // 2, pl.ds(2 * lax.rem(j, 2), 2), :, 0:64].reshape(TILE, WIDE)

    def up_rows(j):
        return w_gu[j // 2, pl.ds(2 * lax.rem(j, 2), 2), :, 64:128].reshape(TILE, WIDE)

    def down_rows(j):
        return w_down[j // 2, pl.ds(2 * lax.rem(j, 2), 2)].reshape(TILE, WIDE)

    def lanes(j, size=TILE):
        return pl.ds(pl.multiple_of(j * size, size), size)

    def forward_open(slot, many):
        size = many * ROWS
        part = slice(slot, slot + many)
        inputs[part, :, D:WIDE] = (
            dot_nt(inputs[part, :, 0:D].reshape(size, D), first_gu[...]).astype(bf16).reshape(many, ROWS, 128)
        )

        def step(j, _):
            rows = inputs[part].reshape(size, WIDE)
            gate = dot_nt(rows, gate_rows(j))
            upward = dot_nt(rows, up_rows(j))
            square = gate * gate
            bent = jnp.tanh(gate * (ROOT + CUBE * square))
            half = 0.5 * bent + 0.5
            gelu = gate * half
            slope = half + gelu * ((1.0 - bent) * (ROOT + 3.0 * CUBE * square))
            shape = (many, ROWS, TILE)
            hidden[part, :, lanes(j)] = (gelu * upward).astype(bf16).reshape(shape)
            act_gate[part, :, lanes(j)] = gelu.astype(bf16).reshape(shape)
            act_up[part, :, lanes(j)] = (upward * slope).astype(bf16).reshape(shape)
            return 0

        lax.fori_loop(0, 8, step, 0, unroll=4)

    def forward_close(slot, many):
        size = many * ROWS
        part = slice(slot, slot + many)

        def close(n, _):
            rows = hidden[part].reshape(size, HIDDEN)
            total[0:size, lanes(n)] = dot(rows, w_down[:, :, :, :, lanes(n)].reshape(HIDDEN, TILE))
            return 0

        lax.fori_loop(0, 5, close, 0)
        down_latent = total[0:size, D:WIDE].astype(bf16)
        down_latents[slot * ROWS : slot * ROWS + size] = down_latent
        total[0:size, 0:D] += dot(down_latent, second_down[...])

    def backward_open(slot, many):
        size = many * ROWS
        part = slice(slot, slot + many)
        latent_grad = dot_nt(down_grads[part, :, 0:D].reshape(size, D), second_down[...])
        down_grads[part, :, D:WIDE] = latent_grad.astype(bf16).reshape(many, ROWS, 128)

        def step(j, _):
            shape = (many, ROWS, TILE)
            hidden_grad = dot_nt(down_grads[part].reshape(size, WIDE), down_rows(j)).reshape(shape)
            gate_grad = (hidden_grad * act_up[part, :, lanes(j)].astype(f32)).astype(bf16)
            up_grad = (hidden_grad * act_gate[part, :, lanes(j)].astype(f32)).astype(bf16)
            act_up[part, :, lanes(j)] = gate_grad
            act_gate[part, :, lanes(j)] = up_grad
            return 0

        lax.fori_loop(0, 8, step, 0, unroll=4)

    def backward_close(slot, many):
        size = many * ROWS
        part = slice(slot, slot + many)

        def close(n, _):
            total[0:size, lanes(n)] = dot(
                act_up[part].reshape(size, HIDDEN), w_gu[:, :, :, 0:64, lanes(n)].reshape(HIDDEN, TILE)
            ) + dot(
                act_gate[part].reshape(size, HIDDEN), w_gu[:, :, :, 64:128, lanes(n)].reshape(HIDDEN, TILE)
            )
            return 0

        lax.fori_loop(0, 5, close, 0)
        gu_grad = total[0:size, D:WIDE].astype(bf16)
        gu_grads[slot * ROWS : slot * ROWS + size] = gu_grad
        total[0:size, 0:D] += dot(gu_grad, first_gu[...])

    def factors():
        latent = inputs[:, :, D:WIDE].reshape(SEQ * ROWS, 128)[:, 0:32]
        latent_grad = down_grads[:, :, D:WIDE].reshape(SEQ * ROWS, 128)[:, 32:48]

        def piece(j, _):
            gate_part = dot_tn(latent, act_up[:, :, lanes(j)].reshape(SEQ * ROWS, TILE))
            up_part = dot_tn(latent, act_gate[:, :, lanes(j)].reshape(SEQ * ROWS, TILE))
            down_part = dot_tn(latent_grad, hidden[:, :, lanes(j)].reshape(SEQ * ROWS, TILE))
            packed[0:16, lanes(j)] = gate_part[0:16].astype(bf16)
            packed[16:32, lanes(j)] = up_part[16:32].astype(bf16)
            packed[32:48, lanes(j)] = down_part.astype(bf16)
            return 0

        lax.fori_loop(0, 8, piece, 0, unroll=2)

    def scatter(base, finish, others, own=None):
        finish(3, 1)
        far[...] = total[0:ROWS, 0:D].astype(bf16)
        far_moves = [
            remote(far.at[low], landed_half.at[0], rs_s.at[base + 4], rs_r.at[base + 4], behind),
            remote(far.at[high], landed_half.at[1], rs_s.at[base + 5], rs_r.at[base + 5], ahead),
        ]
        for moving in far_moves:
            moving.start()
        finish(1, 2)
        near_moves = [
            remote(near.at[0, low], landed.at[0, low], rs_s.at[base], rs_r.at[base], ahead),
            remote(near.at[0, high], landed.at[0, high], rs_s.at[base + 1], rs_r.at[base + 1], ahead),
            remote(near.at[1, high], landed.at[1, high], rs_s.at[base + 2], rs_r.at[base + 2], behind),
            remote(near.at[1, low], landed.at[1, low], rs_s.at[base + 3], rs_r.at[base + 3], behind),
        ]
        near[0, low] = total[0:HALF, 0:D].astype(bf16)
        near_moves[0].start()
        near[1, high] = total[ROWS + HALF : 2 * ROWS, 0:D].astype(bf16)
        near_moves[2].start()
        near[0, high] = total[HALF:ROWS, 0:D].astype(bf16)
        near[1, low] = total[ROWS : ROWS + HALF, 0:D].astype(bf16)
        if own is not None:
            own()
        far_moves[1].wait()
        near[0, high] = (near[0, high].astype(f32) + landed_half[1].astype(f32)).astype(bf16)
        near_moves[1].start()
        far_moves[0].wait()
        near[1, low] = (near[1, low].astype(f32) + landed_half[0].astype(f32)).astype(bf16)
        near_moves[3].start()
        others()
        for moving in near_moves:
            moving.wait()

    def forward_own():
        forward_close(0, 1)
        mixed_grad[...] = total[0:ROWS, 0:D]

    m_plane.start()
    forward_open(0, 1)
    g_down.last()
    token_moves[2].wait()
    token_moves[3].wait()
    forward_open(1, 2)
    token_moves[4].wait()
    token_moves[5].wait()
    forward_open(3, 1)
    g_down.finish()
    scatter(0, forward_close, forward_own)
    m_plane.middle()
    down_proj = mixed_grad[...] + landed[0].astype(f32) + landed[1].astype(f32)
    layer_out[...] = (mixed[...] + normed(down_proj, gain_fourth)).astype(bf16)
    leave(0)
    down_grads[0, :, 0:D] = norm_back(down_proj, gain_fourth, out_grad[...].astype(f32)).astype(bf16)
    grad_moves = passing(down_grads, ag_s, ag_r)
    for i in range(4):
        grad_moves[i].start()

    early_parts = early.reshape(SEQ, FF_BLOCKS, 16, 128)
    e_line = LineSum(early_parts, early_landed, line_s.at[0], line_r.at[0])

    def unpad(j, _):
        start = jnp.minimum((j * 128 // 216) // 2 * 128, HIDDEN // 2 - 256)
        lane = start + lax.broadcasted_iota(jnp.int32, (256, 128), 0)
        within = lane & 63
        unit = (lane >> 6) * 216 + me * UNITS + within
        goal = j * 128 + lax.broadcasted_iota(jnp.int32, (256, 128), 1)
        chosen = jnp.where((unit == goal) & (within < UNITS), 1.0, 0.0).astype(bf16)
        for half in (0, 1):
            rows = packed[:, pl.ds(pl.multiple_of(start + half * HIDDEN // 2, 128), 256)]
            moved = dot(rows, chosen).astype(bf16)
            for i in range(3):
                early[54 * i + 27 * half + j] = moved[16 * i : 16 * i + 16]
        return 0

    def put(start, rows, buffer):
        for i in range(rows.shape[1] // 128):
            buffer[start + i] = rows[:, i * 128 : (i + 1) * 128].astype(bf16)

    def spread_factors():
        lax.fori_loop(0, 27, unpad, 0, unroll=3)
        all_gu_grads = gu_grads[...]
        gu_part = dot_tn(all_gu_grads[:, 0:32], inputs[:, :, 0:D].reshape(SEQ * ROWS, D))
        put(162, gu_part[0:16], early)
        put(171, gu_part[16:32], early)
        put(180, dot_tn(down_latents[:, 32:48], down_grads[:, :, 0:D].reshape(SEQ * ROWS, D)), early)
        for i in range(189, 192):
            early[i] = jnp.zeros((16, 128), bf16)
        e_line.start()

    backward_open(0, 1)
    backward_close(0, 1)
    mixed_grad[...] = total[0:ROWS, 0:D]
    m_plane.late()
    grad_moves[0].wait()
    grad_moves[4].start()
    grad_moves[1].wait()
    grad_moves[5].start()
    grad_moves[2].wait()
    grad_moves[3].wait()
    backward_open(1, 2)
    grad_moves[4].wait()
    grad_moves[5].wait()
    backward_open(3, 1)

    def all_factors():
        factors()
        spread_factors()

    scatter(6, backward_close, all_factors)
    own_sum = mixed_grad[...] + landed[0].astype(f32) + landed[1].astype(f32)
    mixed_grad[...] = out_grad[...].astype(f32) + norm_back(mixed[...], gain_third, own_sum)

    head_grads = [down_grads.at[3, :, 256 * h : 256 * h + 256] for h in range(4)]
    key_part, value_part = total.at[0:ROWS, 512:768], total.at[0:ROWS, 768:1024]
    kv_own = total.at[ROWS : 2 * ROWS, 512:1024]

    def query_part(h):
        row, lane = h // 2, lax.rem(h, 2)
        return total.at[pl.ds(pl.multiple_of(row * ROWS, ROWS), ROWS), pl.ds(pl.multiple_of(lane * 256, 256), 256)]

    def head_grad(h):
        return down_grads[3, :, pl.ds(pl.multiple_of(h * 256, 256), 256)]

    far[...] = norm_back(attn_proj[...], gain_second, mixed_grad[...]).astype(bf16)
    o_grad = dot_nt(far[...], second_o[...]).astype(bf16)

    for h in range(4):
        low = (dot_nt(far[...], got_o[h].reshape(256, D)) + dot(o_grad, first_o[h])).astype(bf16)
        head_grads[h][...] = low
        query_part(h)[...] = jnp.zeros((ROWS, 256), f32)

    def attend_back(chunk):
        keys, held = kv_all[chunk, :, 0:256], kv_all[chunk, :, 256:512]
        allowed = allowed_pairs(segment_rows, segment_column, me, chunk)
        key_part[...] = jnp.zeros_like(key_part)
        value_part[...] = jnp.zeros_like(value_part)

        def head(h, _):
            bent = jnp.tanh(dot_nt(queries[h], keys) * (SCORE / softcap))
            weight = jnp.where(allowed, jnp.exp(softcap * bent), 0.0).astype(bf16).astype(f32)
            probs = weight / total_of(h)
            grads = head_grad(h)
            centre = jnp.sum(grads.astype(f32) * context[h], -1, keepdims=True)
            prob_grad = dot_nt(grads, held)
            raw_grad = (probs * (prob_grad - centre) * ((1.0 - bent * bent) * SCORE)).astype(bf16)
            query_part(h)[...] += dot(raw_grad, keys)
            key_part[...] += dot_tn(raw_grad, queries[h])
            value_part[...] += dot_tn(probs.astype(bf16), grads)
            return 0

        lax.fori_loop(0, 4, head, 0)

    def back_copy(shift):
        peer = line[3 - shift]
        return remote(w_down.at[shift - 1, 2:4, :, :, 0:512], w_down.at[shift - 1, 0:2, :, :, 0:512], back_s.at[shift - 1], back_r.at[shift - 1], peer)

    for shift in (3, 2, 1):
        def earlier(shift=shift):
            attend_back(me - shift)
            w_down[shift - 1, 2:4, :, :, 0:256] = key_part[...].astype(bf16).reshape(2, 2, BLOCK, 256)
            w_down[shift - 1, 2:4, :, :, 256:512] = value_part[...].astype(bf16).reshape(2, 2, BLOCK, 256)
            back_copy(shift).start()

        pl.when(me >= shift)(earlier)

    e_line.finish()

    def add_early(i, _):
        for k in range(3):
            own = early_parts[me, 3 * i + k].astype(f32)
            for s in range(3):
                own = own + early_landed[s, 3 * i + k].astype(f32)
            early_sum[i // 4, lax.rem(i, 4), k] = own.astype(bf16)
        return 0

    lax.fori_loop(0, 16, add_early, 0)
    e_plane = PlaneExchange(early_sum, e2, e3, e4, plane_s.at[0], plane_r.at[0])
    e_plane.start()

    attend_back(me)
    for h in range(4):
        put(39 + 2 * h, dot_tn(o_grad, context[h].astype(bf16)), late)
    put(47, dot_tn(o_latent[...], far[...]), late)
    kv_own[:, 0:256] = key_part[...]
    kv_own[:, 256:512] = value_part[...]

    e_plane.middle()
    e_plane.late()
    e_plane.total(m_plane, early_total)
    early_line[me] = early_total[...].astype(bf16)
    e_spread = LineGather(early_line, spread_s.at[0], spread_r.at[0])
    e_spread.start()
    for shift in (1, 2, 3):
        def collect(shift=shift):
            back_copy(shift).wait_recv()
            kv_own[...] += w_down[shift - 1, 0:2, :, :, 0:512].reshape(ROWS, 512).astype(f32)

        pl.when(me + shift < SEQ)(collect)

    key_value = kv_own[...].astype(bf16)
    thin = dot_nt(key_value, second_kv[...])
    back = dot(key_value[:, 0:256], key_rows()) + dot(key_value[:, 256:512], value_rows())
    for h in range(4):
        low = query_part(h)[...].astype(bf16)
        back = back + dot(low, got_qkv[h, :, :, 0:32].reshape(256, D))
        thin = thin + dot_nt(low, second_q[h])
        put(27 + 2 * h, dot_tn(qkv_latent[...], low)[0:16], late)
    qkv_grad = thin.astype(bf16)
    back = back + dot(qkv_grad, first_qkv[...])
    in_grad = dot_tn(qkv_grad, first_norm[...])
    for i in range(3):
        put(9 * i, in_grad[16 * i : 16 * i + 16], late)
    kv_out_grad = dot_tn(qkv_latent[...], key_value)
    put(35, kv_out_grad[16:32, 0:256], late)
    put(37, kv_out_grad[32:48, 256:512], late)
    late_parts = late.reshape(SEQ, LATE, 16, 128)
    l_line = LineSum(late_parts, late_landed, line_s.at[1], line_r.at[1])
    l_line.start()
    e_spread.finish()
    own_early = pltpu.make_async_copy(early_line, all_early.at[y, z, core], loc.at[0])
    own_early.start()
    e_out = PlaneGather(early_line, all_early, out_s.at[0], out_r.at[0])
    e_out.start()
    near[0] = (mixed_grad[...] + norm_back(layer_input[...].astype(f32), gain_first, back)).astype(bf16)
    result = pltpu.make_async_copy(near.at[0], input_grad, loc.at[2])
    result.start()

    l_line.finish()
    for i in range(16):
        low = jnp.zeros((16, 128), bf16)
        if i < LATE:
            own = late_parts[me, i].astype(f32)
            for s in range(3):
                own = own + late_landed[s, i].astype(f32)
            low = own.astype(bf16)
        late_sum[i // 4, i % 4, 0] = low
    l_plane = PlaneExchange(late_sum, l2, l3, l4, plane_s.at[1], plane_r.at[1])
    l_plane.start()
    own_early.wait()
    e_out.middle()
    l_plane.middle()
    l_plane.late()
    l_plane.total(m_plane, late_total)
    late_line[me] = late_total[...].astype(bf16)
    l_spread = LineGather(late_line, spread_s.at[1], spread_r.at[1])
    l_spread.start()
    e_out.late()
    l_spread.finish()
    own_late = pltpu.make_async_copy(late_line, all_late.at[y, z, core], loc.at[1])
    own_late.start()
    l_out = PlaneGather(late_line, all_late, out_s.at[1], out_r.at[1], direct=True)
    l_out.start()
    own_late.wait()
    l_out.middle()
    e_out.last()
    l_out.late()
    e_out.finish()
    l_out.last()
    l_out.finish()
    result.wait()
    for shift in (1, 2, 3):
        pl.when(me >= shift)(lambda shift=shift: back_copy(shift).wait_send())
    for shift in (1, 2, 3):
        pl.when(me + shift < SEQ)(lambda shift=shift: kv_copy(shift).wait_send())


def layer(*arrays):
    dma = pltpu.SemaphoreType.DMA
    vmem = pltpu.VMEM

    def reduction(slots):
        whole = vmem((4, 4, slots, 16, 128), bf16)
        return [
            whole, whole, whole,
            vmem((slots, 4, 16, 128), f32),
            vmem((SEQ, slots, 4, 16, 128), bf16),
        ]

    return staged_call(
        layer_kernel, "layer", arrays, "v" * 13 + "hhvvvv",
        [
            ((ROWS, D), bf16, "v"),
            ((ROWS, D), bf16, "h"),
            ((4, 4, 2, SEQ, 3, 4, 16, 128), bf16, "h"),
            ((4, 4, 2, SEQ, 1, 4, 16, 128), bf16, "h"),
        ],
        [
            vmem((4, ROWS, 256), bf16),
            vmem((ROWS, 128), f32),
            vmem((4, ROWS, 256), f32),
            vmem((ROWS, D), f32),
            vmem((ROWS, 48), bf16),
            vmem((ROWS, 16), bf16),
            vmem((ROWS, D), f32),
            vmem((4, 4, 3, 16, 128), bf16),
            vmem((4, 4, 2, 48, D), bf16),
            vmem((4, 4, 2, 32, D), bf16),
            vmem((ROWS, D), bf16),
            vmem((SEQ, ROWS, 512), bf16),
            vmem((ROWS, D), f32),
            vmem((4, 4, 2, 2 * BLOCK, WIDE), bf16),
            vmem((4, 4, 2, BLOCK, WIDE), bf16),
            vmem((SEQ, ROWS, WIDE), bf16),
            vmem((SEQ, ROWS, WIDE), bf16),
            vmem((SEQ, ROWS, HIDDEN), bf16),
            vmem((SEQ, ROWS, HIDDEN), bf16),
            vmem((SEQ, ROWS, HIDDEN), bf16),
            vmem((2 * ROWS, WIDE), f32),
            vmem((SEQ * ROWS, 128), bf16),
            vmem((SEQ * ROWS, 128), bf16),
            vmem((48, HIDDEN), bf16),
            vmem((SEQ * FF_BLOCKS, 16, 128), bf16),
            vmem((3, FF_BLOCKS, 16, 128), bf16),
            vmem((ROWS, D), bf16),
            vmem((2, HALF, D), bf16),
            vmem((2, ROWS, D), bf16),
            vmem((2, ROWS, D), bf16),
        ]
        + [vmem((4, 4, 1, 2, 8, 128), f32)] * 4
        + reduction(3)
        + [
            vmem((SEQ * LATE, 16, 128), bf16),
            vmem((3, LATE, 16, 128), bf16),
            vmem((4, 4, 1, 16, 128), bf16),
        ]
        + reduction(1)
        + [
            dma((4, 11)), dma((4, 11)), dma((3,)), dma((3,)), dma((6,)), dma((6,)),
            dma((12,)), dma((12,)), dma((6,)), dma((6,)), dma((2, 3)), dma((2, 3)), dma((6,)),
            dma((3,)), dma((3,)), dma((3, 10)), dma((3, 10)), dma((2, 3)), dma((2, 3)), dma((2, 11)), dma((2, 11)),
        ],
        collective_id=1,
    )


def tables_kernel(
    early, late, done_out, done_grad,
    qkv_in, q_out, kv_out, o_in, o_out, mlp_in, mlp_out, down_in, down_out, layer_out, input_grad,
):
    def copy(source, start, count, out):
        for i in range(count):
            x, place = divmod(start + i, FF_BLOCKS if source is early else LATE)
            owner, slot = divmod(place, 3 if source is early else 1)
            out[:, i * 128 : (i + 1) * 128] = source[owner // 4, owner % 4, 0, x, slot, 0].astype(f32)

    layer_out[...] = done_out[...]
    input_grad[...] = done_grad[...]
    for i in range(2):
        copy(early, 54 * i, 54, mlp_out.at[0, i])
        copy(early, 162 + 9 * i, 9, mlp_in.at[0, i])
        copy(late, 35 + 2 * i, 2, kv_out.at[0, i])
    copy(early, 108, 54, down_in.at[0])
    copy(early, 180, 9, down_out.at[0])
    for i in range(3):
        copy(late, 9 * i, 9, qkv_in.at[0, i])
    copy(late, 27, 8, q_out.at[0])
    copy(late, 39, 8, o_in.at[0])
    copy(late, 47, 9, o_out.at[0])


def put_tables(early, late, done_out, done_grad):
    shapes = (
        (3, 16, D), (16, 1024), (2, 16, 256), (16, 1024), (16, D),
        (2, 16, D), (2, 16, 6912), (16, 6912), (16, D),
    )

    def one(shape):
        rest = len(shape)
        return pl.BlockSpec((1,) + shape, lambda a, rest=rest: (a,) + (0,) * rest)

    rows = pl.BlockSpec((ROWS // 8, D), lambda a: (a, 0))

    def blocks(slots):
        return pl.BlockSpec(
            (4, 4, 1, SEQ, slots, 1, 16, 128), lambda a: (0, 0, a // 4, 0, 0, a % 4, 0, 0)
        )

    return pl.pallas_call(
        tables_kernel,
        grid=(8,),
        out_shape=[jax.ShapeDtypeStruct((8,) + shape, f32) for shape in shapes]
        + [jax.ShapeDtypeStruct((ROWS, D), bf16)] * 2,
        in_specs=[blocks(3), blocks(1), rows, rows],
        out_specs=[one(shape) for shape in shapes] + [rows, rows],
        compiler_params=pltpu.CompilerParams(vmem_limit_bytes=63 * MIB),
        name="tables",
    )(early, late, done_out, done_grad)


def prepare_kernel(
    arrive, leave, ids, place_x, segments, w_query, w_key, w_value, w_gate, w_up, w_down,
    qkv_adapt_in, q_adapt_out, kv_adapt_out, o_adapt_in, o_adapt_out,
    mlp_adapt_in, mlp_adapt_out, down_adapt_in, down_adapt_out,
    gain_one, gain_two, gain_three, gain_four,
    pack_qkv, pack_gu, pack_down, own_marks, segment_rows, segment_column,
    first_qkv, second_q, second_kv, first_o, second_o, first_gu, second_down, ext_gu, ext_down, gains,
    table, q_held, kv_held, o_held, in_held, out_held, sem,
):
    chosen, me = ids[0], place_x[0]
    mlp_out, down_in = mlp_adapt_out.at[chosen], down_adapt_in.at[chosen]
    moves = [
        (mlp_out.at[0], table.at[0:16]),
        (mlp_out.at[1], table.at[16:32]),
        (down_in, table.at[32:48]),
        (q_adapt_out.at[chosen], q_held),
        (kv_adapt_out.at[chosen], kv_held),
        (o_adapt_in.at[chosen], o_held),
        (o_adapt_out.at[chosen], second_o),
        (mlp_adapt_in.at[chosen], in_held),
        (down_adapt_out.at[chosen], out_held),
        (qkv_adapt_in.at[chosen], first_qkv),
    ]
    moves = [pltpu.make_async_copy(src, dst, sem.at[i]) for i, (src, dst) in enumerate(moves)]
    for moving in moves:
        moving.start()
    iota = lambda shape, axis: lax.broadcasted_iota(jnp.int32, shape, axis)
    ones = lambda where: jnp.where(where, 1.0, 0.0).astype(bf16)

    def placed(count, first):
        return ones(iota((48, count), 0) == iota((48, count), 1) + first)

    table[48:128] = jnp.zeros((80, 6912), bf16)
    arrive()
    rows = dot(placed(32, 0), w_query[...]) + dot(placed(8, 32), w_key[...])
    pack_qkv[...] = (rows + dot(placed(8, 40), w_value[...])).astype(bf16)
    row, unit = iota((BLOCK, 216), 0), iota((BLOCK, 216), 1)
    quarter = ones((unit == me * UNITS + row) & (row < UNITS))
    pack_gu[0:64] = dot(quarter, w_gate[...]).astype(bf16)
    pack_gu[64:128] = dot(quarter, w_up[...]).astype(bf16)
    pack_down[...] = dot(quarter, w_down[...]).astype(bf16)

    for i, gain in enumerate((gain_one, gain_two, gain_three, gain_four)):
        gains[i : i + 1] = gain[...].reshape(1, D)
    leave(0, 1, 2)
    adapter = iota((8, 128), 0)
    for half in (0, 1):
        own_marks[half] = jnp.where((adapter + 4 * half == chosen) & (adapter < 4), 1.0, 0.0)
    for i in range(SEQ):
        segment_rows[i] = segments[:, i * ROWS : (i + 1) * ROWS]
    square = iota((ROWS, ROWS), 0) == iota((ROWS, ROWS), 1)
    segment_column[...] = jnp.sum(jnp.where(square, segment_rows[me], 0), -1, keepdims=True)

    for moving in moves:
        moving.wait()
    second_q[...] = jnp.zeros_like(second_q)
    for h in range(4):
        second_q[h, 0:16] = q_held[:, h * 256 : (h + 1) * 256]
        first_o[h] = o_held[:, h * 256 : (h + 1) * 256]
    second_kv[...] = jnp.zeros_like(second_kv)
    second_kv[16:32, 0:256] = kv_held[0]
    second_kv[32:48, 256:512] = kv_held[1]
    first_gu[0:16] = in_held[0]
    first_gu[16:32] = in_held[1]
    first_gu[32:128] = jnp.zeros((96, D), bf16)
    second_down[0:32] = jnp.zeros((32, D), bf16)
    second_down[32:48] = out_held[...]
    second_down[48:128] = jnp.zeros((80, D), bf16)

    def spread(d, _):
        first = 216 * d + me * UNITS
        start = jnp.minimum(first // 128 * 128, 6912 - 256)
        row = iota((BLOCK, 256), 0)
        picked = ones((first + row == start + iota((BLOCK, 256), 1)) & (row < UNITS))
        held = dot_nt(picked, table[:, pl.ds(pl.multiple_of(start, 128), 256)])
        lane = iota((BLOCK, 128), 1)
        ext_gu[d, 0:64] = jnp.where(lane < 16, held, 0.0).astype(bf16)
        ext_gu[d, 64:128] = jnp.where((lane >= 16) & (lane < 32), held, 0.0).astype(bf16)
        ext_down[d] = jnp.where(lane >= 32, held, 0.0).astype(bf16)
        return 0

    lax.fori_loop(0, 32, spread, 0, unroll=4)


def prepare(*arrays):
    shapes = [
        ((48, D), bf16), ((128, D), bf16), ((64, D), bf16), ((2, 8, 128), f32),
        ((SEQ, 1, ROWS), jnp.int32), ((ROWS, 1), jnp.int32),
        ((3, 16, D), bf16), ((4, 48, 256), bf16), ((48, 512), bf16), ((4, 16, 256), bf16), ((16, D), bf16),
        ((128, D), bf16), ((128, D), bf16), ((32, 2 * BLOCK, 128), bf16), ((32, BLOCK, 128), bf16),
        ((4, D), f32),
    ]
    return staged_call(
        prepare_kernel, "prepare", arrays, "ss" + "v" * 7 + "h" * 9 + "v" * 4,
        [shape + ("v",) for shape in shapes],
        [
            pltpu.VMEM((128, 6912), bf16),
            pltpu.VMEM((16, 1024), bf16),
            pltpu.VMEM((2, 16, 256), bf16),
            pltpu.VMEM((16, 1024), bf16),
            pltpu.VMEM((2, 16, D), bf16),
            pltpu.VMEM((16, D), bf16),
            pltpu.SemaphoreType.DMA((10,)),
        ],
    )


def body(
    layer_input, out_grad, segment_ids, adapter_ids,
    gain_attn_in, gain_attn_out, gain_mlp_in, gain_mlp_out,
    w_query, w_key, w_value, w_out, w_gate, w_up, w_down,
    qkv_adapt_in, q_adapt_out, kv_adapt_out, o_adapt_in, o_adapt_out,
    mlp_adapt_in, mlp_adapt_out, down_adapt_in, down_adapt_out,
):
    me = lax.axis_index("seq").astype(jnp.int32)
    (
        pack_qkv, pack_gu, pack_down, own_marks, segment_rows, segment_column,
        first_qkv, second_q, second_kv, first_o, second_o, first_gu, second_down, ext_gu, ext_down, gains,
    ) = prepare(
        adapter_ids, me.reshape(1), segment_ids, w_query.T, w_key.T, w_value.T, w_gate.T, w_up.T, w_down,
        qkv_adapt_in, q_adapt_out, kv_adapt_out, o_adapt_in, o_adapt_out,
        mlp_adapt_in, mlp_adapt_out, down_adapt_in, down_adapt_out,
        gain_attn_in, gain_attn_out, gain_mlp_in, gain_mlp_out,
    )
    first_qkv = first_qkv.reshape(48, D)
    layer_out, input_grad, all_early, all_late = layer(
        layer_input[0], pack_qkv, w_out, pack_gu, pack_down, segment_rows, segment_column, gains,
        first_qkv, second_q, second_kv, first_o, second_o,
        ext_gu.reshape(4, 4, 2, 2 * BLOCK, 128), ext_down.reshape(4, 4, 2, BLOCK, 128),
        first_gu, second_down, out_grad[0], own_marks,
    )
    *tables, layer_out, input_grad = put_tables(all_early, all_late, layer_out, input_grad)
    return (layer_out[None], input_grad[None], *tables)


def solution(mesh):
    tokens = P("dp", "seq", None)
    columns, rows = P(None, "dp"), P("dp", None)
    placed = (
        (tokens, tokens, P("dp", None), P("dp"))
        + (P(),) * 4
        + (columns, columns, columns, rows, columns, columns, rows)
        + (P(),) * 9
    )
    return jax.shard_map(
        body,
        mesh=mesh,
        in_specs=placed,
        out_specs=(tokens, tokens) + (P(),) * 9,
        check_vma=False,
    )
```
